512 devices in a mesh: ctx: 128 (over z, x, y_hi), head: 4 (over y_lo, core).
Axes of the slice: x: 4, y: 4 (y_hi: 2, y_lo: 2; y = y_hi * 2 + y_lo), z: 16, core: 2. Of those that a mesh axis runs over, the one named last changes fastest.
Arguments:
- fine_q: bfloat16 [16384, 2048], P('ctx', 'head'), may hold values from -19 to 19
- fine_k: bfloat16 [16384, 2048], P('ctx', 'head'), may hold values from -19 to 19
- fine_v: bfloat16 [16384, 2048], P('ctx', 'head'), may hold values from -6 to 6
- fine_x: bfloat16 [16384, 2048], P('ctx', 'head'), may hold values from -6 to 6
- conv_weight: bfloat16 [8, 2048, 4096], P(None, 'head', 'ctx'), may hold values from -0.046875 to 0.046875
- qkv_weight: bfloat16 [128, 256, 3, 512], P('ctx', None, None, 'head'), may hold values from -0.09375 to 0.09375
Outputs:
- fine_out: bfloat16 [16384, 2048], P('ctx', 'head')
- coarse_out: bfloat16 [128, 128, 512], P('ctx', None, 'head')
The draws below stay inside these ranges and needn't reach their ends.
All inputs are finite; a program needn't handle non-finite values.
Results may differ from the reference program's by a relative error of at most 0.008.
Values may be sent and summed in bfloat16 or wider, within the bound.
A program may use at most 128 MiB of HBM per device.

```python
import jax
import jax.numpy as jnp
from jax import lax

D_FINE = 2048
D_COARSE = 4096
STRIDE = 8
FINE_STEPS = 2
COARSE_STEPS = 4
FINE_DEV = 128
HEAD_DIM = 128
HEADS_SUB = 4
BLOCKS = 16
ROWBLK = 256
FINE_LEN = 16384
COARSE_LEN = 2048
N_CTX = 128


def draw_fine_q(key, part):
    key = jax.random.fold_in(key, 1)
    own_rows = jax.random.truncated_normal(key, -4.0, 4.0, (FINE_LEN, D_FINE), jnp.float32)
    return own_rows.astype(jnp.bfloat16)


def draw_fine_k(key, part):
    key = jax.random.fold_in(key, 2)
    own_rows = jax.random.truncated_normal(key, -4.0, 4.0, (FINE_LEN, D_FINE), jnp.float32)
    return own_rows.astype(jnp.bfloat16)


def shard_levels(key, shape, shards, low, top_value):
    level = 1.0
    for axis_at, parts in shards:
        heights = jax.random.uniform(jax.random.fold_in(jax.random.fold_in(key, 6), axis_at), (parts,), jnp.float32, low / len(shards), top_value / len(shards))
        level = level * jnp.repeat(jnp.exp(heights), shape[axis_at] // parts).reshape((-1,) + (1,) * (len(shape) - 1 - axis_at))
    return level


def bell_draw(rng, dims, deviation, most, split=(), held_as=jnp.bfloat16):
    level = shard_levels(rng, dims, split, -0.22, 0.18) if split else 1.0
    values = jax.random.normal(rng, dims, jnp.float32) * deviation * level
    return jnp.minimum(jnp.maximum(values, -most), most).astype(held_as)


def setup_inputs(seed: int = 0) -> dict:
    splits = jax.random.split(jax.random.key(seed), 7)
    return {
        "fine_q": draw_fine_q(jax.random.fold_in(splits[6], 71), 0),
        "fine_k": draw_fine_k(jax.random.fold_in(splits[6], 71), 0),
        "fine_v": bell_draw(splits[2], (FINE_LEN, D_FINE), 1.0, 6.0, ((0, 128), (1, 4))),
        "fine_x": bell_draw(splits[3], (FINE_LEN, D_FINE), 1.0, 6.0, ((0, 128), (1, 4))),
        "conv_weight": bell_draw(splits[4], (STRIDE, D_FINE, D_COARSE), (STRIDE * D_FINE) ** -0.5, 0.046875, ((1, 4), (2, 128))),
        "qkv_weight": bell_draw(splits[5], (N_CTX, ROWBLK, 3, HEADS_SUB * HEAD_DIM), D_COARSE ** -0.5, 0.09375, ((0, 128), (3, 4))),
    }


def window_valid(row_count, step_count, block_place):
    query_pos = lax.broadcasted_iota(jnp.int32, (row_count, step_count * row_count), 0)
    key_pos = lax.broadcasted_iota(jnp.int32, (row_count, step_count * row_count), 1)
    blocks_back = step_count - 1 - key_pos // row_count
    inner_pos = key_pos % row_count
    return (blocks_back <= block_place) & ((blocks_back > 0) | (inner_pos <= query_pos))


def attend(queries, key_rows, value_rows, key_valid, head_size):
    row_count = queries.shape[0]
    key_count = key_rows.shape[0]
    head_count = queries.shape[1] // head_size
    q_heads = queries.astype(jnp.float32).reshape(row_count, head_count, head_size)
    k_heads = key_rows.astype(jnp.float32).reshape(key_count, head_count, head_size)
    v_heads = value_rows.astype(jnp.float32).reshape(key_count, head_count, head_size)
    scores = jnp.einsum("rhd,shd->hrs", q_heads, k_heads) * (head_size ** -0.5)
    scores = jnp.where(key_valid[None], scores, -1e30)
    row_max = jnp.max(scores, axis=-1, keepdims=True)
    exp_terms = jnp.exp(scores - row_max)
    weights = (exp_terms / jnp.sum(exp_terms, axis=-1, keepdims=True)).astype(jnp.bfloat16)
    mixed_heads = jnp.einsum("hrs,shd->rhd", weights.astype(jnp.float32), v_heads)
    return mixed_heads.reshape(row_count, head_count * head_size)


def window_attention(queries, key_all, value_all, block_rows, step_count):
    total_rows = queries.shape[0]
    block_total = total_rows // block_rows
    pad_rows = (step_count - 1) * block_rows
    key_pad = jnp.concatenate([jnp.zeros((pad_rows, key_all.shape[1]), key_all.dtype), key_all], 0)
    value_pad = jnp.concatenate([jnp.zeros((pad_rows, value_all.shape[1]), value_all.dtype), value_all], 0)

    def one_block(block_index):
        start = (block_index * block_rows).astype(jnp.int32)
        query_rows = lax.dynamic_slice_in_dim(queries, start, block_rows, 0)
        key_rows = lax.dynamic_slice_in_dim(key_pad, start, step_count * block_rows, 0)
        value_rows = lax.dynamic_slice_in_dim(value_pad, start, step_count * block_rows, 0)
        key_valid = window_valid(block_rows, step_count, block_index)
        return attend(query_rows, key_rows, value_rows, key_valid, HEAD_DIM)

    mixed_blocks = lax.map(one_block, jnp.arange(block_total, dtype=jnp.int32))
    return mixed_blocks.reshape(total_rows, -1)


def reference(fine_q, fine_k, fine_v, fine_x, conv_weight, qkv_weight):
    fine_mix = window_attention(fine_q, fine_k, fine_v, FINE_DEV, FINE_STEPS)
    fine_out = (fine_x.astype(jnp.float32) + fine_mix).astype(jnp.bfloat16)
    grouped = fine_out.reshape(COARSE_LEN, STRIDE * D_FINE)
    coarse = jnp.dot(grouped, conv_weight.reshape(STRIDE * D_FINE, D_COARSE), preferred_element_type=jnp.float32).astype(jnp.bfloat16)
    arranged = qkv_weight.reshape(BLOCKS, STRIDE, ROWBLK, 3, HEADS_SUB * HEAD_DIM)
    arranged = arranged.transpose(0, 2, 3, 1, 4).reshape(D_COARSE, 3 * D_COARSE)
    projected = jnp.dot(coarse, arranged, preferred_element_type=jnp.float32).astype(jnp.bfloat16)
    projected = projected.reshape(COARSE_LEN, 3, D_COARSE)
    coarse_mix = window_attention(projected[:, 0], projected[:, 1], projected[:, 2], FINE_DEV, COARSE_STEPS)
    coarse_sum = (coarse.astype(jnp.float32) + coarse_mix).astype(jnp.bfloat16)
    coarse_out = coarse_sum.reshape(BLOCKS, FINE_DEV, STRIDE, HEADS_SUB * HEAD_DIM).transpose(0, 2, 1, 3)
    return fine_out, coarse_out.reshape(N_CTX, FINE_DEV, HEADS_SUB * HEAD_DIM)
```

```python
import jax
import jax.numpy as jnp
from jax import lax
from jax.experimental import pallas as pl
from jax.experimental.pallas import tpu as pltpu
from jax.sharding import PartitionSpec as P

STRIDE = 8
HEAD_DIM = 128
NZ = 16
MESH = pl.DeviceIdType.MESH
BF16 = jnp.bfloat16
F32 = jnp.float32
SCALE = HEAD_DIM ** -0.5
NEG = -1e30
GROUPS = ((0, 1), (2, 3), (4, 5), (6,), (7,))
TO_RIGHT = (7, 8, 8)
SHIFT = (0, 1, 1)
ORDER = (1, 2, 0)


def slot_of(offset):
    if offset == -8:
        offset = 8
    return -offset if offset <= 0 else 7 + offset


def dot_t(a, b):
    return lax.dot_general(a, b, (((1,), (1,)), ((), ())), preferred_element_type=F32)


def dot(a, b):
    return jnp.dot(a, b, preferred_element_type=F32)


def whole_wait(ref, sem):
    pltpu.make_async_copy(ref, ref, sem).wait()


def kernel(
    q_in, k_in, v_in, x_in, cw_in, pw_in, fine_out, coarse_out,
    q_v, k_v, v_v, x_v, pk_v, pv_v, mix_v, fo_v, ts_v, acts, wt_v, w2_v, pw_v, p2_v,
    sb_v, rb_v, gs_v, gb_v, cc_v, pr_v, rr_v, rl_v, sr_v, sl_v, r1_v, res_v, xs_v, f_v, kv_v, co_v,
    in_sem, fs, fr, ws, wr, as_, ar, zs, zr, ss, sr, gs, gr, rs_s, rs_r, r1s, r1r, xs, xr, ks, kr, out_sem,
):
    ctx = lax.axis_index("ctx")
    head = lax.axis_index("head")
    z = lax.div(ctx, 8)
    s = lax.rem(ctx, 8)
    yl = lax.div(head, 2)
    core = lax.rem(head, 2)
    chip = 2 * s + yl
    half = lax.div(s, 4)
    quarter = lax.rem(s, 4)
    sibling = (ctx, 2 * yl + 1 - core)
    after = (lax.rem(ctx + 1, 128), head)
    before = (lax.rem(ctx + 127, 128), head)
    right = (lax.rem(z + 1, NZ) * 8 + s, head)
    left = (lax.rem(z + NZ - 1, NZ) * 8 + s, head)
    zt = lax.rem(chip - z + NZ, NZ)
    far = (zt * 8 + s, head)

    chips = []
    for j in range(1, 16):
        c = lax.rem(chip + j, 16)
        chips.append((c, (z * 8 + lax.div(c, 2), lax.rem(c, 2) * 2 + core)))
    subs = [lax.rem(s + j, 8) for j in range(1, 8)]
    res_chip = (z * 8 + lax.div(zt, 2), lax.rem(zt, 2) * 2 + core)

    def remote(src, dst, send, recv, dev):
        cp = pltpu.make_async_remote_copy(
            src_ref=src, dst_ref=dst, send_sem=send, recv_sem=recv, device_id=dev, device_id_type=MESH
        )
        cp.start()
        return cp

    loads = []
    for i, (src, dst) in enumerate([(q_in, q_v), (k_in, k_v), (v_in, v_v), (x_in, x_v)]):
        cp = pltpu.make_async_copy(src, dst, in_sem.at[i])
        cp.start()
        loads.append(cp)

    barrier = pltpu.get_barrier_semaphore()

    def greet(dev):
        pl.semaphore_signal(barrier, inc=1, device_id=dev, device_id_type=MESH)

    for dev in (after, before, right, left, sibling):
        greet(dev)

    for _, dev in chips:
        greet(dev)
    for to in subs:
        greet((z * 8 + to, 2 * yl + 1 - core))

    @pl.when(zt != z)
    def _():
        greet(far)

    pl.semaphore_wait(barrier, 27 + jnp.where(zt != z, 1, 0))

    k_cp = remote(k_in, pk_v, fs.at[0], fr.at[0], after)
    v_cp = remote(v_in, pv_v, fs.at[1], fr.at[1], after)

    row = lax.broadcasted_iota(jnp.int32, (128, 128), 0)
    col = lax.broadcasted_iota(jnp.int32, (128, 128), 1)
    causal = col <= row
    for cp in loads:
        cp.wait()
    k_cp.wait_recv()
    v_cp.wait_recv()

    for to in subs:
        remote(cw_in.at[to], wt_v.at[core, s], ws.at[0], wr.at[0], (z * 8 + to, head))
    pltpu.make_async_copy(cw_in.at[s], wt_v.at[core, s], wr.at[0]).start()
    pw_cp = remote(pw_in, pw_v.at[core], ws.at[1], wr.at[1], sibling)
    pw_own = pltpu.make_async_copy(pw_in, pw_v.at[core], wr.at[2])
    pw_own.start()

    has_before = ctx > 0
    for i in range(4):
        cols = slice(i * 128, (i + 1) * 128)
        q = q_v[:, cols]
        own = jnp.where(causal, dot_t(q, k_v[:, cols]) * SCALE, NEG)
        prev = jnp.where(has_before, dot_t(q, pk_v[:, cols]) * SCALE, NEG)
        top = jnp.maximum(jnp.max(own, 1, keepdims=True), jnp.max(prev, 1, keepdims=True))
        e_own = jnp.exp(own - top)
        e_prev = jnp.exp(prev - top)
        total = jnp.sum(e_own, 1, keepdims=True) + jnp.sum(e_prev, 1, keepdims=True)
        mixed = dot(e_own.astype(BF16), v_v[:, cols]) + dot(e_prev.astype(BF16), pv_v[:, cols])
        mix_v[i] = x_v[:, cols].astype(F32) + mixed / total
    for tap in range(8):
        for i in range(4):
            ts_v[tap, :, i * 128 : (i + 1) * 128] = mix_v[i, pl.ds(tap, 16, stride=8), :].astype(BF16)

    for to in subs:
        remote(ts_v.at[to], acts.at[0, core, quarter], as_.at[0], ar.at[0], (z * 8 + to, 2 * yl + half))

    @pl.when(core == half)
    def _():
        pltpu.make_async_copy(ts_v.at[s], acts.at[0, core, quarter], ar.at[0]).start()

    @pl.when(core != half)
    def _():
        remote(ts_v.at[s], acts.at[0, core, quarter], as_.at[1], ar.at[0], sibling)

    for i in range(4):
        fo_v[:, i * 128 : (i + 1) * 128] = mix_v[i].astype(BF16)
    fo_cp = pltpu.make_async_copy(fo_v, fine_out, out_sem.at[0])
    fo_cp.start()

    whole_wait(acts.at[0], ar.at[0])
    to_right = {}
    to_left = {}

    def pass_right(k, part):
        a, b = slot_of(-(k - 1)), slot_of(-k)
        to_right[k, part] = remote(
            acts.at[a, part], acts.at[b, part], zs.at[0, k - 1, part], zr.at[0, k - 1, part], right
        )

    def pass_left(k, part):
        a, b = slot_of(k - 1), slot_of(k)
        to_left[k, part] = remote(
            acts.at[a, part], acts.at[b, part], zs.at[1, k - 1, part], zr.at[1, k - 1, part], left
        )

    for part in range(2):
        pass_right(1, part)
        pass_left(1, part)

    whole_wait(wt_v.at[core], wr.at[0])
    wt_cp = remote(wt_v.at[core], wt_v.at[core], ws.at[2], wr.at[3], sibling)
    pw_own.wait()
    whole_wait(pw_v.at[1 - core], wr.at[1])
    for m in range(3):
        for part in range(2):
            at = m * 256 + part * 128
            p2_v[:, at : at + 128] = pw_v[part, m]
    whole_wait(wt_v.at[1 - core], wr.at[3])
    for part in range(2):
        w2_v[part] = wt_v[part].reshape(256, 512).T

    def group_slots(pairs):
        return [slot_of(o) for p in pairs for o in (-p, p + 1)]

    def conv(g):
        pairs = GROUPS[g]
        n, at = len(pairs), pairs[0]
        total = None
        for part in range(2):
            rows = jnp.concatenate([acts[a, part].reshape(64, 512) for a in group_slots(pairs)], 0)
            term = dot(rows, w2_v[part])
            total = term if total is None else total + term
        for i in range(n):
            lo = total[i * 128 : (i + 1) * 128, :128].reshape(16, 8, 128)
            hi = total[i * 128 : (i + 1) * 128, 128:].reshape(16, 8, 128)
            sb_v[:, at + i] = jnp.concatenate([lo, hi], 1).astype(BF16)
        span = pl.ds(at, n)
        for to, dev in chips:
            remote(sb_v.at[to, span], rb_v.at[chip, span], ss.at[g], sr.at[g], dev)
        pltpu.make_async_copy(sb_v.at[chip, span], rb_v.at[chip, span], sr.at[g]).start()

    def reduce(g):
        n, at = len(GROUPS[g]), GROUPS[g][0]
        span = pl.ds(at, n)
        whole_wait(rb_v.at[:, span], sr.at[g])
        gs_v[at : at + n] = jnp.sum(rb_v[:, at : at + n].astype(F32), 0).astype(BF16)
        for _, dev in chips:
            remote(gs_v.at[span], gb_v.at[chip, span], gs.at[g], gr.at[g], dev)
        pltpu.make_async_copy(gs_v.at[span], gb_v.at[chip, span], gr.at[g]).start()

    def project(g):
        pairs = GROUPS[g]
        n, at = len(pairs), pairs[0]
        whole_wait(gb_v.at[:, pl.ds(at, n)], gr.at[g])
        blocks = []
        for i in range(n):
            got = gb_v[:, at + i].astype(F32)
            blocks.append(jnp.concatenate([got[:, :8].reshape(128, 128), got[:, 8:].reshape(128, 128)], 1))
        rows = jnp.concatenate(blocks, 0).astype(BF16)
        terms = dot(rows, p2_v[...])
        for i, a in enumerate(group_slots(pairs)):
            cc_v[a] = rows[i * 64 : (i + 1) * 64]
            for m in range(3):
                pr_v[a, m] = terms[i * 64 : (i + 1) * 64, m * 256 : (m + 1) * 256]

    def ring(step):
        for part in range(2):
            if step <= 7 or part == 0:
                to_right[step, part].wait_recv()
                if step < 7 or (step == 7 and part == 0):
                    pass_right(step + 1, part)
            if step <= 7 or part == 1:
                to_left[step, part].wait_recv()
                if step < 7 or (step == 7 and part == 1):
                    pass_left(step + 1, part)

    ring(1)
    ring(2)
    conv(0)
    ring(3)
    ring(4)
    conv(1)
    reduce(0)
    ring(5)
    project(0)
    ring(6)
    conv(2)
    reduce(1)
    ring(7)
    conv(3)
    reduce(2)
    project(1)
    ring(8)
    conv(4)
    reduce(3)
    project(2)
    reduce(4)
    project(3)

    sums_right = {}
    sums_left = {}

    def add_right(k, m):
        term = pr_v[slot_of(TO_RIGHT[m] - SHIFT[m] - k), m]
        if k:
            sums_right[k, m].wait_recv()
            term = rr_v[k - 1, m].astype(F32) + term
        sr_v[k, m] = term.astype(BF16)
        sums_right[k + 1, m] = remote(sr_v.at[k, m], rr_v.at[k, m], rs_s.at[0, k, m], rs_r.at[0, k, m], right)

    def add_left(k, m):
        term = pr_v[slot_of(k - (15 - TO_RIGHT[m]) - SHIFT[m]), m]
        if k:
            sums_left[k, m].wait_recv()
            term = rl_v[k - 1, m].astype(F32) + term
        sl_v[k, m] = term.astype(BF16)
        sums_left[k + 1, m] = remote(sl_v.at[k, m], rl_v.at[k, m], rs_s.at[1, k, m], rs_r.at[1, k, m], left)

    for m in ORDER:
        add_right(0, m)
    project(4)
    for m in ORDER:
        add_left(0, m)

    offset = lax.rem(zt - z + NZ, NZ)
    place = jnp.where(offset == 0, 0, jnp.where(offset <= 8, 7 + offset, NZ - offset))

    @pl.when(zt != z)
    def _():
        remote(cc_v.at[place], r1_v, r1s.at[0], r1r.at[0], far)

    @pl.when(zt == z)
    def _():
        pltpu.make_async_copy(cc_v.at[place], r1_v, r1r.at[0]).start()

    k_cp.wait_send()
    v_cp.wait_send()
    whole_wait(wt_v.at[0, pl.ds(0, 7)], ws.at[0])
    pw_cp.wait_send()
    wt_cp.wait_send()
    whole_wait(ts_v.at[pl.ds(0, 7)], as_.at[0])

    @pl.when(core != half)
    def _():
        whole_wait(ts_v.at[0], as_.at[1])

    for cp in list(to_right.values()) + list(to_left.values()):
        cp.wait_send()
    for g, pairs in enumerate(GROUPS):
        whole_wait(sb_v.at[pl.ds(0, 15), pl.ds(pairs[0], len(pairs))], ss.at[g])

    for k in range(1, 8):
        for m in ORDER:
            if k < TO_RIGHT[m]:
                add_right(k, m)
            if k < 15 - TO_RIGHT[m]:
                add_left(k, m)
        if k == 4:
            whole_wait(r1_v, r1r.at[0])

            @pl.when(z != 0)
            def _():
                remote(r1_v, res_v, r1s.at[1], r1r.at[1], res_chip)

            @pl.when(z == 0)
            def _():
                pltpu.make_async_copy(r1_v, res_v, r1r.at[1]).start()
            for g, pairs in enumerate(GROUPS):
                whole_wait(sb_v.at[pl.ds(0, 15), pl.ds(pairs[0], len(pairs))], gs.at[g])

    first = core == 0

    def exchange(m, both):
        f_v[m, core] = jnp.where(first, both[:, :128], both[:, 128:])
        xs_v[m] = jnp.where(first, both[:, 128:], both[:, :128])
        return remote(xs_v.at[m], f_v.at[m, core], xs.at[m], xr.at[m], sibling)

    whole_wait(res_v, r1r.at[1])
    swaps = {3: exchange(3, res_v[...])}
    for m in ORDER:
        nr = TO_RIGHT[m]
        sums_right[nr, m].wait_recv()
        sums_left[15 - nr, m].wait_recv()
        both = pr_v[slot_of(-SHIFT[m]), m] + rr_v[nr - 1, m].astype(F32) + rl_v[14 - nr, m].astype(F32)
        swaps[m] = exchange(m, both.astype(BF16))
    kv_cp = {}
    for i in range(2):
        whole_wait(f_v.at[1 + i, 1 - core], xr.at[1 + i])
        kv_cp[1, i] = remote(f_v.at[1 + i], kv_v.at[1, i], ks.at[1, i], kr.at[1, i], right)
        kv_cp[0, i] = remote(f_v.at[1 + i], kv_v.at[0, i], ks.at[0, i], kr.at[0, i], left)
    for cp in list(sums_right.values()) + list(sums_left.values()):
        cp.wait_send()

    @pl.when(zt != z)
    def _():
        whole_wait(r1_v, r1s.at[0])

    @pl.when(z != 0)
    def _():
        whole_wait(r1_v, r1s.at[1])

    whole_wait(f_v.at[0, 1 - core], xr.at[0])
    whole_wait(f_v.at[3, 1 - core], xr.at[3])
    for cp in swaps.values():
        cp.wait_send()
    for i in range(2):
        kv_cp[1, i].wait_recv()
        kv_cp[2, i] = remote(kv_v.at[1, i], kv_v.at[2, i], ks.at[2, i], kr.at[2, i], right)
    for i in range(2):
        kv_cp[0, i].wait_recv()
    for i in range(2):
        kv_cp[2, i].wait_recv()

    q = f_v[0].reshape(128, 128)
    keys, vals = [
        [ref[...].reshape(128, 128) for ref in (kv_v.at[0, i], f_v.at[1 + i], kv_v.at[1, i], kv_v.at[2, i])]
        for i in range(2)
    ]
    scores = []
    for back in range(4):
        seen = causal if back == 0 else z >= back
        scores.append(jnp.where(seen, dot_t(q, keys[back]) * SCALE, NEG))
    top = scores[0].max(1, keepdims=True)
    for back in range(1, 4):
        top = jnp.maximum(top, scores[back].max(1, keepdims=True))
    total = None
    mixed = None
    for back in range(4):
        e = jnp.exp(scores[back] - top)
        part_sum = jnp.sum(e, 1, keepdims=True)
        part_mix = dot(e.astype(BF16), vals[back])
        total = part_sum if total is None else total + part_sum
        mixed = part_mix if mixed is None else mixed + part_mix
    co_v[...] = (f_v[3].reshape(128, 128).astype(F32) + mixed / total).astype(BF16)
    co_cp = pltpu.make_async_copy(co_v, coarse_out.at[0], out_sem.at[1])
    co_cp.start()

    for cp in kv_cp.values():
        cp.wait_send()
    fo_cp.wait()
    co_cp.wait()


def per_device(fine_q, fine_k, fine_v, fine_x, conv_weight, qkv_weight):
    cw = conv_weight.transpose(0, 2, 1)
    pw = qkv_weight[0].transpose(1, 0, 2)
    dma = pltpu.SemaphoreType.DMA
    vmem = pltpu.VMEM
    scratch = [
        vmem((128, 512), BF16), vmem((128, 512), BF16), vmem((128, 512), BF16), vmem((128, 512), BF16),
        vmem((128, 512), BF16), vmem((128, 512), BF16),
        vmem((4, 128, 128), F32),
        vmem((128, 512), BF16),
        vmem((8, 16, 512), BF16),
        vmem((16, 2, 4, 16, 512), BF16),
        vmem((2, 8, 32, 512), BF16),
        vmem((2, 512, 256), BF16),
        vmem((2, 3, 256, 128), BF16),
        vmem((256, 768), BF16),
        vmem((16, 8, 16, 128), BF16),
        vmem((16, 8, 16, 128), BF16),
        vmem((8, 16, 128), BF16),
        vmem((16, 8, 16, 128), BF16),
        vmem((16, 64, 256), BF16),
        vmem((16, 3, 64, 256), F32),
        vmem((8, 3, 64, 256), BF16),
        vmem((8, 3, 64, 256), BF16),
        vmem((8, 3, 64, 256), BF16),
        vmem((8, 3, 64, 256), BF16),
        vmem((64, 256), BF16),
        vmem((64, 256), BF16),
        vmem((4, 64, 128), BF16),
        vmem((4, 2, 64, 128), BF16),
        vmem((3, 2, 2, 64, 128), BF16),
        vmem((128, 128), BF16),
        dma((4,)), dma((2,)), dma((2,)), dma((3,)), dma((4,)), dma((2,)), dma((1,)),
        dma((2, 8, 2)), dma((2, 8, 2)),
        dma((5,)), dma((5,)), dma((5,)), dma((5,)),
        dma((2, 8, 3)), dma((2, 8, 3)),
        dma((2,)), dma((2,)), dma((4,)), dma((4,)),
        dma((3, 2)), dma((3, 2)), dma((2,)),
    ]
    return pl.pallas_call(
        kernel,
        out_shape=(
            jax.ShapeDtypeStruct((128, 512), BF16),
            jax.ShapeDtypeStruct((1, 128, 128), BF16),
        ),
        in_specs=[pl.BlockSpec(memory_space=pl.ANY)] * 6,
        out_specs=[pl.BlockSpec(memory_space=pl.ANY)] * 2,
        scratch_shapes=scratch,
        compiler_params=pltpu.CompilerParams(
            collective_id=0, has_side_effects=True, vmem_limit_bytes=60 * 1024 * 1024
        ),
    )(fine_q, fine_k, fine_v, fine_x, cw, pw)


def solution(mesh):
    placed = (
        P("ctx", "head"),
        P("ctx", "head"),
        P("ctx", "head"),
        P("ctx", "head"),
        P(None, "head", "ctx"),
        P("ctx", None, None, "head"),
    )
    return jax.shard_map(
        per_device,
        mesh=mesh,
        in_specs=placed,
        out_specs=(P("ctx", "head"), P("ctx", None, "head")),
        check_vma=False,
    )
```

```python
import jax
import jax.numpy as jnp
from jax import lax
from jax.experimental import pallas as pl
from jax.experimental.pallas import tpu as pltpu
from jax.sharding import PartitionSpec as P

STRIDE = 8
HEAD_DIM = 128
NZ = 16
MESH = pl.DeviceIdType.MESH
BF16 = jnp.bfloat16
F32 = jnp.float32
SCALE = HEAD_DIM ** -0.5
NEG = -1e30
GROUPS = ((0, 1), (2, 3), (4, 5), (6,), (7,))
TO_RIGHT = (7, 8, 8)
SHIFT = (0, 1, 1)
ORDER = (1, 2, 0)


def slot_of(offset):
    if offset == -8:
        offset = 8
    return -offset if offset <= 0 else 7 + offset


def dot_t(a, b):
    return lax.dot_general(a, b, (((1,), (1,)), ((), ())), preferred_element_type=F32)


def dot(a, b):
    return jnp.dot(a, b, preferred_element_type=F32)


def whole_wait(ref, sem):
    pltpu.make_async_copy(ref, ref, sem).wait()


def kernel(
    q_in, k_in, v_in, x_in, cw_in, pw_in, fine_out, coarse_out,
    q_v, k_v, v_v, x_v, pk_v, pv_v, mix_v, fo_v, ts_v, acts, wt_v, w2_v, pw_v, p2_v,
    sb_v, rb_v, gs_v, gb_v, cc_v, pr_v, rr_v, rl_v, sr_v, sl_v, r1_v, res_v, xs_v, f_v, ys_v, kv_v, co_v,
    in_sem, fs, fr, ws, wr, as_, ar, zs, zr, ss, sr, gs, gr, rs_s, rs_r, r1s, r1r, xs, xr, ks, kr, out_sem,
):
    ctx = lax.axis_index("ctx")
    head = lax.axis_index("head")
    z = lax.div(ctx, 8)
    s = lax.rem(ctx, 8)
    yl = lax.div(head, 2)
    core = lax.rem(head, 2)
    chip = 2 * s + yl
    half = lax.div(s, 4)
    quarter = lax.rem(s, 4)
    sibling = (ctx, 2 * yl + 1 - core)
    after = (lax.rem(ctx + 1, 128), head)
    before = (lax.rem(ctx + 127, 128), head)
    right = (lax.rem(z + 1, NZ) * 8 + s, head)
    left = (lax.rem(z + NZ - 1, NZ) * 8 + s, head)
    zt = lax.rem(chip - z + NZ, NZ)
    far = (zt * 8 + s, head)

    chips = []
    for j in range(1, 16):
        c = lax.rem(chip + j, 16)
        chips.append((c, (z * 8 + lax.div(c, 2), lax.rem(c, 2) * 2 + core)))
    subs = [lax.rem(s + j, 8) for j in range(1, 8)]
    res_chip = (z * 8 + lax.div(zt, 2), lax.rem(zt, 2) * 2 + core)

    def plane_at(away, c):
        return (lax.rem(z + away, NZ) * 8 + s, 2 * yl + c)

    def remote(src, dst, send, recv, dev):
        cp = pltpu.make_async_remote_copy(
            src_ref=src, dst_ref=dst, send_sem=send, recv_sem=recv, device_id=dev, device_id_type=MESH
        )
        cp.start()
        return cp

    loads = []
    for i, (src, dst) in enumerate([(q_in, q_v), (k_in, k_v), (v_in, v_v), (x_in, x_v)]):
        cp = pltpu.make_async_copy(src, dst, in_sem.at[i])
        cp.start()
        loads.append(cp)

    barrier = pltpu.get_barrier_semaphore()

    def greet(dev):
        pl.semaphore_signal(barrier, inc=1, device_id=dev, device_id_type=MESH)

    for dev in (after, before):
        greet(dev)
    for away in (1, 2, NZ - 2, NZ - 1):
        for c in range(2):
            greet(plane_at(away, c))

    for _, dev in chips:
        greet(dev)
    greet(sibling)
    for to in subs:
        greet((z * 8 + to, 2 * yl + 1 - core))

    @pl.when(zt != z)
    def _():
        greet(far)

    pl.semaphore_wait(barrier, 33 + jnp.where(zt != z, 1, 0))

    fine_cp = []
    for hp in range(2):
        cols = pl.ds(hp * 256, 256)
        for i, (src, dst) in enumerate([(k_in, pk_v), (v_in, pv_v)]):
            fine_cp.append(remote(src.at[:, cols], dst.at[hp], fs.at[2 * hp + i], fr.at[2 * hp + i], after))

    row = lax.broadcasted_iota(jnp.int32, (128, 128), 0)
    col = lax.broadcasted_iota(jnp.int32, (128, 128), 1)
    causal = col <= row
    for cp in loads:
        cp.wait()
    own_part = []
    for i in range(4):
        cols = slice(i * 128, (i + 1) * 128)
        scores = jnp.where(causal, dot_t(q_v[:, cols], k_v[:, cols]) * SCALE, NEG)
        top = jnp.max(scores, 1, keepdims=True)
        e = jnp.exp(scores - top)
        mix_v[i] = dot(e.astype(BF16), v_v[:, cols])
        own_part.append((top, jnp.sum(e, 1, keepdims=True)))
    has_before = ctx > 0
    for hp in range(2):
        fine_cp[2 * hp].wait_recv()
        fine_cp[2 * hp + 1].wait_recv()
        for j in range(2):
            i = 2 * hp + j
            cols = slice(i * 128, (i + 1) * 128)
            near = slice(j * 128, (j + 1) * 128)
            scores = jnp.where(has_before, dot_t(q_v[:, cols], pk_v[hp, :, near]) * SCALE, NEG)
            own_top, own_sum = own_part[i]
            top = jnp.maximum(own_top, jnp.max(scores, 1, keepdims=True))
            scale = jnp.exp(own_top - top)
            e = jnp.exp(scores - top)
            total = own_sum * scale + jnp.sum(e, 1, keepdims=True)
            mixed = mix_v[i] * scale + dot(e.astype(BF16), pv_v[hp, :, near])
            mix_v[i] = x_v[:, cols].astype(F32) + mixed / total
            for tap in range(8):
                ts_v[hp, tap, :, near] = mix_v[i, pl.ds(tap, 16, stride=8), :].astype(BF16)
        for to in subs:
            remote(
                ts_v.at[hp, to], acts.at[0, hp, core, quarter], as_.at[hp], ar.at[hp], (z * 8 + to, 2 * yl + half)
            )

        @pl.when(core == half)
        def _():
            pltpu.make_async_copy(ts_v.at[hp, s], acts.at[0, hp, core, quarter], ar.at[hp]).start()

        @pl.when(core != half)
        def _():
            remote(ts_v.at[hp, s], acts.at[0, hp, core, quarter], as_.at[2 + hp], ar.at[hp], sibling)

    to_right = {}
    to_left = {}
    parts = [(hp, c) for hp in range(2) for c in range(2)]

    def pass_right(k, hp, c):
        a, b = slot_of(-(k - 1)), slot_of(-k)
        to_right[k, hp, c] = remote(
            acts.at[a, hp, c], acts.at[b, hp, c], zs.at[0, k - 1, hp, c], zr.at[0, k - 1, hp, c], right
        )

    def pass_left(k, hp, c):
        a, b = slot_of(k - 1), slot_of(k)
        to_left[k, hp, c] = remote(
            acts.at[a, hp, c], acts.at[b, hp, c], zs.at[1, k - 1, hp, c], zr.at[1, k - 1, hp, c], left
        )

    for hp in range(2):
        whole_wait(acts.at[0, hp], ar.at[hp])
        for c in range(2):
            pass_right(1, hp, c)
            pass_left(1, hp, c)

    for to in subs:
        remote(cw_in.at[to], wt_v.at[core, s], ws.at[0], wr.at[0], (z * 8 + to, head))
    pltpu.make_async_copy(cw_in.at[s], wt_v.at[core, s], wr.at[0]).start()
    pw_cp = remote(pw_in, pw_v.at[core], ws.at[1], wr.at[1], sibling)
    pw_own = pltpu.make_async_copy(pw_in, pw_v.at[core], wr.at[2])
    pw_own.start()
    for i in range(4):
        fo_v[:, i * 128 : (i + 1) * 128] = mix_v[i].astype(BF16)
    fo_cp = pltpu.make_async_copy(fo_v, fine_out, out_sem.at[0])
    fo_cp.start()

    pieces = []
    kept = {}

    def piece(ready):
        def add(f):
            pieces.append((ready, f))
            return f

        return add

    @piece(3)
    def _():
        whole_wait(wt_v.at[core], wr.at[0])
        kept["wt"] = remote(wt_v.at[core], wt_v.at[core], ws.at[2], wr.at[3], sibling)

    @piece(3)
    def _():
        pw_own.wait()
        whole_wait(pw_v.at[1 - core], wr.at[1])
        for m in range(3):
            for part in range(2):
                at = m * 256 + part * 128
                p2_v[:, at : at + 128] = pw_v[part, m]

    def turn(c, hp):
        w2_v[c, hp * 256 : (hp + 1) * 256, :] = wt_v[c, :, :, hp * 256 : (hp + 1) * 256].reshape(256, 256).T

    @piece(4)
    def _():
        turn(core, 0)

    @piece(5)
    def _():
        turn(core, 1)

    @piece(6)
    def _():
        whole_wait(wt_v.at[1 - core], wr.at[3])
        turn(1 - core, 0)

    @piece(7)
    def _():
        turn(1 - core, 1)

    def group_slots(pairs):
        return [slot_of(o) for p in pairs for o in (-p, p + 1)]

    def in_thirds(ready, send):
        for third in range(3):

            @piece(ready)
            def _(third=third):
                for to, dev in chips[5 * third : 5 * third + 5]:
                    send(to, dev)

    def conv(g, ready):
        pairs = GROUPS[g]
        n, at = len(pairs), pairs[0]
        span = pl.ds(at, n)

        @piece(ready)
        def _():
            total = None
            for hp, c in parts:
                rows = jnp.concatenate([acts[a, hp, c].reshape(64, 256) for a in group_slots(pairs)], 0)
                term = dot(rows, w2_v[c, hp * 256 : (hp + 1) * 256, :])
                total = term if total is None else total + term
            for i in range(n):
                lo = total[i * 128 : (i + 1) * 128, :128].reshape(16, 8, 128)
                hi = total[i * 128 : (i + 1) * 128, 128:].reshape(16, 8, 128)
                sb_v[:, at + i] = jnp.concatenate([lo, hi], 1).astype(BF16)
            pltpu.make_async_copy(sb_v.at[chip, span], rb_v.at[chip, span], sr.at[g]).start()

        in_thirds(
            ready, lambda to, dev: remote(sb_v.at[to, span], rb_v.at[chip, span], ss.at[g], sr.at[g], dev)
        )

    def reduce(g, ready):
        n, at = len(GROUPS[g]), GROUPS[g][0]
        span = pl.ds(at, n)

        @piece(ready)
        def _():
            whole_wait(rb_v.at[:, span], sr.at[g])
            gs_v[at : at + n] = jnp.sum(rb_v[:, at : at + n].astype(F32), 0).astype(BF16)
            pltpu.make_async_copy(gs_v.at[span], gb_v.at[chip, span], gr.at[g]).start()

        in_thirds(ready, lambda to, dev: remote(gs_v.at[span], gb_v.at[chip, span], gs.at[g], gr.at[g], dev))

    def project(g, ready):
        pairs = GROUPS[g]
        n, at = len(pairs), pairs[0]

        @piece(ready)
        def _():
            whole_wait(gb_v.at[:, pl.ds(at, n)], gr.at[g])
            blocks = []
            for i in range(n):
                got = gb_v[:, at + i].astype(F32)
                blocks.append(jnp.concatenate([got[:, :8].reshape(128, 128), got[:, 8:].reshape(128, 128)], 1))
            rows = jnp.concatenate(blocks, 0).astype(BF16)
            terms = dot(rows, p2_v[...])
            for i, a in enumerate(group_slots(pairs)):
                cc_v[a] = rows[i * 64 : (i + 1) * 64]
                for m in range(3):
                    pr_v[a, m] = terms[i * 64 : (i + 1) * 64, m * 256 : (m + 1) * 256]

    conv(0, 8)
    conv(1, 16)
    reduce(0, 17)
    project(0, 22)
    conv(2, 24)
    reduce(1, 25)
    conv(3, 28)
    project(1, 29)
    reduce(2, 30)
    conv(4, 32)
    reduce(3, 32)
    project(2, 32)
    reduce(4, 32)
    project(3, 32)

    done = 0
    for step in range(1, 9):
        for hp, c in parts:
            if step <= 7 or hp == 0:
                to_right[step, hp, c].wait_recv()
                if step < 7 or (step == 7 and hp == 0):
                    pass_right(step + 1, hp, c)
            if step <= 7 or hp == 1:
                to_left[step, hp, c].wait_recv()
                if step < 7 or (step == 7 and hp == 1):
                    pass_left(step + 1, hp, c)
            done += 1
            for _ in range(2):
                if done < 32 and pieces and pieces[0][0] <= done:
                    pieces.pop(0)[1]()
    for _, f in pieces:
        f()

    sums_right = {}
    sums_left = {}

    def add_right(k, m):
        term = pr_v[slot_of(TO_RIGHT[m] - SHIFT[m] - k), m]
        if k:
            sums_right[k, m].wait_recv()
            term = rr_v[k - 1, m].astype(F32) + term
        sr_v[k, m] = term.astype(BF16)
        sums_right[k + 1, m] = remote(sr_v.at[k, m], rr_v.at[k, m], rs_s.at[0, k, m], rs_r.at[0, k, m], right)

    def add_left(k, m):
        term = pr_v[slot_of(k - (15 - TO_RIGHT[m]) - SHIFT[m]), m]
        if k:
            sums_left[k, m].wait_recv()
            term = rl_v[k - 1, m].astype(F32) + term
        sl_v[k, m] = term.astype(BF16)
        sums_left[k + 1, m] = remote(sl_v.at[k, m], rl_v.at[k, m], rs_s.at[1, k, m], rs_r.at[1, k, m], left)

    for m in ORDER:
        add_right(0, m)
    pieces.clear()
    project(4, 32)
    pieces.pop()[1]()
    for m in ORDER:
        add_left(0, m)

    offset = lax.rem(zt - z + NZ, NZ)
    place = jnp.where(offset == 0, 0, jnp.where(offset <= 8, 7 + offset, NZ - offset))

    @pl.when(zt != z)
    def _():
        remote(cc_v.at[place], r1_v, r1s.at[0], r1r.at[0], far)

    @pl.when(zt == z)
    def _():
        pltpu.make_async_copy(cc_v.at[place], r1_v, r1r.at[0]).start()

    for cp in fine_cp:
        cp.wait_send()
    whole_wait(wt_v.at[0, pl.ds(0, 7)], ws.at[0])
    pw_cp.wait_send()
    kept["wt"].wait_send()
    for hp in range(2):
        whole_wait(ts_v.at[hp, pl.ds(0, 7)], as_.at[hp])

    @pl.when(core != half)
    def _():
        for hp in range(2):
            whole_wait(ts_v.at[hp, 0], as_.at[2 + hp])

    for cp in list(to_right.values()) + list(to_left.values()):
        cp.wait_send()
    for g, pairs in enumerate(GROUPS):
        whole_wait(sb_v.at[pl.ds(0, 15), pl.ds(pairs[0], len(pairs))], ss.at[g])

    for k in range(1, 8):
        for m in ORDER:
            if k < TO_RIGHT[m]:
                add_right(k, m)
            if k < 15 - TO_RIGHT[m]:
                add_left(k, m)
        if k == 4:
            whole_wait(r1_v, r1r.at[0])

            @pl.when(z != 0)
            def _():
                remote(r1_v, res_v, r1s.at[1], r1r.at[1], res_chip)

            @pl.when(z == 0)
            def _():
                pltpu.make_async_copy(r1_v, res_v, r1r.at[1]).start()
            for g, pairs in enumerate(GROUPS):
                whole_wait(sb_v.at[pl.ds(0, 15), pl.ds(pairs[0], len(pairs))], gs.at[g])

    first = core == 0

    def exchange(i, both):
        f_v[i, core] = jnp.where(first, both[:, :128], both[:, 128:])
        xs_v[i] = jnp.where(first, both[:, 128:], both[:, :128])
        return remote(xs_v.at[i], f_v.at[i, core], xs.at[i], xr.at[i], sibling)

    whole_wait(res_v, r1r.at[1])
    swaps = [exchange(1, res_v[...])]
    kv_cp = []
    for m in ORDER:
        nr = TO_RIGHT[m]
        sums_right[nr, m].wait_recv()
        sums_left[15 - nr, m].wait_recv()
        both = pr_v[slot_of(-SHIFT[m]), m] + rr_v[nr - 1, m].astype(F32) + rl_v[14 - nr, m].astype(F32)
        both = both.astype(BF16)
        if m == 0:
            swaps.append(exchange(0, both))
            continue
        i = m - 1
        for c in range(2):
            ys_v[i, c] = both[:, c * 128 : (c + 1) * 128]
        kv_v[i, 1, core] = jnp.where(first, both[:, :128], both[:, 128:])
        for back, away in ((3, 2), (2, 1), (0, NZ - 1)):
            for c in range(2):
                kv_cp.append(
                    remote(
                        ys_v.at[i, c], kv_v.at[i, back, core], ks.at[i, back, c], kr.at[i, back, core], plane_at(away, c)
                    )
                )
        kv_cp.append(
            remote(ys_v.at[i, 1 - core], kv_v.at[i, 1, core], ks.at[i, 1, 0], kr.at[i, 1, core], sibling)
        )
    for cp in list(sums_right.values()) + list(sums_left.values()):
        cp.wait_send()

    @pl.when(zt != z)
    def _():
        whole_wait(r1_v, r1s.at[0])

    @pl.when(z != 0)
    def _():
        whole_wait(r1_v, r1s.at[1])

    for i in range(2):
        whole_wait(f_v.at[i, 1 - core], xr.at[i])
    for cp in swaps:
        cp.wait_send()
    for i in range(2):
        whole_wait(kv_v.at[i, 1, 1 - core], kr.at[i, 1, 1 - core])
        for back in (0, 2, 3):
            for c in range(2):
                whole_wait(kv_v.at[i, back, c], kr.at[i, back, c])

    q = f_v[0].reshape(128, 128)
    keys, vals = [[kv_v[i, back].reshape(128, 128) for back in range(4)] for i in range(2)]
    scores = []
    for back in range(4):
        seen = causal if back == 0 else z >= back
        scores.append(jnp.where(seen, dot_t(q, keys[back]) * SCALE, NEG))
    top = scores[0].max(1, keepdims=True)
    for back in range(1, 4):
        top = jnp.maximum(top, scores[back].max(1, keepdims=True))
    total = None
    mixed = None
    for back in range(4):
        e = jnp.exp(scores[back] - top)
        part_sum = jnp.sum(e, 1, keepdims=True)
        part_mix = dot(e.astype(BF16), vals[back])
        total = part_sum if total is None else total + part_sum
        mixed = part_mix if mixed is None else mixed + part_mix
    co_v[...] = (f_v[1].reshape(128, 128).astype(F32) + mixed / total).astype(BF16)
    co_cp = pltpu.make_async_copy(co_v, coarse_out.at[0], out_sem.at[1])
    co_cp.start()

    for cp in kv_cp:
        cp.wait_send()
    fo_cp.wait()
    co_cp.wait()


def per_device(fine_q, fine_k, fine_v, fine_x, conv_weight, qkv_weight):
    cw = conv_weight.transpose(0, 2, 1)
    pw = qkv_weight[0].transpose(1, 0, 2)
    dma = pltpu.SemaphoreType.DMA
    vmem = pltpu.VMEM
    scratch = [
        vmem((128, 512), BF16), vmem((128, 512), BF16), vmem((128, 512), BF16), vmem((128, 512), BF16),
        vmem((2, 128, 256), BF16), vmem((2, 128, 256), BF16),
        vmem((4, 128, 128), F32),
        vmem((128, 512), BF16),
        vmem((2, 8, 16, 256), BF16),
        vmem((16, 2, 2, 4, 16, 256), BF16),
        vmem((2, 8, 32, 512), BF16),
        vmem((2, 512, 256), BF16),
        vmem((2, 3, 256, 128), BF16),
        vmem((256, 768), BF16),
        vmem((16, 8, 16, 128), BF16),
        vmem((16, 8, 16, 128), BF16),
        vmem((8, 16, 128), BF16),
        vmem((16, 8, 16, 128), BF16),
        vmem((16, 64, 256), BF16),
        vmem((16, 3, 64, 256), F32),
        vmem((8, 3, 64, 256), BF16),
        vmem((8, 3, 64, 256), BF16),
        vmem((8, 3, 64, 256), BF16),
        vmem((8, 3, 64, 256), BF16),
        vmem((64, 256), BF16),
        vmem((64, 256), BF16),
        vmem((2, 64, 128), BF16),
        vmem((2, 2, 64, 128), BF16),
        vmem((2, 2, 64, 128), BF16),
        vmem((2, 4, 2, 64, 128), BF16),
        vmem((128, 128), BF16),
        dma((4,)), dma((4,)), dma((4,)), dma((3,)), dma((4,)), dma((4,)), dma((2,)),
        dma((2, 8, 2, 2)), dma((2, 8, 2, 2)),
        dma((5,)), dma((5,)), dma((5,)), dma((5,)),
        dma((2, 8, 3)), dma((2, 8, 3)),
        dma((2,)), dma((2,)), dma((2,)), dma((2,)),
        dma((2, 4, 2)), dma((2, 4, 2)), dma((2,)),
    ]
    return pl.pallas_call(
        kernel,
        out_shape=(
            jax.ShapeDtypeStruct((128, 512), BF16),
            jax.ShapeDtypeStruct((1, 128, 128), BF16),
        ),
        in_specs=[pl.BlockSpec(memory_space=pl.ANY)] * 6,
        out_specs=[pl.BlockSpec(memory_space=pl.ANY)] * 2,
        scratch_shapes=scratch,
        compiler_params=pltpu.CompilerParams(
            collective_id=0, has_side_effects=True, vmem_limit_bytes=60 * 1024 * 1024
        ),
    )(fine_q, fine_k, fine_v, fine_x, cw, pw)


def solution(mesh):
    placed = (
        P("ctx", "head"),
        P("ctx", "head"),
        P("ctx", "head"),
        P("ctx", "head"),
        P(None, "head", "ctx"),
        P("ctx", None, None, "head"),
    )
    return jax.shard_map(
        per_device,
        mesh=mesh,
        in_specs=placed,
        out_specs=(P("ctx", "head"), P("ctx", None, "head")),
        check_vma=False,
    )
```

```python
import jax
import jax.numpy as jnp
from jax import lax
from jax.experimental import pallas as pl
from jax.experimental.pallas import tpu as pltpu
from jax.sharding import PartitionSpec as P

STRIDE = 8
HEAD_DIM = 128
NZ = 16
MESH = pl.DeviceIdType.MESH
BF16 = jnp.bfloat16
F32 = jnp.float32
SCALE = HEAD_DIM ** -0.5
NEG = -1e30
GROUPS = 4
TO_RIGHT = (7, 8, 8)
SHIFT = (0, 1, 1)
ORDER = (1, 2, 0)


def slot_of(offset):
    if offset == -8:
        offset = 8
    return -offset if offset <= 0 else 7 + offset


def dot_t(a, b):
    return lax.dot_general(a, b, (((1,), (1,)), ((), ())), preferred_element_type=F32)


def dot(a, b):
    return jnp.dot(a, b, preferred_element_type=F32)


def whole_wait(ref, sem):
    pltpu.make_async_copy(ref, ref, sem).wait()


def kernel(
    q_in, k_in, v_in, x_in, cw_in, pw_in, fine_out, coarse_out,
    q_v, k_v, v_v, x_v, pk_v, pv_v, mix_v, st_v, fo_v, ts_v, acts, wt_v, w2_v, pw_v, p2_v,
    sb_v, rb_v, gs_v, gb_v, cc_v, pr_v, rr_v, rl_v, sr_v, sl_v, r1_v, res_v, xs_v, f_v, ys_v, kv_v, co_v,
    in_sem, fs, fr, ws, wr, as_, ar, zs, zr, ss, sr, gs, gr, rs_s, rs_r, r1s, r1r, xs, xr, ks, kr, out_sem,
):
    ctx = lax.axis_index("ctx")
    head = lax.axis_index("head")
    z = lax.div(ctx, 8)
    s = lax.rem(ctx, 8)
    yl = lax.div(head, 2)
    core = lax.rem(head, 2)
    chip = 2 * s + yl
    half = lax.div(s, 4)
    quarter = lax.rem(s, 4)
    sibling = (ctx, 2 * yl + 1 - core)
    after = (lax.rem(ctx + 1, 128), head)
    before = (lax.rem(ctx + 127, 128), head)
    right = (lax.rem(z + 1, NZ) * 8 + s, head)
    left = (lax.rem(z + NZ - 1, NZ) * 8 + s, head)
    zt = lax.rem(chip - z + NZ, NZ)
    far = (zt * 8 + s, head)

    def chip_at(c):
        return (z * 8 + lax.div(c, 2), lax.rem(c, 2) * 2 + core)

    def loop(low, high, body):
        def step(i, carry):
            body(i)
            return carry

        lax.fori_loop(low, high, step, 0)


    def plane_at(away, c):
        return (lax.rem(z + away, NZ) * 8 + s, 2 * yl + c)

    def remote(src, dst, send, recv, dev):
        cp = pltpu.make_async_remote_copy(
            src_ref=src, dst_ref=dst, send_sem=send, recv_sem=recv, device_id=dev, device_id_type=MESH
        )
        cp.start()
        return cp

    loads = []
    for i, (src, dst) in enumerate([(q_in, q_v), (k_in, k_v), (v_in, v_v), (x_in, x_v)]):
        cp = pltpu.make_async_copy(src, dst, in_sem.at[i])
        cp.start()
        loads.append(cp)

    barrier = pltpu.get_barrier_semaphore()

    def greet(dev):
        pl.semaphore_signal(barrier, inc=1, device_id=dev, device_id_type=MESH)

    for dev in (after, before):
        greet(dev)
    for away in (1, 2, NZ - 2, NZ - 1):
        for c in range(2):
            greet(plane_at(away, c))

    loop(1, 16, lambda j: greet(chip_at(lax.rem(chip + j, 16))))
    loop(0, 8, lambda j: greet((z * 8 + j, 2 * yl + 1 - core)))

    @pl.when(zt != z)
    def _():
        greet(far)

    pl.semaphore_wait(barrier, 33 + jnp.where(zt != z, 1, 0))

    fine_cp = []
    for hp in range(2):
        cols = pl.ds(hp * 256, 256)
        for i, (src, dst) in enumerate([(k_in, pk_v), (v_in, pv_v)]):
            fine_cp.append(remote(src.at[:, cols], dst.at[hp], fs.at[2 * hp + i], fr.at[2 * hp + i], after))

    row = lax.broadcasted_iota(jnp.int32, (128, 128), 0)
    col = lax.broadcasted_iota(jnp.int32, (128, 128), 1)
    causal = col <= row
    for cp in loads:
        cp.wait()

    def own_part(hp):
        for j in range(2):
            i = 2 * hp + j
            cols = pl.ds(pl.multiple_of(i * 128, 128), 128)
            scores = jnp.where(causal, dot_t(q_v[:, cols], k_v[:, cols]) * SCALE, NEG)
            top = jnp.max(scores, 1, keepdims=True)
            e = jnp.exp(scores - top)
            mix_v[i] = dot(e.astype(BF16), v_v[:, cols])
            st_v[i, 0] = top
            st_v[i, 1] = jnp.sum(e, 1, keepdims=True)

    loop(0, 2, own_part)
    has_before = ctx > 0

    def whole_part(hp):
        whole_wait(pk_v.at[hp], fr.at[2 * hp])
        whole_wait(pv_v.at[hp], fr.at[2 * hp + 1])
        for j in range(2):
            i = 2 * hp + j
            cols = pl.ds(pl.multiple_of(i * 128, 128), 128)
            near = slice(j * 128, (j + 1) * 128)
            scores = jnp.where(has_before, dot_t(q_v[:, cols], pk_v[hp, :, near]) * SCALE, NEG)
            own_top, own_sum = st_v[i, 0], st_v[i, 1]
            top = jnp.maximum(own_top, jnp.max(scores, 1, keepdims=True))
            scale = jnp.exp(own_top - top)
            e = jnp.exp(scores - top)
            total = own_sum * scale + jnp.sum(e, 1, keepdims=True)
            mixed = mix_v[i] * scale + dot(e.astype(BF16), pv_v[hp, :, near])
            result = x_v[:, cols].astype(F32) + mixed / total
            mix_v[i] = result
            fo_v[:, cols] = result.astype(BF16)
            for tap in range(8):
                ts_v[hp, tap, :, near] = mix_v[i, pl.ds(tap, 16, stride=8), :].astype(BF16)

        def send(j):
            to = lax.rem(s + j, 8)
            remote(
                ts_v.at[hp, to], acts.at[0, hp, core, quarter], as_.at[hp], ar.at[hp], (z * 8 + to, 2 * yl + half)
            )

        loop(1, 8, send)

        @pl.when(core == half)
        def _():
            pltpu.make_async_copy(ts_v.at[hp, s], acts.at[0, hp, core, quarter], ar.at[hp]).start()

        @pl.when(core != half)
        def _():
            remote(ts_v.at[hp, s], acts.at[0, hp, core, quarter], as_.at[2 + hp], ar.at[hp], sibling)

    loop(0, 2, whole_part)

    parts = [(hp, c) for hp in range(2) for c in range(2)]

    def place_right(k):
        return jnp.where(k == 8, 15, k)

    def place_left(k):
        return jnp.where(k == 0, 0, 7 + k)

    def pass_right(k, hp, c):
        remote(
            acts.at[place_right(k - 1), hp, c], acts.at[place_right(k), hp, c],
            zs.at[0, k - 1, hp, c], zr.at[0, k - 1, hp, c], right,
        )

    def pass_left(k, hp, c):
        remote(
            acts.at[place_left(k - 1), hp, c], acts.at[place_left(k), hp, c],
            zs.at[1, k - 1, hp, c], zr.at[1, k - 1, hp, c], left,
        )

    def got_right(k, hp, c):
        whole_wait(acts.at[place_right(k), hp, c], zr.at[0, k - 1, hp, c])

    def got_left(k, hp, c):
        whole_wait(acts.at[place_left(k), hp, c], zr.at[1, k - 1, hp, c])

    for hp in range(2):
        whole_wait(acts.at[0, hp], ar.at[hp])
        for c in range(2):
            pass_right(1, hp, c)
            pass_left(1, hp, c)

    def send_weights(j):
        to = lax.rem(s + j, 8)
        remote(cw_in.at[to], wt_v.at[core, s], ws.at[0], wr.at[0], (z * 8 + to, head))

    loop(1, 8, send_weights)
    pltpu.make_async_copy(cw_in.at[s], wt_v.at[core, s], wr.at[0]).start()
    pw_cp = remote(pw_in, pw_v.at[core], ws.at[1], wr.at[1], sibling)
    pw_own = pltpu.make_async_copy(pw_in, pw_v.at[core], wr.at[2])
    pw_own.start()
    fo_cp = pltpu.make_async_copy(fo_v, fine_out, out_sem.at[0])
    fo_cp.start()

    def turn(c):
        def part(hp):
            cols = pl.ds(pl.multiple_of(hp * 256, 256), 256)
            w2_v[c, cols, :] = wt_v[c, :, :, cols].reshape(256, 256).T

        loop(0, 2, part)

    def group_slots(g):
        return [2 * g, 2 * g + 8, 2 * g + 1, 2 * g + 9]

    def conv(g):
        total = None
        for hp, c in parts:
            rows = jnp.concatenate([acts[a, hp, c].reshape(64, 256) for a in group_slots(g)], 0)
            term = dot(rows, w2_v[c, hp * 256 : (hp + 1) * 256, :])
            total = term if total is None else total + term
        for i in range(2):
            lo = total[i * 128 : (i + 1) * 128, :128].reshape(16, 8, 128)
            hi = total[i * 128 : (i + 1) * 128, 128:].reshape(16, 8, 128)
            sb_v[g, :, i] = jnp.concatenate([lo, hi], 1).astype(BF16)

        def send(j):
            to = lax.rem(chip + j, 16)
            remote(sb_v.at[g, to], rb_v.at[g, chip], ss.at[g], sr.at[g], chip_at(to))

        loop(1, 16, send)
        pltpu.make_async_copy(sb_v.at[g, chip], rb_v.at[g, chip], sr.at[g]).start()

    def reduce(g):
        whole_wait(rb_v.at[g], sr.at[g])
        gs_v[g] = jnp.sum(rb_v[g].astype(F32), 0).astype(BF16)

        def send(j):
            remote(gs_v.at[g], gb_v.at[g, chip], gs.at[g], gr.at[g], chip_at(lax.rem(chip + j, 16)))

        loop(1, 16, send)
        pltpu.make_async_copy(gs_v.at[g], gb_v.at[g, chip], gr.at[g]).start()

    def project(g):
        whole_wait(gb_v.at[g], gr.at[g])
        blocks = []
        for i in range(2):
            got = gb_v[g, :, i].astype(F32)
            blocks.append(jnp.concatenate([got[:, :8].reshape(128, 128), got[:, 8:].reshape(128, 128)], 1))
        rows = jnp.concatenate(blocks, 0).astype(BF16)
        for i, a in enumerate(group_slots(g)):
            cc_v[a] = rows[i * 64 : (i + 1) * 64]

        def one(m):
            terms = dot(rows, p2_v[m])
            for i, a in enumerate(group_slots(g)):
                pr_v[a, m] = terms[i * 64 : (i + 1) * 64]

        for m in range(3):
            one(m)

    def turn_of(i):
        more = i < GROUPS - 1

        def odd(parts):
            k = 2 * i + 1
            for hp, c in parts:
                got_right(k, hp, c)
                got_left(k, hp, c)
                if hp == 0:
                    pass_right(k + 1, hp, c)
                    pl.when(more)(lambda: pass_left(k + 1, hp, c))
                else:
                    pass_left(k + 1, hp, c)
                    pl.when(more)(lambda: pass_right(k + 1, hp, c))

        def even(parts):
            k = 2 * i + 2
            for hp, c in parts:
                if hp == 0:
                    got_right(k, hp, c)
                else:
                    got_left(k, hp, c)

                @pl.when(more)
                def _():
                    if hp == 0:
                        got_left(k, hp, c)
                    else:
                        got_right(k, hp, c)
                    pass_right(k + 1, hp, c)
                    pass_left(k + 1, hp, c)

        ringing = pl.when(i < GROUPS)
        ringing(lambda: odd(parts[:2]))

        @pl.when(i == 0)
        def _():
            whole_wait(wt_v.at[core], wr.at[0])
            remote(wt_v.at[core], wt_v.at[core], ws.at[2], wr.at[3], sibling)
            pw_own.wait()
            whole_wait(pw_v.at[1 - core], wr.at[1])
            for m in range(3):
                for part in range(2):
                    p2_v[m, :, part * 128 : (part + 1) * 128] = pw_v[part, m]

        pl.when(i >= 2)(lambda: project(i - 2))
        ringing(lambda: odd(parts[2:]))
        pl.when(i == 0)(lambda: turn(core))
        pl.when((i >= 1) & (i <= GROUPS))(lambda: reduce(i - 1))
        ringing(lambda: even(parts))

        @pl.when(i == 0)
        def _():
            whole_wait(wt_v.at[1 - core], wr.at[3])
            turn(1 - core)

        ringing(lambda: conv(i))

    loop(0, GROUPS + 2, turn_of)

    def place_of(offset):
        return jnp.where(offset <= 0, -offset, 7 + offset)

    def add_right(k, m):
        whole_wait(rr_v.at[k - 1, m], rs_r.at[0, k - 1, m])
        term = rr_v[k - 1, m].astype(F32) + pr_v[place_of(TO_RIGHT[m] - SHIFT[m] - k), m]
        sr_v[k, m] = term.astype(BF16)
        remote(sr_v.at[k, m], rr_v.at[k, m], rs_s.at[0, k, m], rs_r.at[0, k, m], right)

    def add_left(k, m):
        whole_wait(rl_v.at[k - 1, m], rs_r.at[1, k - 1, m])
        term = rl_v[k - 1, m].astype(F32) + pr_v[place_of(k - (15 - TO_RIGHT[m]) - SHIFT[m]), m]
        sl_v[k, m] = term.astype(BF16)
        remote(sl_v.at[k, m], rl_v.at[k, m], rs_s.at[1, k, m], rs_r.at[1, k, m], left)

    for m in ORDER:
        sr_v[0, m] = pr_v[slot_of(7), m].astype(BF16)
        remote(sr_v.at[0, m], rr_v.at[0, m], rs_s.at[0, 0, m], rs_r.at[0, 0, m], right)
        sl_v[0, m] = pr_v[slot_of(8), m].astype(BF16)
        remote(sl_v.at[0, m], rl_v.at[0, m], rs_s.at[1, 0, m], rs_r.at[1, 0, m], left)

    offset = lax.rem(zt - z + NZ, NZ)
    place = jnp.where(offset == 0, 0, jnp.where(offset <= 8, 7 + offset, NZ - offset))

    @pl.when(zt != z)
    def _():
        remote(cc_v.at[place], r1_v, r1s.at[0], r1r.at[0], far)

    @pl.when(zt == z)
    def _():
        pltpu.make_async_copy(cc_v.at[place], r1_v, r1r.at[0]).start()

    for i in range(4):
        whole_wait(pk_v.at[0], fs.at[i])
    whole_wait(wt_v.at[0, pl.ds(0, 7)], ws.at[0])
    pw_cp.wait_send()
    whole_wait(wt_v.at[0], ws.at[2])
    for hp in range(2):
        whole_wait(ts_v.at[hp, pl.ds(0, 7)], as_.at[hp])

    @pl.when(core != half)
    def _():
        for hp in range(2):
            whole_wait(ts_v.at[hp, 0], as_.at[2 + hp])

    def ring_left(k):
        for c in range(2):
            for way in range(2):
                whole_wait(acts.at[0, 0, c], zs.at[way, k, way, c])
                pl.when(k < 7)(lambda: whole_wait(acts.at[0, 0, c], zs.at[way, k, 1 - way, c]))

    loop(0, 8, ring_left)
    loop(0, GROUPS, lambda g: whole_wait(sb_v.at[g, pl.ds(0, 15)], ss.at[g]))

    def sums(k):
        for m in ORDER:
            add_right(k, m)
            add_left(k, m)

        @pl.when(k == 4)
        def _():
            whole_wait(r1_v, r1r.at[0])

            @pl.when(z != 0)
            def _():
                remote(r1_v, res_v, r1s.at[1], r1r.at[1], chip_at(zt))

            @pl.when(z == 0)
            def _():
                pltpu.make_async_copy(r1_v, res_v, r1r.at[1]).start()

    loop(1, 7, sums)
    loop(0, GROUPS, lambda g: whole_wait(sb_v.at[g, pl.ds(0, 15)], gs.at[g]))
    for m in ORDER:
        if TO_RIGHT[m] == 8:
            add_right(7, m)
        else:
            add_left(7, m)

    first = core == 0

    def exchange(i, both):
        f_v[i, core] = jnp.where(first, both[:, :128], both[:, 128:])
        xs_v[i] = jnp.where(first, both[:, 128:], both[:, :128])
        return remote(xs_v.at[i], f_v.at[i, core], xs.at[i], xr.at[i], sibling)

    whole_wait(res_v, r1r.at[1])
    swaps = [exchange(1, res_v[...])]
    kv_cp = []
    for m in ORDER:
        nr = TO_RIGHT[m]
        whole_wait(rr_v.at[nr - 1, m], rs_r.at[0, nr - 1, m])
        whole_wait(rl_v.at[14 - nr, m], rs_r.at[1, 14 - nr, m])
        both = pr_v[slot_of(-SHIFT[m]), m] + rr_v[nr - 1, m].astype(F32) + rl_v[14 - nr, m].astype(F32)
        both = both.astype(BF16)
        if m == 0:
            swaps.append(exchange(0, both))
            continue
        i = m - 1
        for c in range(2):
            ys_v[i, c] = both[:, c * 128 : (c + 1) * 128]
        kv_v[i, 1, core] = jnp.where(first, both[:, :128], both[:, 128:])
        for back, away in ((3, 2), (2, 1), (0, NZ - 1)):
            for c in range(2):
                kv_cp.append(
                    remote(
                        ys_v.at[i, c], kv_v.at[i, back, core], ks.at[i, back, c], kr.at[i, back, core], plane_at(away, c)
                    )
                )
        kv_cp.append(
            remote(ys_v.at[i, 1 - core], kv_v.at[i, 1, core], ks.at[i, 1, 0], kr.at[i, 1, core], sibling)
        )
    def sums_left(k):
        for m in ORDER:
            for way in range(2):
                whole_wait(sr_v.at[0, m], rs_s.at[way, k, m])

    loop(0, 7, sums_left)
    for m in ORDER:
        whole_wait(sr_v.at[0, m], rs_s.at[0 if TO_RIGHT[m] == 8 else 1, 7, m])

    @pl.when(zt != z)
    def _():
        whole_wait(r1_v, r1s.at[0])

    @pl.when(z != 0)
    def _():
        whole_wait(r1_v, r1s.at[1])

    for i in range(2):
        whole_wait(f_v.at[i, 1 - core], xr.at[i])
    for cp in swaps:
        cp.wait_send()
    for i in range(2):
        whole_wait(kv_v.at[i, 1, 1 - core], kr.at[i, 1, 1 - core])
        for back in (0, 2, 3):
            for c in range(2):
                whole_wait(kv_v.at[i, back, c], kr.at[i, back, c])

    q = f_v[0].reshape(128, 128)
    keys, vals = [[kv_v[i, back].reshape(128, 128) for back in range(4)] for i in range(2)]
    scores = []
    for back in range(4):
        seen = causal if back == 0 else z >= back
        scores.append(jnp.where(seen, dot_t(q, keys[back]) * SCALE, NEG))
    top = scores[0].max(1, keepdims=True)
    for back in range(1, 4):
        top = jnp.maximum(top, scores[back].max(1, keepdims=True))
    total = None
    mixed = None
    for back in range(4):
        e = jnp.exp(scores[back] - top)
        part_sum = jnp.sum(e, 1, keepdims=True)
        part_mix = dot(e.astype(BF16), vals[back])
        total = part_sum if total is None else total + part_sum
        mixed = part_mix if mixed is None else mixed + part_mix
    co_v[...] = (f_v[1].reshape(128, 128).astype(F32) + mixed / total).astype(BF16)
    co_cp = pltpu.make_async_copy(co_v, coarse_out.at[0], out_sem.at[1])
    co_cp.start()

    for cp in kv_cp:
        cp.wait_send()
    fo_cp.wait()
    co_cp.wait()


def per_device(fine_q, fine_k, fine_v, fine_x, conv_weight, qkv_weight):
    cw = conv_weight.transpose(0, 2, 1)
    pw = qkv_weight[0].transpose(1, 0, 2)
    dma = pltpu.SemaphoreType.DMA
    vmem = pltpu.VMEM
    scratch = [
        vmem((128, 512), BF16), vmem((128, 512), BF16), vmem((128, 512), BF16), vmem((128, 512), BF16),
        vmem((2, 128, 256), BF16), vmem((2, 128, 256), BF16),
        vmem((4, 128, 128), F32),
        vmem((4, 2, 128, 1), F32),
        vmem((128, 512), BF16),
        vmem((2, 8, 16, 256), BF16),
        vmem((16, 2, 2, 4, 16, 256), BF16),
        vmem((2, 8, 32, 512), BF16),
        vmem((2, 512, 256), BF16),
        vmem((2, 3, 256, 128), BF16),
        vmem((3, 256, 256), BF16),
        vmem((4, 16, 2, 16, 128), BF16),
        vmem((4, 16, 2, 16, 128), BF16),
        vmem((4, 2, 16, 128), BF16),
        vmem((4, 16, 2, 16, 128), BF16),
        vmem((16, 64, 256), BF16),
        vmem((16, 3, 64, 256), F32),
        vmem((8, 3, 64, 256), BF16),
        vmem((8, 3, 64, 256), BF16),
        vmem((8, 3, 64, 256), BF16),
        vmem((8, 3, 64, 256), BF16),
        vmem((64, 256), BF16),
        vmem((64, 256), BF16),
        vmem((2, 64, 128), BF16),
        vmem((2, 2, 64, 128), BF16),
        vmem((2, 2, 64, 128), BF16),
        vmem((2, 4, 2, 64, 128), BF16),
        vmem((128, 128), BF16),
        dma((4,)), dma((4,)), dma((4,)), dma((3,)), dma((4,)), dma((4,)), dma((2,)),
        dma((2, 8, 2, 2)), dma((2, 8, 2, 2)),
        dma((4,)), dma((4,)), dma((4,)), dma((4,)),
        dma((2, 8, 3)), dma((2, 8, 3)),
        dma((2,)), dma((2,)), dma((2,)), dma((2,)),
        dma((2, 4, 2)), dma((2, 4, 2)), dma((2,)),
    ]
    return pl.pallas_call(
        kernel,
        out_shape=(
            jax.ShapeDtypeStruct((128, 512), BF16),
            jax.ShapeDtypeStruct((1, 128, 128), BF16),
        ),
        in_specs=[pl.BlockSpec(memory_space=pl.ANY)] * 6,
        out_specs=[pl.BlockSpec(memory_space=pl.ANY)] * 2,
        scratch_shapes=scratch,
        compiler_params=pltpu.CompilerParams(
            collective_id=0, has_side_effects=True, vmem_limit_bytes=60 * 1024 * 1024
        ),
    )(fine_q, fine_k, fine_v, fine_x, cw, pw)


def solution(mesh):
    placed = (
        P("ctx", "head"),
        P("ctx", "head"),
        P("ctx", "head"),
        P("ctx", "head"),
        P(None, "head", "ctx"),
        P("ctx", None, None, "head"),
    )
    return jax.shard_map(
        per_device,
        mesh=mesh,
        in_specs=placed,
        out_specs=(P("ctx", "head"), P("ctx", None, "head")),
        check_vma=False,
    )
```

```python
import jax
import jax.numpy as jnp
from jax import lax
from jax.experimental import pallas as pl
from jax.experimental.pallas import tpu as pltpu
from jax.sharding import PartitionSpec as P

STRIDE = 8
HEAD_DIM = 128
NZ = 16
MESH = pl.DeviceIdType.MESH
BF16 = jnp.bfloat16
F32 = jnp.float32
SCALE = HEAD_DIM ** -0.5
NEG = -1e30
GROUPS = 4
ORDER = (1, 2, 0)


def slot_of(offset):
    if offset == -8:
        offset = 8
    return -offset if offset <= 0 else 7 + offset


def dot_t(a, b):
    return lax.dot_general(a, b, (((1,), (1,)), ((), ())), preferred_element_type=F32)


def dot(a, b):
    return jnp.dot(a, b, preferred_element_type=F32)


def whole_wait(ref, sem):
    pltpu.make_async_copy(ref, ref, sem).wait()


def kernel(
    q_in, k_in, v_in, x_in, cw_in, pw_in, fine_out, coarse_out,
    q_v, k_v, v_v, x_v, pk_v, pv_v, mix_v, st_v, fo_v, ts_v, acts, wt_v, w2_v, pw_v,
    sb_v, rb_v, gs_v, gt_v, gb_v, cc_v, acc_v, xs_v, f_v, ys_v, kv_v, co_v,
    in_sem, fs, fr, ws, wr, as_, ar, zs, zr, ss, sr, gs, gr, hs, hr, wzs, wzr, wss, wsr, xs, xr, ks, kr, out_sem,
):
    ctx = lax.axis_index("ctx")
    head = lax.axis_index("head")
    z = lax.div(ctx, 8)
    s = lax.rem(ctx, 8)
    yl = lax.div(head, 2)
    core = lax.rem(head, 2)
    chip = 2 * s + yl
    half = lax.div(s, 4)
    quarter = lax.rem(s, 4)
    sibling = (ctx, 2 * yl + 1 - core)
    after = (lax.rem(ctx + 1, 128), head)
    before = (lax.rem(ctx + 127, 128), head)
    right = (lax.rem(z + 1, NZ) * 8 + s, head)
    left = (lax.rem(z + NZ - 1, NZ) * 8 + s, head)

    def chip_at(c):
        return (z * 8 + lax.div(c, 2), lax.rem(c, 2) * 2 + core)

    def loop(low, high, body):
        def step(i, carry):
            body(i)
            return carry

        lax.fori_loop(low, high, step, 0)


    def plane_at(away, c):
        return (lax.rem(z + away, NZ) * 8 + s, 2 * yl + c)

    def remote(src, dst, send, recv, dev):
        cp = pltpu.make_async_remote_copy(
            src_ref=src, dst_ref=dst, send_sem=send, recv_sem=recv, device_id=dev, device_id_type=MESH
        )
        cp.start()
        return cp

    loads = []
    for i, (src, dst) in enumerate([(q_in, q_v), (k_in, k_v), (v_in, v_v), (x_in, x_v)]):
        cp = pltpu.make_async_copy(src, dst, in_sem.at[i])
        cp.start()
        loads.append(cp)

    barrier = pltpu.get_barrier_semaphore()

    def greet(dev):
        pl.semaphore_signal(barrier, inc=1, device_id=dev, device_id_type=MESH)

    for dev in (after, before):
        greet(dev)
    loop(1, NZ, lambda j: greet(plane_at(j, core)))
    for away in (1, 2, 3, NZ - 3, NZ - 2, NZ - 1):
        greet(plane_at(away, 1 - core))
    loop(1, 16, lambda j: greet(chip_at(lax.rem(chip + j, 16))))
    loop(0, 8, lambda j: greet((z * 8 + j, 2 * yl + 1 - core)))

    pl.semaphore_wait(barrier, 46)

    fine_cp = []
    for hp in range(2):
        cols = pl.ds(hp * 256, 256)
        for i, (src, dst) in enumerate([(k_in, pk_v), (v_in, pv_v)]):
            fine_cp.append(remote(src.at[:, cols], dst.at[hp], fs.at[2 * hp + i], fr.at[2 * hp + i], after))

    lanes = pl.ds(pl.multiple_of(core * 128, 128), 128)
    other_lanes = pl.ds(pl.multiple_of((1 - core) * 128, 128), 128)

    def held(slot):
        return pw_v.at[slot, :, :, lanes]

    pw_own = pltpu.make_async_copy(pw_in, held(0), wr.at[2])
    pw_own.start()
    remote(pw_in, held(1), wzs.at[0, 0], wzr.at[0, 0], right)
    remote(pw_in, held(8), wzs.at[1, 0], wzr.at[1, 0], left)
    remote(pw_in, held(0), wss.at[0], wsr.at[0], sibling)

    def weights_step(k, on=True):
        whole_wait(held(k), wzr.at[0, k - 1])
        if on:
            remote(held(k), held(k + 1), wzs.at[0, k], wzr.at[0, k], right)
        else:
            remote(pw_v.at[7, 2, :, lanes], pw_v.at[15, 2, :, lanes], wzs.at[0, 7], wzr.at[0, 7], right)
        whole_wait(held(7 + k), wzr.at[1, k - 1])
        if on:
            remote(held(7 + k), held(8 + k), wzs.at[1, k], wzr.at[1, k], left)
        else:
            two = pl.ds(0, 2)
            remote(pw_v.at[14, two, :, lanes], pw_v.at[15, two, :, lanes], wzs.at[1, 7], wzr.at[1, 7], left)
        remote(held(k), held(k), wss.at[k], wsr.at[k], sibling)
        remote(held(7 + k), held(7 + k), wss.at[7 + k], wsr.at[7 + k], sibling)

    def weights_end():
        whole_wait(pw_v.at[15, 2, :, lanes], wzr.at[0, 7])
        whole_wait(pw_v.at[15, pl.ds(0, 2), :, lanes], wzr.at[1, 7])
        remote(held(15), held(15), wss.at[15], wsr.at[15], sibling)

    row = lax.broadcasted_iota(jnp.int32, (128, 128), 0)
    col = lax.broadcasted_iota(jnp.int32, (128, 128), 1)
    causal = col <= row
    for cp in loads:
        cp.wait()

    def own_part(hp):
        for j in range(2):
            i = 2 * hp + j
            cols = pl.ds(pl.multiple_of(i * 128, 128), 128)
            scores = jnp.where(causal, dot_t(q_v[:, cols], k_v[:, cols]) * SCALE, NEG)
            top = jnp.max(scores, 1, keepdims=True)
            e = jnp.exp(scores - top)
            mix_v[i] = dot(e.astype(BF16), v_v[:, cols])
            st_v[i, 0] = top
            st_v[i, 1] = jnp.sum(e, 1, keepdims=True)

    loop(0, 2, own_part)
    has_before = ctx > 0

    def whole_part(hp):
        whole_wait(pk_v.at[hp], fr.at[2 * hp])
        whole_wait(pv_v.at[hp], fr.at[2 * hp + 1])
        for j in range(2):
            i = 2 * hp + j
            cols = pl.ds(pl.multiple_of(i * 128, 128), 128)
            near = slice(j * 128, (j + 1) * 128)
            scores = jnp.where(has_before, dot_t(q_v[:, cols], pk_v[hp, :, near]) * SCALE, NEG)
            own_top, own_sum = st_v[i, 0], st_v[i, 1]
            top = jnp.maximum(own_top, jnp.max(scores, 1, keepdims=True))
            scale = jnp.exp(own_top - top)
            e = jnp.exp(scores - top)
            total = own_sum * scale + jnp.sum(e, 1, keepdims=True)
            mixed = mix_v[i] * scale + dot(e.astype(BF16), pv_v[hp, :, near])
            result = x_v[:, cols].astype(F32) + mixed / total
            mix_v[i] = result
            fo_v[:, cols] = result.astype(BF16)
            for tap in range(8):
                ts_v[hp, tap, :, near] = mix_v[i, pl.ds(tap, 16, stride=8), :].astype(BF16)

        def send(j):
            to = lax.rem(s + j, 8)
            remote(
                ts_v.at[hp, to], acts.at[0, hp, core, quarter], as_.at[hp], ar.at[hp], (z * 8 + to, 2 * yl + half)
            )

        loop(1, 8, send)

        @pl.when(core == half)
        def _():
            pltpu.make_async_copy(ts_v.at[hp, s], acts.at[0, hp, core, quarter], ar.at[hp]).start()

        @pl.when(core != half)
        def _():
            remote(ts_v.at[hp, s], acts.at[0, hp, core, quarter], as_.at[2 + hp], ar.at[hp], sibling)

        pl.when(hp == 0)(lambda: weights_step(1))

    loop(0, 2, whole_part)

    parts = [(hp, c) for hp in range(2) for c in range(2)]

    def place_right(k):
        return jnp.where(k == 8, 15, k)

    def place_left(k):
        return jnp.where(k == 0, 0, 7 + k)

    def pass_right(k, hp, c):
        remote(
            acts.at[place_right(k - 1), hp, c], acts.at[place_right(k), hp, c],
            zs.at[0, k - 1, hp, c], zr.at[0, k - 1, hp, c], right,
        )

    def pass_left(k, hp, c):
        remote(
            acts.at[place_left(k - 1), hp, c], acts.at[place_left(k), hp, c],
            zs.at[1, k - 1, hp, c], zr.at[1, k - 1, hp, c], left,
        )

    def got_right(k, hp, c):
        whole_wait(acts.at[place_right(k), hp, c], zr.at[0, k - 1, hp, c])

    def got_left(k, hp, c):
        whole_wait(acts.at[place_left(k), hp, c], zr.at[1, k - 1, hp, c])

    for hp in range(2):
        whole_wait(acts.at[0, hp], ar.at[hp])
        for c in range(2):
            pass_right(1, hp, c)
            pass_left(1, hp, c)

    def send_weights(j):
        to = lax.rem(s + j, 8)
        remote(cw_in.at[to], wt_v.at[core, s], ws.at[0], wr.at[0], (z * 8 + to, head))

    loop(1, 8, send_weights)
    pltpu.make_async_copy(cw_in.at[s], wt_v.at[core, s], wr.at[0]).start()
    weights_step(2)
    fo_cp = pltpu.make_async_copy(fo_v, fine_out, out_sem.at[0])
    fo_cp.start()

    def turn(c):
        def part(hp):
            cols = pl.ds(pl.multiple_of(hp * 256, 256), 256)
            w2_v[c, cols, :] = wt_v[c, :, :, cols].reshape(256, 256).T

        loop(0, 2, part)

    def group_slots(g):
        return [2 * g, 2 * g + 8, 2 * g + 1, 2 * g + 9]

    def conv(g):
        total = None
        for hp, c in parts:
            rows = jnp.concatenate([acts[a, hp, c].reshape(64, 256) for a in group_slots(g)], 0)
            term = dot(rows, w2_v[c, hp * 256 : (hp + 1) * 256, :])
            total = term if total is None else total + term
        for i in range(2):
            lo = total[i * 128 : (i + 1) * 128, :128].reshape(16, 8, 128)
            hi = total[i * 128 : (i + 1) * 128, 128:].reshape(16, 8, 128)
            sb_v[g, :, i] = jnp.concatenate([lo, hi], 1).astype(BF16)

        def send(j):
            to = lax.rem(chip + j, 16)
            remote(sb_v.at[g, to], rb_v.at[g, chip], ss.at[g], sr.at[g], chip_at(to))

        loop(1, 16, send)
        pltpu.make_async_copy(sb_v.at[g, chip], rb_v.at[g, chip], sr.at[g]).start()

    def reduce(g):
        whole_wait(rb_v.at[g], sr.at[g])
        gs_v[g] = jnp.sum(rb_v[g].astype(F32), 0).astype(BF16)

        for i in range(2):
            p = 2 * g + i
            away = jnp.where(chip < 8, lax.rem(NZ - p, NZ), p + 1)

            @pl.when(away != 0)
            def _():
                remote(gs_v.at[g, i], gt_v.at[g, i], hs.at[g, i], hr.at[g, i], plane_at(away, core))

            @pl.when(away == 0)
            def _():
                pltpu.make_async_copy(gs_v.at[g, i], gt_v.at[g, i], hr.at[g, i]).start()

    def spread(g):
        for i in range(2):
            whole_wait(gt_v.at[g, i], hr.at[g, i])

        def send(j):
            remote(gt_v.at[g], gb_v.at[g, chip], gs.at[g], gr.at[g], chip_at(lax.rem(chip + j, 16)))

        loop(1, 16, send)
        pltpu.make_async_copy(gt_v.at[g], gb_v.at[g, chip], gr.at[g]).start()

    def weight_slots(g):
        return [jnp.where(g == 0, 0, 7 + 2 * g), 8 + 2 * g, 2 * g + 1, jnp.where(g == 3, 15, 2 * g + 2)]

    def project(g):
        slots = weight_slots(g)
        for slot in slots:
            whole_wait(pw_v.at[slot, :, :, other_lanes], wsr.at[slot])
        whole_wait(gb_v.at[g], gr.at[g])
        for i in range(2):
            got = gb_v[g, :, i].astype(F32)
            rows = jnp.concatenate([got[:, :8].reshape(128, 128), got[:, 8:].reshape(128, 128)], 1).astype(BF16)
            cc_v[slots[i]] = rows[:64]
            cc_v[slots[2 + i]] = rows[64:]

        def one(m):
            terms = acc_v[m]
            for slot in slots:
                terms = terms + dot(cc_v[slot], pw_v[slot, m])
            acc_v[m] = terms

        loop(0, 3, one)

    def turn_of(i):
        more = i < GROUPS - 1

        def odd(parts):
            k = 2 * i + 1
            for hp, c in parts:
                got_right(k, hp, c)
                got_left(k, hp, c)
                if hp == 0:
                    pass_right(k + 1, hp, c)
                    pl.when(more)(lambda: pass_left(k + 1, hp, c))
                else:
                    pass_left(k + 1, hp, c)
                    pl.when(more)(lambda: pass_right(k + 1, hp, c))

        def even(parts):
            k = 2 * i + 2
            for hp, c in parts:
                if hp == 0:
                    got_right(k, hp, c)
                else:
                    got_left(k, hp, c)

                @pl.when(more)
                def _():
                    if hp == 0:
                        got_left(k, hp, c)
                    else:
                        got_right(k, hp, c)
                    pass_right(k + 1, hp, c)
                    pass_left(k + 1, hp, c)

        ringing = pl.when(i < GROUPS)
        ringing(lambda: odd(parts[:2]))

        @pl.when(i == 0)
        def _():
            whole_wait(wt_v.at[core], wr.at[0])
            remote(wt_v.at[core], wt_v.at[core], ws.at[2], wr.at[3], sibling)
            pw_own.wait()
            acc_v[...] = jnp.zeros_like(acc_v)

        ringing(lambda: odd(parts[2:]))
        pl.when(i == 0)(lambda: turn(core))
        pl.when((i >= 2) & (i < GROUPS + 2))(lambda: spread(i - 2))
        pl.when((i >= 1) & (i < GROUPS + 1))(lambda: reduce(i - 1))
        pl.when(i == GROUPS)(lambda: weights_step(7, False))
        pl.when(i == GROUPS + 1)(weights_end)
        ringing(lambda: even(parts))

        @pl.when(i == 0)
        def _():
            whole_wait(wt_v.at[1 - core], wr.at[3])
            turn(1 - core)

        ringing(lambda: weights_step(i + 3))
        ringing(lambda: conv(i))
        pl.when(i >= 3)(lambda: project(i - 3))

    loop(0, GROUPS + 3, turn_of)

    first = core == 0

    def exchange(i, both):
        f_v[i, core] = jnp.where(first, both[:, :128], both[:, 128:])
        xs_v[i] = jnp.where(first, both[:, 128:], both[:, :128])
        return remote(xs_v.at[i], f_v.at[i, core], xs.at[i], xr.at[i], sibling)

    offset = lax.rem(chip - z + NZ, NZ)
    place = jnp.where(offset == 0, 0, jnp.where(offset <= 8, 7 + offset, NZ - offset))
    swaps = [exchange(1, cc_v[place])]
    kv_cp = []
    for m in ORDER:
        both = acc_v[m].astype(BF16)
        if m == 0:
            swaps.append(exchange(0, both))
            continue
        i = m - 1
        for c in range(2):
            ys_v[i, c] = both[:, c * 128 : (c + 1) * 128]
        kv_v[i, 0, core] = jnp.where(first, both[:, :128], both[:, 128:])
        for back in (3, 2, 1):
            for c in range(2):
                kv_cp.append(
                    remote(
                        ys_v.at[i, c], kv_v.at[i, back, core], ks.at[i, back, c], kr.at[i, back, core], plane_at(back, c)
                    )
                )
        kv_cp.append(
            remote(ys_v.at[i, 1 - core], kv_v.at[i, 0, core], ks.at[i, 0, 0], kr.at[i, 0, core], sibling)
        )
    for i in range(4):
        whole_wait(pk_v.at[0], fs.at[i])
    whole_wait(wt_v.at[0, pl.ds(0, 7)], ws.at[0])
    whole_wait(wt_v.at[0], ws.at[2])
    for hp in range(2):
        whole_wait(ts_v.at[hp, pl.ds(0, 7)], as_.at[hp])

    @pl.when(core != half)
    def _():
        for hp in range(2):
            whole_wait(ts_v.at[hp, 0], as_.at[2 + hp])

    def ring_left(k):
        for c in range(2):
            for way in range(2):
                whole_wait(acts.at[0, 0, c], zs.at[way, k, way, c])
                pl.when(k < 7)(lambda: whole_wait(acts.at[0, 0, c], zs.at[way, k, 1 - way, c]))

    loop(0, 8, ring_left)
    loop(0, GROUPS, lambda g: whole_wait(sb_v.at[g, pl.ds(0, 15)], ss.at[g]))

    loop(0, GROUPS, lambda g: whole_wait(sb_v.at[g, pl.ds(0, 15)], gs.at[g]))

    def chunks_left(g):
        for i in range(2):
            pl.when((g + i > 0) | (chip >= 8))(lambda: whole_wait(gt_v.at[0, 0], hs.at[g, i]))

    loop(0, GROUPS, chunks_left)

    def weights_left(k):
        for way in range(2):
            whole_wait(held(0), wzs.at[way, k])

    loop(0, 7, weights_left)
    whole_wait(pw_v.at[15, 2, :, lanes], wzs.at[0, 7])
    whole_wait(pw_v.at[15, pl.ds(0, 2), :, lanes], wzs.at[1, 7])
    loop(0, NZ, lambda k: whole_wait(held(0), wss.at[k]))
    for i in range(2):
        whole_wait(f_v.at[i, 1 - core], xr.at[i])
    for cp in swaps:
        cp.wait_send()
    for i in range(2):
        whole_wait(kv_v.at[i, 0, 1 - core], kr.at[i, 0, 1 - core])
        for back in (1, 2, 3):
            for c in range(2):
                whole_wait(kv_v.at[i, back, c], kr.at[i, back, c])

    q = f_v[0].reshape(128, 128)
    keys, vals = [[kv_v[i, back].reshape(128, 128) for back in range(4)] for i in range(2)]
    scores = []
    for back in range(4):
        seen = causal if back == 0 else z >= back
        scores.append(jnp.where(seen, dot_t(q, keys[back]) * SCALE, NEG))
    top = scores[0].max(1, keepdims=True)
    for back in range(1, 4):
        top = jnp.maximum(top, scores[back].max(1, keepdims=True))
    total = None
    mixed = None
    for back in range(4):
        e = jnp.exp(scores[back] - top)
        part_sum = jnp.sum(e, 1, keepdims=True)
        part_mix = dot(e.astype(BF16), vals[back])
        total = part_sum if total is None else total + part_sum
        mixed = part_mix if mixed is None else mixed + part_mix
    co_v[...] = (f_v[1].reshape(128, 128).astype(F32) + mixed / total).astype(BF16)
    co_cp = pltpu.make_async_copy(co_v, coarse_out.at[0], out_sem.at[1])
    co_cp.start()

    for cp in kv_cp:
        cp.wait_send()
    fo_cp.wait()
    co_cp.wait()


def per_device(fine_q, fine_k, fine_v, fine_x, conv_weight, qkv_weight):
    cw = conv_weight.transpose(0, 2, 1)
    pw = qkv_weight[0].transpose(1, 0, 2)
    dma = pltpu.SemaphoreType.DMA
    vmem = pltpu.VMEM
    scratch = [
        vmem((128, 512), BF16), vmem((128, 512), BF16), vmem((128, 512), BF16), vmem((128, 512), BF16),
        vmem((2, 128, 256), BF16), vmem((2, 128, 256), BF16),
        vmem((4, 128, 128), F32),
        vmem((4, 2, 128, 1), F32),
        vmem((128, 512), BF16),
        vmem((2, 8, 16, 256), BF16),
        vmem((16, 2, 2, 4, 16, 256), BF16),
        vmem((2, 8, 32, 512), BF16),
        vmem((2, 512, 256), BF16),
        vmem((16, 3, 256, 256), BF16),
        vmem((4, 16, 2, 16, 128), BF16),
        vmem((4, 16, 2, 16, 128), BF16),
        vmem((4, 2, 16, 128), BF16),
        vmem((4, 2, 16, 128), BF16),
        vmem((4, 16, 2, 16, 128), BF16),
        vmem((16, 64, 256), BF16),
        vmem((3, 64, 256), F32),
        vmem((2, 64, 128), BF16),
        vmem((2, 2, 64, 128), BF16),
        vmem((2, 2, 64, 128), BF16),
        vmem((2, 4, 2, 64, 128), BF16),
        vmem((128, 128), BF16),
        dma((4,)), dma((4,)), dma((4,)), dma((3,)), dma((4,)), dma((4,)), dma((2,)),
        dma((2, 8, 2, 2)), dma((2, 8, 2, 2)),
        dma((4,)), dma((4,)), dma((4,)), dma((4,)),
        dma((4, 2)), dma((4, 2)), dma((2, 8)), dma((2, 8)), dma((16,)), dma((16,)),
        dma((2,)), dma((2,)),
        dma((2, 4, 2)), dma((2, 4, 2)), dma((2,)),
    ]
    return pl.pallas_call(
        kernel,
        out_shape=(
            jax.ShapeDtypeStruct((128, 512), BF16),
            jax.ShapeDtypeStruct((1, 128, 128), BF16),
        ),
        in_specs=[pl.BlockSpec(memory_space=pl.ANY)] * 6,
        out_specs=[pl.BlockSpec(memory_space=pl.ANY)] * 2,
        scratch_shapes=scratch,
        compiler_params=pltpu.CompilerParams(
            collective_id=0, has_side_effects=True, vmem_limit_bytes=60 * 1024 * 1024
        ),
    )(fine_q, fine_k, fine_v, fine_x, cw, pw)


def solution(mesh):
    placed = (
        P("ctx", "head"),
        P("ctx", "head"),
        P("ctx", "head"),
        P("ctx", "head"),
        P(None, "head", "ctx"),
        P("ctx", None, None, "head"),
    )
    return jax.shard_map(
        per_device,
        mesh=mesh,
        in_specs=placed,
        out_specs=(P("ctx", "head"), P("ctx", None, "head")),
        check_vma=False,
    )
```

```python
import jax
import jax.numpy as jnp
from jax import lax
from jax.experimental import pallas as pl
from jax.experimental.pallas import tpu as pltpu
from jax.sharding import PartitionSpec as P

STRIDE = 8
HEAD_DIM = 128
NZ = 16
MESH = pl.DeviceIdType.MESH
BF16 = jnp.bfloat16
F32 = jnp.float32
SCALE = HEAD_DIM ** -0.5
NEG = -1e30
GROUPS = 4
ORDER = (1, 2, 0)


def slot_of(offset):
    if offset == -8:
        offset = 8
    return -offset if offset <= 0 else 7 + offset


def dot_t(a, b):
    return lax.dot_general(a, b, (((1,), (1,)), ((), ())), preferred_element_type=F32)


def dot(a, b):
    return jnp.dot(a, b, preferred_element_type=F32)


def whole_wait(ref, sem):
    pltpu.make_async_copy(ref, ref, sem).wait()


def kernel(
    q_in, k_in, v_in, x_in, cw_in, pw_in, fine_out, coarse_out,
    q_v, k_v, v_v, x_v, pk_v, pv_v, mix_v, st_v, fo_v, ts_v, acts, wt_v, w2_v, pw_v,
    sb_v, rb_v, gs_v, gt_v, gb_v, cc_v, acc_v, xs_v, f_v, ys_v, kv_v, co_v,
    in_sem, fs, fr, ws, wr, as_, ar, zs, zr, ss, sr, gs, gr, hs, hr, wzs, wzr, wss, wsr, xs, xr, ks, kr, out_sem,
):
    ctx = lax.axis_index("ctx")
    head = lax.axis_index("head")
    z = lax.div(ctx, 8)
    s = lax.rem(ctx, 8)
    yl = lax.div(head, 2)
    core = lax.rem(head, 2)
    chip = 2 * s + yl
    half = lax.div(s, 4)
    quarter = lax.rem(s, 4)
    sibling = (ctx, 2 * yl + 1 - core)
    after = (lax.rem(ctx + 1, 128), head)
    before = (lax.rem(ctx + 127, 128), head)
    right = (lax.rem(z + 1, NZ) * 8 + s, head)
    left = (lax.rem(z + NZ - 1, NZ) * 8 + s, head)

    def chip_at(c):
        return (z * 8 + lax.div(c, 2), lax.rem(c, 2) * 2 + core)

    def loop(low, high, body):
        def step(i, carry):
            body(i)
            return carry

        lax.fori_loop(low, high, step, 0)


    def plane_at(away, c):
        return (lax.rem(z + away, NZ) * 8 + s, 2 * yl + c)

    def remote(src, dst, send, recv, dev):
        cp = pltpu.make_async_remote_copy(
            src_ref=src, dst_ref=dst, send_sem=send, recv_sem=recv, device_id=dev, device_id_type=MESH
        )
        cp.start()
        return cp

    loads = []
    for i, (src, dst) in enumerate([(q_in, q_v), (k_in, k_v), (v_in, v_v), (x_in, x_v)]):
        cp = pltpu.make_async_copy(src, dst, in_sem.at[i])
        cp.start()
        loads.append(cp)

    barrier = pltpu.get_barrier_semaphore()

    def greet(dev):
        pl.semaphore_signal(barrier, inc=1, device_id=dev, device_id_type=MESH)

    for dev in (after, before):
        greet(dev)
    loop(1, NZ, lambda j: greet(plane_at(j, core)))
    for away in (1, 2, NZ - 2, NZ - 1):
        greet(plane_at(away, 1 - core))
    loop(1, 16, lambda j: greet(chip_at(lax.rem(chip + j, 16))))
    loop(0, 8, lambda j: greet((z * 8 + j, 2 * yl + 1 - core)))

    pl.semaphore_wait(barrier, 44)

    fine_cp = []
    for hp in range(2):
        cols = pl.ds(hp * 256, 256)
        for i, (src, dst) in enumerate([(k_in, pk_v), (v_in, pv_v)]):
            fine_cp.append(remote(src.at[:, cols], dst.at[hp], fs.at[2 * hp + i], fr.at[2 * hp + i], after))

    lanes = pl.ds(pl.multiple_of(core * 128, 128), 128)
    other_lanes = pl.ds(pl.multiple_of((1 - core) * 128, 128), 128)

    def held(slot, m):
        return pw_v.at[slot, m, :, lanes]

    pw_own = pltpu.make_async_copy(pw_in, pw_v.at[0, :, :, lanes], wr.at[2])
    pw_own.start()
    for m in range(3):
        remote(pw_in.at[m], held(1, m), wzs.at[0, 0, m], wzr.at[0, 0, m], right)
        remote(pw_in.at[m], held(8, m), wzs.at[1, 0, m], wzr.at[1, 0, m], left)
    for m in range(3):
        remote(pw_in.at[m], held(0, m), wss.at[0, m], wsr.at[0, m], sibling)

    def weights_step(k, m):
        whole_wait(held(k, m), wzr.at[0, k - 1, m])
        whole_wait(held(7 + k, m), wzr.at[1, k - 1, m])

        @pl.when((k < 7) | (m == 2))
        def _():
            remote(held(k, m), held(jnp.where(k == 7, 15, k + 1), m), wzs.at[0, k, m], wzr.at[0, k, m], right)

        @pl.when((k < 7) | (m != 2))
        def _():
            remote(held(7 + k, m), held(8 + k, m), wzs.at[1, k, m], wzr.at[1, k, m], left)

        @pl.when((k == 7) & (m == 2))
        def _():
            remote(held(7, m), held(15, m), wss.at[15, m], wsr.at[15, m], plane_at(1, 1 - core))

        @pl.when((k == 7) & (m != 2))
        def _():
            remote(held(14, m), held(15, m), wss.at[15, m], wsr.at[15, m], plane_at(NZ - 1, 1 - core))

        remote(held(k, m), held(k, m), wss.at[k, m], wsr.at[k, m], sibling)
        remote(held(7 + k, m), held(7 + k, m), wss.at[7 + k, m], wsr.at[7 + k, m], sibling)

    def weights_end():
        for m in range(3):
            way = 0 if m == 2 else 1
            whole_wait(held(15, m), wzr.at[way, 7, m])

    row = lax.broadcasted_iota(jnp.int32, (128, 128), 0)
    col = lax.broadcasted_iota(jnp.int32, (128, 128), 1)
    causal = col <= row
    for cp in loads:
        cp.wait()

    def own_part(hp):
        for j in range(2):
            i = 2 * hp + j
            cols = pl.ds(pl.multiple_of(i * 128, 128), 128)
            scores = jnp.where(causal, dot_t(q_v[:, cols], k_v[:, cols]) * SCALE, NEG)
            top = jnp.max(scores, 1, keepdims=True)
            e = jnp.exp(scores - top)
            mix_v[i] = dot(e.astype(BF16), v_v[:, cols])
            st_v[i, 0] = top
            st_v[i, 1] = jnp.sum(e, 1, keepdims=True)

    loop(0, 2, own_part)
    has_before = ctx > 0

    def whole_part(hp):
        whole_wait(pk_v.at[hp], fr.at[2 * hp])
        whole_wait(pv_v.at[hp], fr.at[2 * hp + 1])
        for j in range(2):
            i = 2 * hp + j
            cols = pl.ds(pl.multiple_of(i * 128, 128), 128)
            near = slice(j * 128, (j + 1) * 128)
            scores = jnp.where(has_before, dot_t(q_v[:, cols], pk_v[hp, :, near]) * SCALE, NEG)
            own_top, own_sum = st_v[i, 0], st_v[i, 1]
            top = jnp.maximum(own_top, jnp.max(scores, 1, keepdims=True))
            scale = jnp.exp(own_top - top)
            e = jnp.exp(scores - top)
            total = own_sum * scale + jnp.sum(e, 1, keepdims=True)
            mixed = mix_v[i] * scale + dot(e.astype(BF16), pv_v[hp, :, near])
            result = x_v[:, cols].astype(F32) + mixed / total
            mix_v[i] = result
            fo_v[:, cols] = result.astype(BF16)
            for tap in range(8):
                ts_v[hp, tap, :, near] = mix_v[i, pl.ds(tap, 16, stride=8), :].astype(BF16)

        def send(j):
            to = lax.rem(s + j, 8)
            remote(
                ts_v.at[hp, to], acts.at[0, hp, core, quarter], as_.at[hp], ar.at[hp], (z * 8 + to, 2 * yl + half)
            )

        loop(1, 8, send)

        @pl.when(core == half)
        def _():
            pltpu.make_async_copy(ts_v.at[hp, s], acts.at[0, hp, core, quarter], ar.at[hp]).start()

        @pl.when(core != half)
        def _():
            remote(ts_v.at[hp, s], acts.at[0, hp, core, quarter], as_.at[2 + hp], ar.at[hp], sibling)

        @pl.when(hp == 0)
        def _():
            loop(0, 2, lambda m: weights_step(1, m))


    loop(0, 2, whole_part)

    parts = [(hp, c) for hp in range(2) for c in range(2)]

    def place_right(k):
        return jnp.where(k == 8, 15, k)

    def place_left(k):
        return jnp.where(k == 0, 0, 7 + k)

    def pass_right(k, hp, c):
        remote(
            acts.at[place_right(k - 1), hp, c], acts.at[place_right(k), hp, c],
            zs.at[0, k - 1, hp, c], zr.at[0, k - 1, hp, c], right,
        )

    def pass_left(k, hp, c):
        remote(
            acts.at[place_left(k - 1), hp, c], acts.at[place_left(k), hp, c],
            zs.at[1, k - 1, hp, c], zr.at[1, k - 1, hp, c], left,
        )

    def got_right(k, hp, c):
        whole_wait(acts.at[place_right(k), hp, c], zr.at[0, k - 1, hp, c])

    def got_left(k, hp, c):
        whole_wait(acts.at[place_left(k), hp, c], zr.at[1, k - 1, hp, c])

    for hp in range(2):
        whole_wait(acts.at[0, hp], ar.at[hp])
        for c in range(2):
            pass_right(1, hp, c)
            pass_left(1, hp, c)

    def send_weights(j):
        to = lax.rem(s + j, 8)
        remote(cw_in.at[to], wt_v.at[core, s], ws.at[0], wr.at[0], (z * 8 + to, head))

    loop(1, 8, send_weights)
    pltpu.make_async_copy(cw_in.at[s], wt_v.at[core, s], wr.at[0]).start()
    weights_step(1, 2)
    loop(0, 3, lambda m: weights_step(2, m))
    fo_cp = pltpu.make_async_copy(fo_v, fine_out, out_sem.at[0])
    fo_cp.start()

    def turn(c):
        def part(hp):
            cols = pl.ds(pl.multiple_of(hp * 256, 256), 256)
            w2_v[c, cols, :] = wt_v[c, :, :, cols].reshape(256, 256).T

        loop(0, 2, part)

    def group_slots(g):
        return [2 * g, 2 * g + 8, 2 * g + 1, 2 * g + 9]

    def conv(g):
        total = None
        for hp, c in parts:
            rows = jnp.concatenate([acts[a, hp, c].reshape(64, 256) for a in group_slots(g)], 0)
            term = dot(rows, w2_v[c, hp * 256 : (hp + 1) * 256, :])
            total = term if total is None else total + term
        for i in range(2):
            lo = total[i * 128 : (i + 1) * 128, :128].reshape(16, 8, 128)
            hi = total[i * 128 : (i + 1) * 128, 128:].reshape(16, 8, 128)
            sb_v[g, :, i] = jnp.concatenate([lo, hi], 1).astype(BF16)

        def send(j):
            to = lax.rem(chip + j, 16)
            remote(sb_v.at[g, to], rb_v.at[g, chip], ss.at[g], sr.at[g], chip_at(to))

        loop(1, 16, send)
        pltpu.make_async_copy(sb_v.at[g, chip], rb_v.at[g, chip], sr.at[g]).start()

    def reduce(g):
        whole_wait(rb_v.at[g], sr.at[g])
        gs_v[g] = jnp.sum(rb_v[g].astype(F32), 0).astype(BF16)

        for i in range(2):
            p = 2 * g + i
            away = jnp.where(chip < 8, lax.rem(NZ + 1 - p, NZ), p + 2)

            @pl.when(away != 0)
            def _():
                remote(gs_v.at[g, i], gt_v.at[g, i], hs.at[g, i], hr.at[g, i], plane_at(away, core))

            @pl.when(away == 0)
            def _():
                pltpu.make_async_copy(gs_v.at[g, i], gt_v.at[g, i], hr.at[g, i]).start()

    def spread(g):
        for i in range(2):
            whole_wait(gt_v.at[g, i], hr.at[g, i])

        def send(j):
            remote(gt_v.at[g], gb_v.at[g, chip], gs.at[g], gr.at[g], chip_at(lax.rem(chip + j, 16)))

        loop(1, 16, send)
        pltpu.make_async_copy(gt_v.at[g], gb_v.at[g, chip], gr.at[g]).start()

    def weight_slots(g):
        return [
            jnp.where(g == 0, 1, 6 + 2 * g), jnp.where(g == 0, 0, 7 + 2 * g),
            jnp.where(g == 3, 15, 2 * g + 2), jnp.where(g == 3, 14, 2 * g + 3),
        ]

    def project(g):
        slots = weight_slots(g)
        for slot in slots:
            for m in range(3):
                whole_wait(pw_v.at[slot, m, :, other_lanes], wsr.at[slot, m])
        whole_wait(gb_v.at[g], gr.at[g])
        for i in range(2):
            got = gb_v[g, :, i].astype(F32)
            rows = jnp.concatenate([got[:, :8].reshape(128, 128), got[:, 8:].reshape(128, 128)], 1).astype(BF16)
            cc_v[slots[i]] = rows[:64]
            cc_v[slots[2 + i]] = rows[64:]

        def one(m):
            terms = acc_v[m]
            for slot in slots:
                terms = terms + dot(cc_v[slot], pw_v[slot, m])
            acc_v[m] = terms

        loop(0, 3, one)

    def turn_of(i):
        more = i < GROUPS - 1

        def odd(parts):
            k = 2 * i + 1
            for hp, c in parts:
                got_right(k, hp, c)
                got_left(k, hp, c)
                if hp == 0:
                    pass_right(k + 1, hp, c)
                    pl.when(more)(lambda: pass_left(k + 1, hp, c))
                else:
                    pass_left(k + 1, hp, c)
                    pl.when(more)(lambda: pass_right(k + 1, hp, c))

        def even(parts):
            k = 2 * i + 2
            for hp, c in parts:
                if hp == 0:
                    got_right(k, hp, c)
                else:
                    got_left(k, hp, c)

                @pl.when(more)
                def _():
                    if hp == 0:
                        got_left(k, hp, c)
                    else:
                        got_right(k, hp, c)
                    pass_right(k + 1, hp, c)
                    pass_left(k + 1, hp, c)

        ringing = pl.when(i < GROUPS)
        ringing(lambda: odd(parts[:2]))

        @pl.when(i == 0)
        def _():
            whole_wait(wt_v.at[core], wr.at[0])
            remote(wt_v.at[core], wt_v.at[core], ws.at[2], wr.at[3], sibling)
            pw_own.wait()
            acc_v[...] = jnp.zeros_like(acc_v)

        ringing(lambda: odd(parts[2:]))
        weighing = pl.when(i < GROUPS - 1)
        weighing(lambda: weights_step(i + 3, 0))
        pl.when(i == 0)(lambda: turn(core))
        pl.when((i >= 2) & (i < GROUPS + 2))(lambda: spread(i - 2))
        pl.when((i >= 1) & (i < GROUPS + 1))(lambda: reduce(i - 1))
        pl.when(i == GROUPS + 2)(weights_end)
        ringing(lambda: even(parts[:2]))
        weighing(lambda: weights_step(i + 3, 1))
        ringing(lambda: even(parts[2:]))
        weighing(lambda: weights_step(i + 3, 2))

        @pl.when(i == 0)
        def _():
            whole_wait(wt_v.at[1 - core], wr.at[3])
            turn(1 - core)

        ringing(lambda: conv(i))

        @pl.when((i == GROUPS - 1) | (i == GROUPS))
        def _():
            loop(0, 3, lambda m: weights_step(i + 3, m))

        pl.when(i >= 3)(lambda: project(i - 3))

    loop(0, GROUPS + 3, turn_of)

    first = core == 0

    swaps = []

    def send_back(i, both):
        for c in range(2):
            xs_v[i, c] = both[:, c * 128 : (c + 1) * 128]
            swaps.append(
                remote(xs_v.at[i, c], f_v.at[i, core], xs.at[i, c], xr.at[i, core], plane_at(NZ - 1, c))
            )

    offset = lax.rem(chip - z + NZ, NZ)
    place = jnp.where(offset == 0, 0, jnp.where(offset <= 8, 7 + offset, NZ - offset))
    send_back(1, cc_v[place])
    kv_cp = []
    for m in ORDER:
        both = acc_v[m].astype(BF16)
        if m == 0:
            send_back(0, both)
            continue
        i = m - 1
        for c in range(2):
            ys_v[i, c] = both[:, c * 128 : (c + 1) * 128]
        kv_v[i, 1, core] = jnp.where(first, both[:, :128], both[:, 128:])
        for back, away in ((3, 2), (2, 1), (0, NZ - 1)):
            for c in range(2):
                kv_cp.append(
                    remote(
                        ys_v.at[i, c], kv_v.at[i, back, core], ks.at[i, back, c], kr.at[i, back, core], plane_at(away, c)
                    )
                )
        kv_cp.append(
            remote(ys_v.at[i, 1 - core], kv_v.at[i, 1, core], ks.at[i, 1, 0], kr.at[i, 1, core], sibling)
        )
    for i in range(4):
        whole_wait(pk_v.at[0], fs.at[i])
    whole_wait(wt_v.at[0, pl.ds(0, 7)], ws.at[0])
    whole_wait(wt_v.at[0], ws.at[2])
    for hp in range(2):
        whole_wait(ts_v.at[hp, pl.ds(0, 7)], as_.at[hp])

    @pl.when(core != half)
    def _():
        for hp in range(2):
            whole_wait(ts_v.at[hp, 0], as_.at[2 + hp])

    def ring_left(k):
        for c in range(2):
            for way in range(2):
                whole_wait(acts.at[0, 0, c], zs.at[way, k, way, c])
                pl.when(k < 7)(lambda: whole_wait(acts.at[0, 0, c], zs.at[way, k, 1 - way, c]))

    loop(0, 8, ring_left)
    loop(0, GROUPS, lambda g: whole_wait(sb_v.at[g, pl.ds(0, 15)], ss.at[g]))

    loop(0, GROUPS, lambda g: whole_wait(sb_v.at[g, pl.ds(0, 15)], gs.at[g]))

    def chunks_left(g):
        for i in range(2):
            pl.when((2 * g + i != 1) | (chip >= 8))(lambda: whole_wait(gt_v.at[0, 0], hs.at[g, i]))

    loop(0, GROUPS, chunks_left)

    def weights_left(k):
        for way in range(2):
            for m in range(3):
                whole_wait(held(0, m), wzs.at[way, k, m])

    loop(0, 7, weights_left)
    for m in range(3):
        whole_wait(held(0, m), wzs.at[0 if m == 2 else 1, 7, m])
    loop(0, NZ, lambda k: [whole_wait(held(0, m), wss.at[k, m]) for m in range(3)])
    for i in range(2):
        for c in range(2):
            whole_wait(f_v.at[i, c], xr.at[i, c])
    for cp in swaps:
        cp.wait_send()
    for i in range(2):
        whole_wait(kv_v.at[i, 1, 1 - core], kr.at[i, 1, 1 - core])
        for back in (0, 2, 3):
            for c in range(2):
                whole_wait(kv_v.at[i, back, c], kr.at[i, back, c])

    q = f_v[0].reshape(128, 128)
    keys, vals = [[kv_v[i, back].reshape(128, 128) for back in range(4)] for i in range(2)]
    scores = []
    for back in range(4):
        seen = causal if back == 0 else z >= back
        scores.append(jnp.where(seen, dot_t(q, keys[back]) * SCALE, NEG))
    top = scores[0].max(1, keepdims=True)
    for back in range(1, 4):
        top = jnp.maximum(top, scores[back].max(1, keepdims=True))
    total = None
    mixed = None
    for back in range(4):
        e = jnp.exp(scores[back] - top)
        part_sum = jnp.sum(e, 1, keepdims=True)
        part_mix = dot(e.astype(BF16), vals[back])
        total = part_sum if total is None else total + part_sum
        mixed = part_mix if mixed is None else mixed + part_mix
    co_v[...] = (f_v[1].reshape(128, 128).astype(F32) + mixed / total).astype(BF16)
    co_cp = pltpu.make_async_copy(co_v, coarse_out.at[0], out_sem.at[1])
    co_cp.start()

    for cp in kv_cp:
        cp.wait_send()
    fo_cp.wait()
    co_cp.wait()


def per_device(fine_q, fine_k, fine_v, fine_x, conv_weight, qkv_weight):
    cw = conv_weight.transpose(0, 2, 1)
    pw = qkv_weight[0].transpose(1, 0, 2)
    dma = pltpu.SemaphoreType.DMA
    vmem = pltpu.VMEM
    scratch = [
        vmem((128, 512), BF16), vmem((128, 512), BF16), vmem((128, 512), BF16), vmem((128, 512), BF16),
        vmem((2, 128, 256), BF16), vmem((2, 128, 256), BF16),
        vmem((4, 128, 128), F32),
        vmem((4, 2, 128, 1), F32),
        vmem((128, 512), BF16),
        vmem((2, 8, 16, 256), BF16),
        vmem((16, 2, 2, 4, 16, 256), BF16),
        vmem((2, 8, 32, 512), BF16),
        vmem((2, 512, 256), BF16),
        vmem((16, 3, 256, 256), BF16),
        vmem((4, 16, 2, 16, 128), BF16),
        vmem((4, 16, 2, 16, 128), BF16),
        vmem((4, 2, 16, 128), BF16),
        vmem((4, 2, 16, 128), BF16),
        vmem((4, 16, 2, 16, 128), BF16),
        vmem((16, 64, 256), BF16),
        vmem((3, 64, 256), F32),
        vmem((2, 2, 64, 128), BF16),
        vmem((2, 2, 64, 128), BF16),
        vmem((2, 2, 64, 128), BF16),
        vmem((2, 4, 2, 64, 128), BF16),
        vmem((128, 128), BF16),
        dma((4,)), dma((4,)), dma((4,)), dma((3,)), dma((4,)), dma((4,)), dma((2,)),
        dma((2, 8, 2, 2)), dma((2, 8, 2, 2)),
        dma((4,)), dma((4,)), dma((4,)), dma((4,)),
        dma((4, 2)), dma((4, 2)), dma((2, 8, 3)), dma((2, 8, 3)), dma((16, 3)), dma((16, 3)),
        dma((2, 2)), dma((2, 2)),
        dma((2, 4, 2)), dma((2, 4, 2)), dma((2,)),
    ]
    return pl.pallas_call(
        kernel,
        out_shape=(
            jax.ShapeDtypeStruct((128, 512), BF16),
            jax.ShapeDtypeStruct((1, 128, 128), BF16),
        ),
        in_specs=[pl.BlockSpec(memory_space=pl.ANY)] * 6,
        out_specs=[pl.BlockSpec(memory_space=pl.ANY)] * 2,
        scratch_shapes=scratch,
        compiler_params=pltpu.CompilerParams(
            collective_id=0, has_side_effects=True, vmem_limit_bytes=60 * 1024 * 1024
        ),
    )(fine_q, fine_k, fine_v, fine_x, cw, pw)


def solution(mesh):
    placed = (
        P("ctx", "head"),
        P("ctx", "head"),
        P("ctx", "head"),
        P("ctx", "head"),
        P(None, "head", "ctx"),
        P("ctx", None, None, "head"),
    )
    return jax.shard_map(
        per_device,
        mesh=mesh,
        in_specs=placed,
        out_specs=(P("ctx", "head"), P("ctx", None, "head")),
        check_vma=False,
    )
```

```python
import jax
import jax.numpy as jnp
from jax import lax
from jax.experimental import pallas as pl
from jax.experimental.pallas import tpu as pltpu
from jax.sharding import PartitionSpec as P

STRIDE = 8
HEAD_DIM = 128
NZ = 16
MESH = pl.DeviceIdType.MESH
BF16 = jnp.bfloat16
F32 = jnp.float32
SCALE = HEAD_DIM ** -0.5
NEG = -1e30
GROUPS = 4
TO_RIGHT = (3, 4, 4)
SHIFT = (0, 1, 1)
ORDER = (1, 2, 0)


def slot_of(offset):
    if offset == -4:
        offset = 4
    return -offset if offset <= 0 else 3 + offset


def dot_t(a, b):
    return lax.dot_general(a, b, (((1,), (1,)), ((), ())), preferred_element_type=F32)


def dot(a, b):
    return jnp.dot(a, b, preferred_element_type=F32)


def whole_wait(ref, sem):
    pltpu.make_async_copy(ref, ref, sem).wait()


def kernel(
    q_in, k_in, v_in, x_in, cw_in, pw_in, fine_out, coarse_out,
    q_v, k_v, v_v, x_v, pk_v, pv_v, mix_v, st_v, fo_v, ts_v, acts, wt_v, w2_v, pw_v, p2_v,
    sb_v, rb_v, gs_v, gb_v, cc_v, pr_v, rr_v, rl_v, sr_v, sl_v, r1_v, res_v, xs_v, f_v, ys_v, kv_v, co_v,
    in_sem, fs, fr, ws, wr, as_, ar, zs, zr, ss, sr, gs, gr, pws, pwr, rs_s, rs_r, r1s, r1r, xs, xr, ks, kr, out_sem,
):
    ctx = lax.axis_index("ctx")
    head = lax.axis_index("head")
    z = lax.div(ctx, 8)
    s = lax.rem(ctx, 8)
    yl = lax.div(head, 2)
    core = lax.rem(head, 2)
    chip = 2 * s + yl
    half = lax.div(s, 4)
    quarter = lax.rem(s, 4)
    sibling = (ctx, 2 * yl + 1 - core)
    after = (lax.rem(ctx + 1, 128), head)
    before = (lax.rem(ctx + 127, 128), head)
    right = (lax.rem(z + 2, NZ) * 8 + s, head)
    left = (lax.rem(z + NZ - 2, NZ) * 8 + s, head)
    side = lax.rem(z, 2)
    place_z = lax.div(z, 2)
    twin = z + 1 - 2 * side
    ahead = lax.rem(lax.div(chip, 2) - place_z + 8, 8)
    far = ((2 * ahead + side) * 8 + s, head)
    to_chip = 2 * ahead + lax.rem(chip, 2)

    def chip_at(c):
        return (z * 8 + lax.div(c, 2), lax.rem(c, 2) * 2 + core)

    def loop(low, high, body):
        def step(i, carry):
            body(i)
            return carry

        lax.fori_loop(low, high, step, 0)


    def plane_at(away, c):
        return (lax.rem(z + away, NZ) * 8 + s, 2 * yl + c)

    def remote(src, dst, send, recv, dev):
        cp = pltpu.make_async_remote_copy(
            src_ref=src, dst_ref=dst, send_sem=send, recv_sem=recv, device_id=dev, device_id_type=MESH
        )
        cp.start()
        return cp

    loads = []
    for i, (src, dst) in enumerate([(q_in, q_v), (k_in, k_v), (v_in, v_v), (x_in, x_v)]):
        cp = pltpu.make_async_copy(src, dst, in_sem.at[i])
        cp.start()
        loads.append(cp)

    barrier = pltpu.get_barrier_semaphore()

    def greet(dev):
        pl.semaphore_signal(barrier, inc=1, device_id=dev, device_id_type=MESH)

    for dev in (after, before):
        greet(dev)
    for away in (1, 2, NZ - 2, NZ - 1):
        for c in range(2):
            greet(plane_at(away, c))

    loop(1, 16, lambda j: greet(chip_at(lax.rem(chip + j, 16))))
    loop(0, 8, lambda j: greet((z * 8 + j, 2 * yl + 1 - core)))
    loop(0, 8, lambda j: greet((twin * 8 + j, head)))

    @pl.when(ahead != place_z)
    def _():
        greet(far)

    pl.semaphore_wait(barrier, 41 + jnp.where(ahead != place_z, 1, 0))

    fine_cp = []
    for hp in range(2):
        cols = pl.ds(hp * 256, 256)
        for i, (src, dst) in enumerate([(k_in, pk_v), (v_in, pv_v)]):
            fine_cp.append(remote(src.at[:, cols], dst.at[hp], fs.at[2 * hp + i], fr.at[2 * hp + i], after))

    row = lax.broadcasted_iota(jnp.int32, (128, 128), 0)
    col = lax.broadcasted_iota(jnp.int32, (128, 128), 1)
    causal = col <= row
    for cp in loads:
        cp.wait()

    def own_part(hp):
        for j in range(2):
            i = 2 * hp + j
            cols = pl.ds(pl.multiple_of(i * 128, 128), 128)
            scores = jnp.where(causal, dot_t(q_v[:, cols], k_v[:, cols]) * SCALE, NEG)
            top = jnp.max(scores, 1, keepdims=True)
            e = jnp.exp(scores - top)
            mix_v[i] = dot(e.astype(BF16), v_v[:, cols])
            st_v[i, 0] = top
            st_v[i, 1] = jnp.sum(e, 1, keepdims=True)

    loop(0, 2, own_part)
    has_before = ctx > 0

    def send_weights(j):
        to = lax.rem(s + j, 8)
        remote(cw_in.at[to], wt_v.at[side, core, s], ws.at[3], wr.at[4], (twin * 8 + to, head))

        @pl.when(j > 0)
        def _():
            remote(cw_in.at[to], wt_v.at[side, core, s], ws.at[0], wr.at[0], (z * 8 + to, head))

    def all_weights():
        loop(0, 8, send_weights)
        pltpu.make_async_copy(cw_in.at[s], wt_v.at[side, core, s], wr.at[0]).start()
        for i, (at_z, c) in enumerate([(z, 1 - core), (twin, core), (twin, 1 - core)]):
            remote(pw_in, pw_v.at[side, core], pws.at[i], pwr.at[side, core], (at_z * 8 + s, 2 * yl + c))
        pltpu.make_async_copy(pw_in, pw_v.at[side, core], pwr.at[side, core]).start()

    def whole_part(hp):
        whole_wait(pk_v.at[hp], fr.at[2 * hp])
        whole_wait(pv_v.at[hp], fr.at[2 * hp + 1])
        pl.when(hp == 1)(all_weights)
        for j in range(2):
            i = 2 * hp + j
            cols = pl.ds(pl.multiple_of(i * 128, 128), 128)
            near = slice(j * 128, (j + 1) * 128)
            scores = jnp.where(has_before, dot_t(q_v[:, cols], pk_v[hp, :, near]) * SCALE, NEG)
            own_top, own_sum = st_v[i, 0], st_v[i, 1]
            top = jnp.maximum(own_top, jnp.max(scores, 1, keepdims=True))
            scale = jnp.exp(own_top - top)
            e = jnp.exp(scores - top)
            total = own_sum * scale + jnp.sum(e, 1, keepdims=True)
            mixed = mix_v[i] * scale + dot(e.astype(BF16), pv_v[hp, :, near])
            result = x_v[:, cols].astype(F32) + mixed / total
            mix_v[i] = result
            fo_v[:, cols] = result.astype(BF16)
            for tap in range(8):
                ts_v[hp, tap, :, near] = mix_v[i, pl.ds(tap, 16, stride=8), :].astype(BF16)

        def send(j):
            to = lax.rem(s + j, 8)
            remote(
                ts_v.at[hp, to], acts.at[0, hp, core, quarter], as_.at[hp], ar.at[hp], (z * 8 + to, 2 * yl + half)
            )

        loop(1, 8, send)

        @pl.when(core == half)
        def _():
            pltpu.make_async_copy(ts_v.at[hp, s], acts.at[0, hp, core, quarter], ar.at[hp]).start()

        @pl.when(core != half)
        def _():
            remote(ts_v.at[hp, s], acts.at[0, hp, core, quarter], as_.at[2 + hp], ar.at[hp], sibling)

    loop(0, 2, whole_part)

    parts = [(hp, c) for hp in range(2) for c in range(2)]

    def place_right(k):
        return jnp.where(k == 4, 7, k)

    def place_left(k):
        return jnp.where(k == 0, 0, 3 + k)

    def pass_right(k, hp, c):
        remote(
            acts.at[place_right(k - 1), hp, c], acts.at[place_right(k), hp, c],
            zs.at[0, k - 1, hp, c], zr.at[0, k - 1, hp, c], right,
        )

    def pass_left(k, hp, c):
        remote(
            acts.at[place_left(k - 1), hp, c], acts.at[place_left(k), hp, c],
            zs.at[1, k - 1, hp, c], zr.at[1, k - 1, hp, c], left,
        )

    def got_right(k, hp, c):
        whole_wait(acts.at[place_right(k), hp, c], zr.at[0, k - 1, hp, c])

    def got_left(k, hp, c):
        whole_wait(acts.at[place_left(k), hp, c], zr.at[1, k - 1, hp, c])

    for hp in range(2):
        whole_wait(acts.at[0, hp], ar.at[hp])
        for c in range(2):
            pass_right(1, hp, c)
            pass_left(1, hp, c)

    fo_cp = pltpu.make_async_copy(fo_v, fine_out, out_sem.at[0])
    fo_cp.start()

    def turn(c):
        def part(p):
            for hp in range(2):
                rows = slice(hp * 256, (hp + 1) * 256)
                cols = pl.ds(pl.multiple_of(p * 256, 256), 256)
                w2_v[c, rows, cols] = wt_v[p, c, :, :, rows].reshape(256, 256).T

        loop(0, 2, part)

    def group_slots(g):
        return [g, 4 + g]

    def conv(g):
        total = None
        for hp, c in parts:
            rows = jnp.concatenate([acts[a, hp, c].reshape(64, 256) for a in group_slots(g)], 0)
            term = dot(rows, w2_v[c, hp * 256 : (hp + 1) * 256, :])
            total = term if total is None else total + term
        for i in range(2):
            lo = total[:, i * 256 : i * 256 + 128].reshape(16, 8, 128)
            hi = total[:, i * 256 + 128 : (i + 1) * 256].reshape(16, 8, 128)
            sb_v[g, :, i] = jnp.concatenate([lo, hi], 1).astype(BF16)

        def send(j):
            to = lax.rem(chip + j, 16)
            remote(sb_v.at[g, to], rb_v.at[g, chip], ss.at[g], sr.at[g], chip_at(to))

        loop(1, 16, send)
        pltpu.make_async_copy(sb_v.at[g, chip], rb_v.at[g, chip], sr.at[g]).start()

    def reduce(g):
        whole_wait(rb_v.at[g], sr.at[g])
        gs_v[g] = jnp.sum(rb_v[g].astype(F32), 0).astype(BF16)

        def send(j):
            remote(gs_v.at[g], gb_v.at[g, chip], gs.at[g], gr.at[g], chip_at(lax.rem(chip + j, 16)))

        loop(1, 16, send)
        pltpu.make_async_copy(gs_v.at[g], gb_v.at[g, chip], gr.at[g]).start()

    def project(g):
        whole_wait(gb_v.at[g], gr.at[g])
        rows = []
        for p in range(2):
            got = gb_v[g, :, p].astype(F32)
            rows.append(
                jnp.concatenate([got[:, :8].reshape(128, 128), got[:, 8:].reshape(128, 128)], 1).astype(BF16)
            )
            for i, a in enumerate(group_slots(g)):
                cc_v[a, p] = rows[p][i * 64 : (i + 1) * 64]
        for m in range(3):
            terms = dot(rows[0], p2_v[0, m]) + dot(rows[1], p2_v[1, m])
            for i, a in enumerate(group_slots(g)):
                pr_v[a, m] = terms[i * 64 : (i + 1) * 64]

    def turn_of(i):
        k = i + 1

        def ring(parts):
            for hp, c in parts:
                near, farther = (got_right, got_left) if hp == 0 else (got_left, got_right)
                go, go_too = (pass_right, pass_left) if hp == 0 else (pass_left, pass_right)
                near(k, hp, c)
                pl.when(k < 4)(lambda: go(k + 1, hp, c))

                @pl.when(k < 4)
                def _():
                    farther(k, hp, c)
                    pl.when(k < 3)(lambda: go_too(k + 1, hp, c))

        ringing = pl.when(i < GROUPS)
        ringing(lambda: ring(parts[:2]))

        @pl.when(i == 0)
        def _():
            whole_wait(wt_v.at[side, core], wr.at[0])
            whole_wait(wt_v.at[1 - side, core], wr.at[4])
            for p in range(2):
                remote(wt_v.at[p, core], wt_v.at[p, core], ws.at[1 + p], wr.at[1 + p], sibling)
            for p in range(2):
                for c in range(2):
                    whole_wait(pw_v.at[p, c], pwr.at[p, c])
                    for m in range(3):
                        p2_v[p, m, :, c * 128 : (c + 1) * 128] = pw_v[p, c, m]

        pl.when(i >= 2)(lambda: project(i - 2))
        ringing(lambda: ring(parts[2:3]))
        pl.when((i >= 1) & (i <= GROUPS))(lambda: reduce(i - 1))
        ringing(lambda: ring(parts[3:]))

        @pl.when(i == 0)
        def _():
            turn(core)
            for p in range(2):
                whole_wait(wt_v.at[p, 1 - core], wr.at[1 + p])
            turn(1 - core)

        ringing(lambda: conv(i))

    loop(0, GROUPS + 2, turn_of)

    def place_of(offset):
        return jnp.where(offset <= 0, -offset, 3 + offset)

    def add_right(k, m):
        whole_wait(rr_v.at[k - 1, m], rs_r.at[0, k - 1, m])
        term = rr_v[k - 1, m].astype(F32) + pr_v[place_of(TO_RIGHT[m] - SHIFT[m] - k), m]
        sr_v[k, m] = term.astype(BF16)
        remote(sr_v.at[k, m], rr_v.at[k, m], rs_s.at[0, k, m], rs_r.at[0, k, m], right)

    def add_left(k, m):
        whole_wait(rl_v.at[k - 1, m], rs_r.at[1, k - 1, m])
        term = rl_v[k - 1, m].astype(F32) + pr_v[place_of(k - (7 - TO_RIGHT[m]) - SHIFT[m]), m]
        sl_v[k, m] = term.astype(BF16)
        remote(sl_v.at[k, m], rl_v.at[k, m], rs_s.at[1, k, m], rs_r.at[1, k, m], left)

    for m in ORDER:
        sr_v[0, m] = pr_v[slot_of(3), m].astype(BF16)
        remote(sr_v.at[0, m], rr_v.at[0, m], rs_s.at[0, 0, m], rs_r.at[0, 0, m], right)
        sl_v[0, m] = pr_v[slot_of(4), m].astype(BF16)
        remote(sl_v.at[0, m], rl_v.at[0, m], rs_s.at[1, 0, m], rs_r.at[1, 0, m], left)

    offset = lax.rem(ahead - place_z + 8, 8)
    place = jnp.where(offset == 0, 0, jnp.where(offset <= 4, 3 + offset, 8 - offset))
    columns = cc_v.at[place, lax.rem(chip, 2)]

    @pl.when(ahead != place_z)
    def _():
        remote(columns, r1_v, r1s.at[0], r1r.at[0], far)

    @pl.when(ahead == place_z)
    def _():
        pltpu.make_async_copy(columns, r1_v, r1r.at[0]).start()

    for i in range(4):
        whole_wait(pk_v.at[0], fs.at[i])
    whole_wait(wt_v.at[0, 0, pl.ds(0, 7)], ws.at[0])
    whole_wait(wt_v.at[0, 0], ws.at[3])
    for i in range(2):
        whole_wait(wt_v.at[0, 0], ws.at[1 + i])
    for i in range(3):
        whole_wait(pw_v.at[0, 0], pws.at[i])
    for hp in range(2):
        whole_wait(ts_v.at[hp, pl.ds(0, 7)], as_.at[hp])

    @pl.when(core != half)
    def _():
        for hp in range(2):
            whole_wait(ts_v.at[hp, 0], as_.at[2 + hp])

    def ring_left(k):
        for c in range(2):
            for way in range(2):
                whole_wait(acts.at[0, 0, c], zs.at[way, k, way, c])
                pl.when(k < 3)(lambda: whole_wait(acts.at[0, 0, c], zs.at[way, k, 1 - way, c]))

    loop(0, 4, ring_left)
    loop(0, GROUPS, lambda g: whole_wait(sb_v.at[g, pl.ds(0, 15)], ss.at[g]))

    def sums(k):
        for m in ORDER:
            add_right(k, m)
            add_left(k, m)

        @pl.when(k == 2)
        def _():
            whole_wait(r1_v, r1r.at[0])

            @pl.when(place_z != 0)
            def _():
                remote(r1_v, res_v, r1s.at[1], r1r.at[1], chip_at(to_chip))

            @pl.when(place_z == 0)
            def _():
                pltpu.make_async_copy(r1_v, res_v, r1r.at[1]).start()

    loop(1, 3, sums)
    loop(0, GROUPS, lambda g: whole_wait(sb_v.at[g, pl.ds(0, 15)], gs.at[g]))
    for m in ORDER:
        if TO_RIGHT[m] == 4:
            add_right(3, m)
        else:
            add_left(3, m)

    first = core == 0

    def exchange(i, both):
        f_v[i, core] = jnp.where(first, both[:, :128], both[:, 128:])
        xs_v[i] = jnp.where(first, both[:, 128:], both[:, :128])
        return remote(xs_v.at[i], f_v.at[i, core], xs.at[i], xr.at[i], sibling)

    whole_wait(res_v, r1r.at[1])
    swaps = [exchange(1, res_v[...])]
    kv_cp = []
    for m in ORDER:
        nr = TO_RIGHT[m]
        whole_wait(rr_v.at[nr - 1, m], rs_r.at[0, nr - 1, m])
        whole_wait(rl_v.at[6 - nr, m], rs_r.at[1, 6 - nr, m])
        both = pr_v[slot_of(-SHIFT[m]), m] + rr_v[nr - 1, m].astype(F32) + rl_v[6 - nr, m].astype(F32)
        both = both.astype(BF16)
        if m == 0:
            swaps.append(exchange(0, both))
            continue
        i = m - 1
        for c in range(2):
            ys_v[i, c] = both[:, c * 128 : (c + 1) * 128]
        kv_v[i, 2, core] = jnp.where(first, both[:, :128], both[:, 128:])
        for back, away in ((0, NZ - 2), (1, NZ - 1), (3, 1)):
            for c in range(2):
                kv_cp.append(
                    remote(
                        ys_v.at[i, c], kv_v.at[i, back, core], ks.at[i, back, c], kr.at[i, back, core], plane_at(away, c)
                    )
                )
        kv_cp.append(
            remote(ys_v.at[i, 1 - core], kv_v.at[i, 2, core], ks.at[i, 2, 0], kr.at[i, 2, core], sibling)
        )
    def sums_left(k):
        for m in ORDER:
            for way in range(2):
                whole_wait(sr_v.at[0, m], rs_s.at[way, k, m])

    loop(0, 3, sums_left)
    for m in ORDER:
        whole_wait(sr_v.at[0, m], rs_s.at[0 if TO_RIGHT[m] == 4 else 1, 3, m])

    @pl.when(ahead != place_z)
    def _():
        whole_wait(r1_v, r1s.at[0])

    @pl.when(place_z != 0)
    def _():
        whole_wait(r1_v, r1s.at[1])

    for i in range(2):
        whole_wait(f_v.at[i, 1 - core], xr.at[i])
    for cp in swaps:
        cp.wait_send()
    for i in range(2):
        whole_wait(kv_v.at[i, 2, 1 - core], kr.at[i, 2, 1 - core])
        for back in (0, 1, 3):
            for c in range(2):
                whole_wait(kv_v.at[i, back, c], kr.at[i, back, c])

    q = f_v[0].reshape(128, 128)
    keys, vals = [[kv_v[i, back].reshape(128, 128) for back in range(4)] for i in range(2)]
    scores = []
    for back in range(4):
        seen = causal if back == 0 else z >= back
        scores.append(jnp.where(seen, dot_t(q, keys[back]) * SCALE, NEG))
    top = scores[0].max(1, keepdims=True)
    for back in range(1, 4):
        top = jnp.maximum(top, scores[back].max(1, keepdims=True))
    total = None
    mixed = None
    for back in range(4):
        e = jnp.exp(scores[back] - top)
        part_sum = jnp.sum(e, 1, keepdims=True)
        part_mix = dot(e.astype(BF16), vals[back])
        total = part_sum if total is None else total + part_sum
        mixed = part_mix if mixed is None else mixed + part_mix
    co_v[...] = (f_v[1].reshape(128, 128).astype(F32) + mixed / total).astype(BF16)
    co_cp = pltpu.make_async_copy(co_v, coarse_out.at[0], out_sem.at[1])
    co_cp.start()

    for cp in kv_cp:
        cp.wait_send()
    fo_cp.wait()
    co_cp.wait()


def per_device(fine_q, fine_k, fine_v, fine_x, conv_weight, qkv_weight):
    cw = conv_weight.transpose(0, 2, 1)
    pw = qkv_weight[0].transpose(1, 0, 2)
    dma = pltpu.SemaphoreType.DMA
    vmem = pltpu.VMEM
    scratch = [
        vmem((128, 512), BF16), vmem((128, 512), BF16), vmem((128, 512), BF16), vmem((128, 512), BF16),
        vmem((2, 128, 256), BF16), vmem((2, 128, 256), BF16),
        vmem((4, 128, 128), F32),
        vmem((4, 2, 128, 1), F32),
        vmem((128, 512), BF16),
        vmem((2, 8, 16, 256), BF16),
        vmem((8, 2, 2, 4, 16, 256), BF16),
        vmem((2, 2, 8, 32, 512), BF16),
        vmem((2, 512, 512), BF16),
        vmem((2, 2, 3, 256, 128), BF16),
        vmem((2, 3, 256, 256), BF16),
        vmem((4, 16, 2, 16, 128), BF16),
        vmem((4, 16, 2, 16, 128), BF16),
        vmem((4, 2, 16, 128), BF16),
        vmem((4, 16, 2, 16, 128), BF16),
        vmem((8, 2, 64, 256), BF16),
        vmem((8, 3, 64, 256), F32),
        vmem((4, 3, 64, 256), BF16),
        vmem((4, 3, 64, 256), BF16),
        vmem((4, 3, 64, 256), BF16),
        vmem((4, 3, 64, 256), BF16),
        vmem((64, 256), BF16),
        vmem((64, 256), BF16),
        vmem((2, 64, 128), BF16),
        vmem((2, 2, 64, 128), BF16),
        vmem((2, 2, 64, 128), BF16),
        vmem((2, 4, 2, 64, 128), BF16),
        vmem((128, 128), BF16),
        dma((4,)), dma((4,)), dma((4,)), dma((4,)), dma((5,)), dma((4,)), dma((2,)),
        dma((2, 4, 2, 2)), dma((2, 4, 2, 2)),
        dma((4,)), dma((4,)), dma((4,)), dma((4,)),
        dma((3,)), dma((2, 2)), dma((2, 4, 3)), dma((2, 4, 3)),
        dma((2,)), dma((2,)), dma((2,)), dma((2,)),
        dma((2, 4, 2)), dma((2, 4, 2)), dma((2,)),
    ]
    return pl.pallas_call(
        kernel,
        out_shape=(
            jax.ShapeDtypeStruct((128, 512), BF16),
            jax.ShapeDtypeStruct((1, 128, 128), BF16),
        ),
        in_specs=[pl.BlockSpec(memory_space=pl.ANY)] * 6,
        out_specs=[pl.BlockSpec(memory_space=pl.ANY)] * 2,
        scratch_shapes=scratch,
        compiler_params=pltpu.CompilerParams(
            collective_id=0, has_side_effects=True, vmem_limit_bytes=60 * 1024 * 1024
        ),
    )(fine_q, fine_k, fine_v, fine_x, cw, pw)


def solution(mesh):
    placed = (
        P("ctx", "head"),
        P("ctx", "head"),
        P("ctx", "head"),
        P("ctx", "head"),
        P(None, "head", "ctx"),
        P("ctx", None, None, "head"),
    )
    return jax.shard_map(
        per_device,
        mesh=mesh,
        in_specs=placed,
        out_specs=(P("ctx", "head"), P("ctx", None, "head")),
        check_vma=False,
    )
```

```python
import jax
import jax.numpy as jnp
from jax import lax
from jax.experimental import pallas as pl
from jax.experimental.pallas import tpu as pltpu
from jax.sharding import PartitionSpec as P

STRIDE = 8
HEAD_DIM = 128
NZ = 16
MESH = pl.DeviceIdType.MESH
BF16 = jnp.bfloat16
F32 = jnp.float32
SCALE = HEAD_DIM ** -0.5
NEG = -1e30
GROUPS = 4
ORDER = (1, 2, 0)


def slot_of(offset):
    if offset == -8:
        offset = 8
    return -offset if offset <= 0 else 7 + offset


def dot_t(a, b):
    return lax.dot_general(a, b, (((1,), (1,)), ((), ())), preferred_element_type=F32)


def dot(a, b):
    return jnp.dot(a, b, preferred_element_type=F32)


def whole_wait(ref, sem):
    pltpu.make_async_copy(ref, ref, sem).wait()


def kernel(
    q_in, k_in, v_in, x_in, cw_in, pw_in, fine_out, coarse_out,
    q_v, k_v, v_v, x_v, pk_v, pv_v, mix_v, st_v, fo_v, ts_v, acts, wt_v, w2_v, pw_v,
    sb_v, rb_v, gs_v, gt_v, gb_v, cc_v, acc_v, xs_v, f_v, ys_v, kv_v, co_v,
    in_sem, fs, fr, ws, wr, as_, ar, zs, zr, ss, sr, gs, gr, hs, hr, wzs, wzr, wss, wsr, xs, xr, ks, kr, out_sem,
):
    ctx = lax.axis_index("ctx")
    head = lax.axis_index("head")
    z = lax.div(ctx, 8)
    s = lax.rem(ctx, 8)
    yl = lax.div(head, 2)
    core = lax.rem(head, 2)
    chip = 2 * s + yl
    half = lax.div(s, 4)
    quarter = lax.rem(s, 4)
    sibling = (ctx, 2 * yl + 1 - core)
    after = (lax.rem(ctx + 1, 128), head)
    before = (lax.rem(ctx + 127, 128), head)
    right = (lax.rem(z + 1, NZ) * 8 + s, head)
    left = (lax.rem(z + NZ - 1, NZ) * 8 + s, head)

    def chip_at(c):
        return (z * 8 + lax.div(c, 2), lax.rem(c, 2) * 2 + core)

    def loop(low, high, body):
        def step(i, carry):
            body(i)
            return carry

        lax.fori_loop(low, high, step, 0)


    def plane_at(away, c):
        return (lax.rem(z + away, NZ) * 8 + s, 2 * yl + c)

    def remote(src, dst, send, recv, dev):
        cp = pltpu.make_async_remote_copy(
            src_ref=src, dst_ref=dst, send_sem=send, recv_sem=recv, device_id=dev, device_id_type=MESH
        )
        cp.start()
        return cp

    loads = []
    for i, (src, dst) in enumerate([(q_in, q_v), (k_in, k_v), (v_in, v_v), (x_in, x_v)]):
        cp = pltpu.make_async_copy(src, dst, in_sem.at[i])
        cp.start()
        loads.append(cp)

    barrier = pltpu.get_barrier_semaphore()

    def greet(dev):
        pl.semaphore_signal(barrier, inc=1, device_id=dev, device_id_type=MESH)

    for dev in (after, before):
        greet(dev)
    loop(1, NZ, lambda j: greet(plane_at(j, core)))
    for away in (1, 2, NZ - 2, NZ - 1):
        greet(plane_at(away, 1 - core))
    loop(1, 16, lambda j: greet(chip_at(lax.rem(chip + j, 16))))
    loop(0, 8, lambda j: greet((z * 8 + j, 2 * yl + 1 - core)))

    pl.semaphore_wait(barrier, 44)

    fine_cp = []
    for hp in range(2):
        cols = pl.ds(hp * 256, 256)
        for i, (src, dst) in enumerate([(k_in, pk_v), (v_in, pv_v)]):
            fine_cp.append(remote(src.at[:, cols], dst.at[hp], fs.at[2 * hp + i], fr.at[2 * hp + i], after))

    lanes = pl.ds(pl.multiple_of(core * 128, 128), 128)
    other_lanes = pl.ds(pl.multiple_of((1 - core) * 128, 128), 128)

    def held(slot, m):
        return pw_v.at[slot, m, :, lanes]

    pw_own = pltpu.make_async_copy(pw_in, pw_v.at[0, :, :, lanes], wr.at[2])
    pw_own.start()
    for m in range(3):
        remote(pw_in.at[m], held(1, m), wzs.at[0, 0, m], wzr.at[0, 0, m], right)
        remote(pw_in.at[m], held(8, m), wzs.at[1, 0, m], wzr.at[1, 0, m], left)
    for m in range(3):
        remote(pw_in.at[m], held(0, m), wss.at[0, m], wsr.at[0, m], sibling)

    def weights_step(k, m):
        whole_wait(held(k, m), wzr.at[0, k - 1, m])
        whole_wait(held(7 + k, m), wzr.at[1, k - 1, m])

        @pl.when((k < 7) | (m == 2))
        def _():
            remote(held(k, m), held(jnp.where(k == 7, 15, k + 1), m), wzs.at[0, k, m], wzr.at[0, k, m], right)

        @pl.when((k < 7) | (m != 2))
        def _():
            remote(held(7 + k, m), held(8 + k, m), wzs.at[1, k, m], wzr.at[1, k, m], left)

        @pl.when((k == 7) & (m == 2))
        def _():
            remote(held(7, m), held(15, m), wss.at[15, m], wsr.at[15, m], plane_at(1, 1 - core))

        @pl.when((k == 7) & (m != 2))
        def _():
            remote(held(14, m), held(15, m), wss.at[15, m], wsr.at[15, m], plane_at(NZ - 1, 1 - core))

        remote(held(k, m), held(k, m), wss.at[k, m], wsr.at[k, m], sibling)
        remote(held(7 + k, m), held(7 + k, m), wss.at[7 + k, m], wsr.at[7 + k, m], sibling)

    def weights_end():
        for m in range(3):
            way = 0 if m == 2 else 1
            whole_wait(held(15, m), wzr.at[way, 7, m])

    row = lax.broadcasted_iota(jnp.int32, (128, 128), 0)
    col = lax.broadcasted_iota(jnp.int32, (128, 128), 1)
    causal = col <= row
    for cp in loads:
        cp.wait()

    def own_part(hp):
        for j in range(2):
            i = 2 * hp + j
            cols = pl.ds(pl.multiple_of(i * 128, 128), 128)
            scores = jnp.where(causal, dot_t(q_v[:, cols], k_v[:, cols]) * SCALE, NEG)
            top = jnp.max(scores, 1, keepdims=True)
            e = jnp.exp(scores - top)
            mix_v[i] = dot(e.astype(BF16), v_v[:, cols])
            st_v[i, 0] = top
            st_v[i, 1] = jnp.sum(e, 1, keepdims=True)

    loop(0, 2, own_part)
    has_before = ctx > 0

    def send_weights(j):
        to = lax.rem(s + j, 8)
        remote(cw_in.at[to], wt_v.at[core, s], ws.at[0], wr.at[0], (z * 8 + to, head))

    def all_weights():
        loop(1, 8, send_weights)
        pltpu.make_async_copy(cw_in.at[s], wt_v.at[core, s], wr.at[0]).start()

    def whole_part(hp):
        whole_wait(pk_v.at[hp], fr.at[2 * hp])
        whole_wait(pv_v.at[hp], fr.at[2 * hp + 1])
        pl.when(hp == 1)(all_weights)
        for j in range(2):
            i = 2 * hp + j
            cols = pl.ds(pl.multiple_of(i * 128, 128), 128)
            near = slice(j * 128, (j + 1) * 128)
            scores = jnp.where(has_before, dot_t(q_v[:, cols], pk_v[hp, :, near]) * SCALE, NEG)
            own_top, own_sum = st_v[i, 0], st_v[i, 1]
            top = jnp.maximum(own_top, jnp.max(scores, 1, keepdims=True))
            scale = jnp.exp(own_top - top)
            e = jnp.exp(scores - top)
            total = own_sum * scale + jnp.sum(e, 1, keepdims=True)
            mixed = mix_v[i] * scale + dot(e.astype(BF16), pv_v[hp, :, near])
            result = x_v[:, cols].astype(F32) + mixed / total
            mix_v[i] = result
            fo_v[:, cols] = result.astype(BF16)
            for tap in range(8):
                ts_v[hp, tap, :, near] = mix_v[i, pl.ds(tap, 16, stride=8), :].astype(BF16)

        def send(j):
            to = lax.rem(s + j, 8)
            remote(
                ts_v.at[hp, to], acts.at[0, hp, core, quarter], as_.at[hp], ar.at[hp], (z * 8 + to, 2 * yl + half)
            )

        loop(1, 8, send)

        @pl.when(core == half)
        def _():
            pltpu.make_async_copy(ts_v.at[hp, s], acts.at[0, hp, core, quarter], ar.at[hp]).start()

        @pl.when(core != half)
        def _():
            remote(ts_v.at[hp, s], acts.at[0, hp, core, quarter], as_.at[2 + hp], ar.at[hp], sibling)

        @pl.when(hp == 0)
        def _():
            loop(1, 3, lambda m: weights_step(1, m))

        pl.when(hp == 1)(lambda: weights_step(2, 0))


    weights_step(1, 0)
    loop(0, 2, whole_part)

    parts = [(hp, c) for hp in range(2) for c in range(2)]

    def place_right(k):
        return jnp.where(k == 8, 15, k)

    def place_left(k):
        return jnp.where(k == 0, 0, 7 + k)

    def pass_right(k, hp, c):
        remote(
            acts.at[place_right(k - 1), hp, c], acts.at[place_right(k), hp, c],
            zs.at[0, k - 1, hp, c], zr.at[0, k - 1, hp, c], right,
        )

    def pass_left(k, hp, c):
        remote(
            acts.at[place_left(k - 1), hp, c], acts.at[place_left(k), hp, c],
            zs.at[1, k - 1, hp, c], zr.at[1, k - 1, hp, c], left,
        )

    def got_right(k, hp, c):
        whole_wait(acts.at[place_right(k), hp, c], zr.at[0, k - 1, hp, c])

    def got_left(k, hp, c):
        whole_wait(acts.at[place_left(k), hp, c], zr.at[1, k - 1, hp, c])

    for hp in range(2):
        whole_wait(acts.at[0, hp], ar.at[hp])
        for c in range(2):
            pass_right(1, hp, c)
            pass_left(1, hp, c)

    loop(1, 3, lambda m: weights_step(2, m))
    fo_cp = pltpu.make_async_copy(fo_v, fine_out, out_sem.at[0])
    fo_cp.start()

    def turn(c):
        def part(hp):
            cols = pl.ds(pl.multiple_of(hp * 256, 256), 256)
            w2_v[c, cols, :] = wt_v[c, :, :, cols].reshape(256, 256).T

        loop(0, 2, part)

    def group_slots(g):
        return [2 * g, 2 * g + 8, 2 * g + 1, 2 * g + 9]

    def conv(g):
        total = None
        for hp, c in parts:
            rows = jnp.concatenate([acts[a, hp, c].reshape(64, 256) for a in group_slots(g)], 0)
            term = dot(rows, w2_v[c, hp * 256 : (hp + 1) * 256, :])
            total = term if total is None else total + term
        for i in range(2):
            lo = total[i * 128 : (i + 1) * 128, :128].reshape(16, 8, 128)
            hi = total[i * 128 : (i + 1) * 128, 128:].reshape(16, 8, 128)
            sb_v[g, :, i] = jnp.concatenate([lo, hi], 1).astype(BF16)

        def send(j):
            to = lax.rem(chip + j, 16)
            remote(sb_v.at[g, to], rb_v.at[g, chip], ss.at[g], sr.at[g], chip_at(to))

        loop(1, 16, send)
        pltpu.make_async_copy(sb_v.at[g, chip], rb_v.at[g, chip], sr.at[g]).start()

    def reduce(g):
        whole_wait(rb_v.at[g], sr.at[g])
        gs_v[g] = jnp.sum(rb_v[g].astype(F32), 0).astype(BF16)

        for i in range(2):
            p = 2 * g + i
            away = jnp.where(chip < 8, lax.rem(NZ + 1 - p, NZ), p + 2)

            @pl.when(away != 0)
            def _():
                remote(gs_v.at[g, i], gt_v.at[g, i], hs.at[g, i], hr.at[g, i], plane_at(away, core))

            @pl.when(away == 0)
            def _():
                pltpu.make_async_copy(gs_v.at[g, i], gt_v.at[g, i], hr.at[g, i]).start()

    def spread(g):
        for i in range(2):
            whole_wait(gt_v.at[g, i], hr.at[g, i])

        def send(j):
            remote(gt_v.at[g], gb_v.at[g, chip], gs.at[g], gr.at[g], chip_at(lax.rem(chip + j, 16)))

        loop(1, 16, send)
        pltpu.make_async_copy(gt_v.at[g], gb_v.at[g, chip], gr.at[g]).start()

    def weight_slots(g):
        return [
            jnp.where(g == 0, 1, 6 + 2 * g), jnp.where(g == 0, 0, 7 + 2 * g),
            jnp.where(g == 3, 15, 2 * g + 2), jnp.where(g == 3, 14, 2 * g + 3),
        ]

    def project(g):
        slots = weight_slots(g)
        for slot in slots:
            for m in range(3):
                whole_wait(pw_v.at[slot, m, :, other_lanes], wsr.at[slot, m])
        whole_wait(gb_v.at[g], gr.at[g])
        for i in range(2):
            got = gb_v[g, :, i].astype(F32)
            rows = jnp.concatenate([got[:, :8].reshape(128, 128), got[:, 8:].reshape(128, 128)], 1).astype(BF16)
            cc_v[slots[i]] = rows[:64]
            cc_v[slots[2 + i]] = rows[64:]

        def one(m):
            terms = acc_v[m]
            for slot in slots:
                terms = terms + dot(cc_v[slot], pw_v[slot, m])
            acc_v[m] = terms

        loop(0, 3, one)

    def turn_of(i):
        more = i < GROUPS - 1

        def odd(parts):
            k = 2 * i + 1
            for hp, c in parts:
                got_right(k, hp, c)
                got_left(k, hp, c)
                if hp == 0:
                    pass_right(k + 1, hp, c)
                    pl.when(more)(lambda: pass_left(k + 1, hp, c))
                else:
                    pass_left(k + 1, hp, c)
                    pl.when(more)(lambda: pass_right(k + 1, hp, c))

        def even(parts):
            k = 2 * i + 2
            for hp, c in parts:
                if hp == 0:
                    got_right(k, hp, c)
                else:
                    got_left(k, hp, c)

                @pl.when(more)
                def _():
                    if hp == 0:
                        got_left(k, hp, c)
                    else:
                        got_right(k, hp, c)
                    pass_right(k + 1, hp, c)
                    pass_left(k + 1, hp, c)

        ringing = pl.when(i < GROUPS)
        ringing(lambda: odd(parts[:2]))

        ringing(lambda: odd(parts[2:]))

        @pl.when(i == 0)
        def _():
            whole_wait(wt_v.at[core], wr.at[0])
            remote(wt_v.at[core], wt_v.at[core], ws.at[2], wr.at[3], sibling)
            pw_own.wait()
            acc_v[...] = jnp.zeros_like(acc_v)

        weighing = pl.when(i < GROUPS - 1)
        weighing(lambda: weights_step(i + 3, 0))
        pl.when((i >= 2) & (i < GROUPS + 2))(lambda: spread(i - 2))
        pl.when((i >= 1) & (i < GROUPS + 1))(lambda: reduce(i - 1))
        pl.when(i == GROUPS + 2)(weights_end)
        ringing(lambda: even(parts[:2]))
        pl.when(i == 0)(lambda: turn(core))
        weighing(lambda: weights_step(i + 3, 1))
        ringing(lambda: even(parts[2:]))
        weighing(lambda: weights_step(i + 3, 2))

        @pl.when(i == 0)
        def _():
            whole_wait(wt_v.at[1 - core], wr.at[3])
            turn(1 - core)

        ringing(lambda: conv(i))

        @pl.when((i == GROUPS - 1) | (i == GROUPS))
        def _():
            loop(0, 3, lambda m: weights_step(i + 3, m))

        pl.when(i >= 3)(lambda: project(i - 3))

    loop(0, GROUPS + 3, turn_of)

    first = core == 0

    swaps = []

    def send_back(i, both):
        for c in range(2):
            xs_v[i, c] = both[:, c * 128 : (c + 1) * 128]
            swaps.append(
                remote(xs_v.at[i, c], f_v.at[i, core], xs.at[i, c], xr.at[i, core], plane_at(NZ - 1, c))
            )

    offset = lax.rem(chip - z + NZ, NZ)
    place = jnp.where(offset == 0, 0, jnp.where(offset <= 8, 7 + offset, NZ - offset))
    send_back(1, cc_v[place])
    kv_cp = []
    for m in ORDER:
        both = acc_v[m].astype(BF16)
        if m == 0:
            send_back(0, both)
            continue
        i = m - 1
        for c in range(2):
            ys_v[i, c] = both[:, c * 128 : (c + 1) * 128]
        kv_v[i, 1, core] = jnp.where(first, both[:, :128], both[:, 128:])
        for back, away in ((3, 2), (2, 1), (0, NZ - 1)):
            for c in range(2):
                kv_cp.append(
                    remote(
                        ys_v.at[i, c], kv_v.at[i, back, core], ks.at[i, back, c], kr.at[i, back, core], plane_at(away, c)
                    )
                )
        kv_cp.append(
            remote(ys_v.at[i, 1 - core], kv_v.at[i, 1, core], ks.at[i, 1, 0], kr.at[i, 1, core], sibling)
        )
    for i in range(4):
        whole_wait(pk_v.at[0], fs.at[i])
    whole_wait(wt_v.at[0, pl.ds(0, 7)], ws.at[0])
    whole_wait(wt_v.at[0], ws.at[2])
    for hp in range(2):
        whole_wait(ts_v.at[hp, pl.ds(0, 7)], as_.at[hp])

    @pl.when(core != half)
    def _():
        for hp in range(2):
            whole_wait(ts_v.at[hp, 0], as_.at[2 + hp])

    def ring_left(k):
        for c in range(2):
            for way in range(2):
                whole_wait(acts.at[0, 0, c], zs.at[way, k, way, c])
                pl.when(k < 7)(lambda: whole_wait(acts.at[0, 0, c], zs.at[way, k, 1 - way, c]))

    loop(0, 8, ring_left)
    loop(0, GROUPS, lambda g: whole_wait(sb_v.at[g, pl.ds(0, 15)], ss.at[g]))

    loop(0, GROUPS, lambda g: whole_wait(sb_v.at[g, pl.ds(0, 15)], gs.at[g]))

    def chunks_left(g):
        for i in range(2):
            pl.when((2 * g + i != 1) | (chip >= 8))(lambda: whole_wait(gt_v.at[0, 0], hs.at[g, i]))

    loop(0, GROUPS, chunks_left)

    def weights_left(k):
        for way in range(2):
            for m in range(3):
                whole_wait(held(0, m), wzs.at[way, k, m])

    loop(0, 7, weights_left)
    for m in range(3):
        whole_wait(held(0, m), wzs.at[0 if m == 2 else 1, 7, m])
    loop(0, NZ, lambda k: [whole_wait(held(0, m), wss.at[k, m]) for m in range(3)])
    for i in range(2):
        for c in range(2):
            whole_wait(f_v.at[i, c], xr.at[i, c])
    for cp in swaps:
        cp.wait_send()
    for i in range(2):
        whole_wait(kv_v.at[i, 1, 1 - core], kr.at[i, 1, 1 - core])
        for back in (0, 2, 3):
            for c in range(2):
                whole_wait(kv_v.at[i, back, c], kr.at[i, back, c])

    q = f_v[0].reshape(128, 128)
    keys, vals = [[kv_v[i, back].reshape(128, 128) for back in range(4)] for i in range(2)]
    scores = []
    for back in range(4):
        seen = causal if back == 0 else z >= back
        scores.append(jnp.where(seen, dot_t(q, keys[back]) * SCALE, NEG))
    top = scores[0].max(1, keepdims=True)
    for back in range(1, 4):
        top = jnp.maximum(top, scores[back].max(1, keepdims=True))
    total = None
    mixed = None
    for back in range(4):
        e = jnp.exp(scores[back] - top)
        part_sum = jnp.sum(e, 1, keepdims=True)
        part_mix = dot(e.astype(BF16), vals[back])
        total = part_sum if total is None else total + part_sum
        mixed = part_mix if mixed is None else mixed + part_mix
    co_v[...] = (f_v[1].reshape(128, 128).astype(F32) + mixed / total).astype(BF16)
    co_cp = pltpu.make_async_copy(co_v, coarse_out.at[0], out_sem.at[1])
    co_cp.start()

    for cp in kv_cp:
        cp.wait_send()
    fo_cp.wait()
    co_cp.wait()


def per_device(fine_q, fine_k, fine_v, fine_x, conv_weight, qkv_weight):
    cw = conv_weight.transpose(0, 2, 1)
    pw = qkv_weight[0].transpose(1, 0, 2)
    dma = pltpu.SemaphoreType.DMA
    vmem = pltpu.VMEM
    scratch = [
        vmem((128, 512), BF16), vmem((128, 512), BF16), vmem((128, 512), BF16), vmem((128, 512), BF16),
        vmem((2, 128, 256), BF16), vmem((2, 128, 256), BF16),
        vmem((4, 128, 128), F32),
        vmem((4, 2, 128, 1), F32),
        vmem((128, 512), BF16),
        vmem((2, 8, 16, 256), BF16),
        vmem((16, 2, 2, 4, 16, 256), BF16),
        vmem((2, 8, 32, 512), BF16),
        vmem((2, 512, 256), BF16),
        vmem((16, 3, 256, 256), BF16),
        vmem((4, 16, 2, 16, 128), BF16),
        vmem((4, 16, 2, 16, 128), BF16),
        vmem((4, 2, 16, 128), BF16),
        vmem((4, 2, 16, 128), BF16),
        vmem((4, 16, 2, 16, 128), BF16),
        vmem((16, 64, 256), BF16),
        vmem((3, 64, 256), F32),
        vmem((2, 2, 64, 128), BF16),
        vmem((2, 2, 64, 128), BF16),
        vmem((2, 2, 64, 128), BF16),
        vmem((2, 4, 2, 64, 128), BF16),
        vmem((128, 128), BF16),
        dma((4,)), dma((4,)), dma((4,)), dma((3,)), dma((4,)), dma((4,)), dma((2,)),
        dma((2, 8, 2, 2)), dma((2, 8, 2, 2)),
        dma((4,)), dma((4,)), dma((4,)), dma((4,)),
        dma((4, 2)), dma((4, 2)), dma((2, 8, 3)), dma((2, 8, 3)), dma((16, 3)), dma((16, 3)),
        dma((2, 2)), dma((2, 2)),
        dma((2, 4, 2)), dma((2, 4, 2)), dma((2,)),
    ]
    return pl.pallas_call(
        kernel,
        out_shape=(
            jax.ShapeDtypeStruct((128, 512), BF16),
            jax.ShapeDtypeStruct((1, 128, 128), BF16),
        ),
        in_specs=[pl.BlockSpec(memory_space=pl.ANY)] * 6,
        out_specs=[pl.BlockSpec(memory_space=pl.ANY)] * 2,
        scratch_shapes=scratch,
        compiler_params=pltpu.CompilerParams(
            collective_id=0, has_side_effects=True, vmem_limit_bytes=60 * 1024 * 1024
        ),
    )(fine_q, fine_k, fine_v, fine_x, cw, pw)


def solution(mesh):
    placed = (
        P("ctx", "head"),
        P("ctx", "head"),
        P("ctx", "head"),
        P("ctx", "head"),
        P(None, "head", "ctx"),
        P("ctx", None, None, "head"),
    )
    return jax.shard_map(
        per_device,
        mesh=mesh,
        in_specs=placed,
        out_specs=(P("ctx", "head"), P("ctx", None, "head")),
        check_vma=False,
    )
```

```python
import jax
import jax.numpy as jnp
from jax import lax
from jax.experimental import pallas as pl
from jax.experimental.pallas import tpu as pltpu
from jax.sharding import PartitionSpec as P

STRIDE = 8
HEAD_DIM = 128
NZ = 16
MESH = pl.DeviceIdType.MESH
BF16 = jnp.bfloat16
F32 = jnp.float32
SCALE = HEAD_DIM ** -0.5
NEG = -1e30
GROUPS = 4
ORDER = (1, 0, 2)


def slot_of(offset):
    if offset == -8:
        offset = 8
    return -offset if offset <= 0 else 7 + offset


def dot_t(a, b):
    return lax.dot_general(a, b, (((1,), (1,)), ((), ())), preferred_element_type=F32)


def dot(a, b):
    return jnp.dot(a, b, preferred_element_type=F32)


def whole_wait(ref, sem):
    pltpu.make_async_copy(ref, ref, sem).wait()


def kernel(
    q_in, k_in, v_in, x_in, cw_in, pw_in, fine_out, coarse_out,
    q_v, k_v, v_v, x_v, pk_v, pv_v, mix_v, st_v, fo_v, ts_v, acts, wt_v, w2_v, pw_v,
    sb_v, rb_v, gs_v, gt_v, gb_v, cc_v, acc_v, xs_v, f_v, ys_v, kv_v, co_v,
    in_sem, fs, fr, ws, wr, as_, ar, zs, zr, ss, sr, gs, gr, hs, hr, wzs, wzr, wss, wsr, xs, xr, ks, kr, out_sem,
):
    ctx = lax.axis_index("ctx")
    head = lax.axis_index("head")
    z = lax.div(ctx, 8)
    s = lax.rem(ctx, 8)
    yl = lax.div(head, 2)
    core = lax.rem(head, 2)
    chip = 2 * s + yl
    half = lax.div(s, 4)
    quarter = lax.rem(s, 4)
    sibling = (ctx, 2 * yl + 1 - core)
    after = (lax.rem(ctx + 1, 128), head)
    before = (lax.rem(ctx + 127, 128), head)
    right = (lax.rem(z + 1, NZ) * 8 + s, head)
    left = (lax.rem(z + NZ - 1, NZ) * 8 + s, head)

    def chip_at(c):
        return (z * 8 + lax.div(c, 2), lax.rem(c, 2) * 2 + core)

    def loop(low, high, body):
        def step(i, carry):
            body(i)
            return carry

        lax.fori_loop(low, high, step, 0)


    def plane_at(away, c):
        return (lax.rem(z + away, NZ) * 8 + s, 2 * yl + c)

    def remote(src, dst, send, recv, dev):
        cp = pltpu.make_async_remote_copy(
            src_ref=src, dst_ref=dst, send_sem=send, recv_sem=recv, device_id=dev, device_id_type=MESH
        )
        cp.start()
        return cp

    loads = []
    for i, (src, dst) in enumerate([(q_in, q_v), (k_in, k_v), (v_in, v_v), (x_in, x_v)]):
        cp = pltpu.make_async_copy(src, dst, in_sem.at[i])
        cp.start()
        loads.append(cp)

    barrier = pltpu.get_barrier_semaphore()

    def greet(dev):
        pl.semaphore_signal(barrier, inc=1, device_id=dev, device_id_type=MESH)

    for dev in (after, before):
        greet(dev)
    loop(1, NZ, lambda j: greet(plane_at(j, core)))
    for away in (1, 2, NZ - 2, NZ - 1):
        greet(plane_at(away, 1 - core))
    loop(1, 16, lambda j: greet(chip_at(lax.rem(chip + j, 16))))
    loop(0, 8, lambda j: greet((z * 8 + j, 2 * yl + 1 - core)))

    pl.semaphore_wait(barrier, 44)

    fine_cp = []
    for hp in range(2):
        cols = pl.ds(hp * 256, 256)
        for i, (src, dst) in enumerate([(k_in, pk_v), (v_in, pv_v)]):
            fine_cp.append(remote(src.at[:, cols], dst.at[hp], fs.at[2 * hp + i], fr.at[2 * hp + i], after))

    lanes = pl.ds(pl.multiple_of(core * 128, 128), 128)
    other_lanes = pl.ds(pl.multiple_of((1 - core) * 128, 128), 128)

    def held(slot, m):
        return pw_v.at[slot, m, :, lanes]

    pw_own = pltpu.make_async_copy(pw_in, pw_v.at[0, :, :, lanes], wr.at[2])
    pw_own.start()
    for m in range(3):
        remote(pw_in.at[m], held(1, m), wzs.at[0, 0, m], wzr.at[0, 0, m], right)
        remote(pw_in.at[m], held(8, m), wzs.at[1, 0, m], wzr.at[1, 0, m], left)
    for m in range(3):
        remote(pw_in.at[m], held(0, m), wss.at[0, m], wsr.at[0, m], sibling)

    def weights_step(k, m):
        whole_wait(held(k, m), wzr.at[0, k - 1, m])
        whole_wait(held(7 + k, m), wzr.at[1, k - 1, m])

        @pl.when((k < 7) | (m == 2))
        def _():
            remote(held(k, m), held(jnp.where(k == 7, 15, k + 1), m), wzs.at[0, k, m], wzr.at[0, k, m], right)

        @pl.when((k < 7) | (m != 2))
        def _():
            remote(held(7 + k, m), held(8 + k, m), wzs.at[1, k, m], wzr.at[1, k, m], left)

        @pl.when((k == 7) & (m == 2))
        def _():
            remote(held(7, m), held(15, m), wss.at[15, m], wsr.at[15, m], plane_at(1, 1 - core))

        @pl.when((k == 7) & (m != 2))
        def _():
            remote(held(14, m), held(15, m), wss.at[15, m], wsr.at[15, m], plane_at(NZ - 1, 1 - core))

        remote(held(k, m), held(k, m), wss.at[k, m], wsr.at[k, m], sibling)
        remote(held(7 + k, m), held(7 + k, m), wss.at[7 + k, m], wsr.at[7 + k, m], sibling)

    def weights_end():
        for m in range(3):
            way = 0 if m == 2 else 1
            whole_wait(held(15, m), wzr.at[way, 7, m])

    row = lax.broadcasted_iota(jnp.int32, (128, 128), 0)
    col = lax.broadcasted_iota(jnp.int32, (128, 128), 1)
    causal = col <= row
    for cp in loads:
        cp.wait()

    def own_part(hp):
        for j in range(2):
            i = 2 * hp + j
            cols = pl.ds(pl.multiple_of(i * 128, 128), 128)
            scores = jnp.where(causal, dot_t(q_v[:, cols], k_v[:, cols]) * SCALE, NEG)
            top = jnp.max(scores, 1, keepdims=True)
            e = jnp.exp(scores - top)
            mix_v[i] = dot(e.astype(BF16), v_v[:, cols])
            st_v[i, 0] = top
            st_v[i, 1] = jnp.sum(e, 1, keepdims=True)

    loop(0, 2, own_part)
    has_before = ctx > 0

    def send_weights(j):
        to = lax.rem(s + j, 8)
        remote(cw_in.at[to], wt_v.at[core, s], ws.at[0], wr.at[0], (z * 8 + to, head))

    def all_weights():
        loop(1, 8, send_weights)
        pltpu.make_async_copy(cw_in.at[s], wt_v.at[core, s], wr.at[0]).start()

    def whole_part(hp):
        whole_wait(pk_v.at[hp], fr.at[2 * hp])
        whole_wait(pv_v.at[hp], fr.at[2 * hp + 1])
        pl.when(hp == 0)(all_weights)
        for j in range(2):
            i = 2 * hp + j
            cols = pl.ds(pl.multiple_of(i * 128, 128), 128)
            near = slice(j * 128, (j + 1) * 128)
            scores = jnp.where(has_before, dot_t(q_v[:, cols], pk_v[hp, :, near]) * SCALE, NEG)
            own_top, own_sum = st_v[i, 0], st_v[i, 1]
            top = jnp.maximum(own_top, jnp.max(scores, 1, keepdims=True))
            scale = jnp.exp(own_top - top)
            e = jnp.exp(scores - top)
            total = own_sum * scale + jnp.sum(e, 1, keepdims=True)
            mixed = mix_v[i] * scale + dot(e.astype(BF16), pv_v[hp, :, near])
            result = x_v[:, cols].astype(F32) + mixed / total
            mix_v[i] = result
            fo_v[:, cols] = result.astype(BF16)
            for tap in range(8):
                ts_v[hp, tap, :, near] = mix_v[i, pl.ds(tap, 16, stride=8), :].astype(BF16)

        def send(j):
            to = lax.rem(s + j, 8)
            remote(
                ts_v.at[hp, to], acts.at[0, hp, core, quarter], as_.at[hp], ar.at[hp], (z * 8 + to, 2 * yl + half)
            )

        loop(1, 8, send)

        @pl.when(core == half)
        def _():
            pltpu.make_async_copy(ts_v.at[hp, s], acts.at[0, hp, core, quarter], ar.at[hp]).start()

        @pl.when(core != half)
        def _():
            remote(ts_v.at[hp, s], acts.at[0, hp, core, quarter], as_.at[2 + hp], ar.at[hp], sibling)

        @pl.when(hp == 0)
        def _():
            loop(1, 3, lambda m: weights_step(1, m))

        pl.when(hp == 1)(lambda: weights_step(2, 0))


    weights_step(1, 0)
    loop(0, 2, whole_part)

    parts = [(hp, c) for hp in range(2) for c in range(2)]

    def place_right(k):
        return jnp.where(k == 8, 15, k)

    def place_left(k):
        return jnp.where(k == 0, 0, 7 + k)

    def pass_right(k, hp, c):
        remote(
            acts.at[place_right(k - 1), hp, c], acts.at[place_right(k), hp, c],
            zs.at[0, k - 1, hp, c], zr.at[0, k - 1, hp, c], right,
        )

    def pass_left(k, hp, c):
        remote(
            acts.at[place_left(k - 1), hp, c], acts.at[place_left(k), hp, c],
            zs.at[1, k - 1, hp, c], zr.at[1, k - 1, hp, c], left,
        )

    def got_right(k, hp, c):
        whole_wait(acts.at[place_right(k), hp, c], zr.at[0, k - 1, hp, c])

    def got_left(k, hp, c):
        whole_wait(acts.at[place_left(k), hp, c], zr.at[1, k - 1, hp, c])

    for hp in range(2):
        whole_wait(acts.at[0, hp], ar.at[hp])
        for c in range(2):
            pass_right(1, hp, c)
            pass_left(1, hp, c)

    loop(1, 3, lambda m: weights_step(2, m))
    fo_cp = pltpu.make_async_copy(fo_v, fine_out, out_sem.at[0])
    fo_cp.start()

    def turn(c):
        def part(hp):
            cols = pl.ds(pl.multiple_of(hp * 256, 256), 256)
            w2_v[c, cols, :] = wt_v[c, :, :, cols].reshape(256, 256).T

        loop(0, 2, part)

    def group_slots(g):
        return [2 * g, 2 * g + 8, 2 * g + 1, 2 * g + 9]

    def conv(g):
        total = None
        for hp, c in parts:
            rows = jnp.concatenate([acts[a, hp, c].reshape(64, 256) for a in group_slots(g)], 0)
            term = dot(rows, w2_v[c, hp * 256 : (hp + 1) * 256, :])
            total = term if total is None else total + term
        for i in range(2):
            lo = total[i * 128 : (i + 1) * 128, :128].reshape(16, 8, 128)
            hi = total[i * 128 : (i + 1) * 128, 128:].reshape(16, 8, 128)
            sb_v[g, :, i] = jnp.concatenate([lo, hi], 1).astype(BF16)

        def send(j):
            to = lax.rem(chip + j, 16)
            remote(sb_v.at[g, to], rb_v.at[g, chip], ss.at[g], sr.at[g], chip_at(to))

        loop(1, 16, send)
        pltpu.make_async_copy(sb_v.at[g, chip], rb_v.at[g, chip], sr.at[g]).start()

    def reduce(g):
        whole_wait(rb_v.at[g], sr.at[g])
        gs_v[g] = jnp.sum(rb_v[g].astype(F32), 0).astype(BF16)

        for i in range(2):
            p = 2 * g + i
            away = jnp.where(chip < 8, lax.rem(NZ + 1 - p, NZ), p + 2)

            @pl.when(away != 0)
            def _():
                remote(gs_v.at[g, i], gt_v.at[g, i], hs.at[g, i], hr.at[g, i], plane_at(away, core))

            @pl.when(away == 0)
            def _():
                pltpu.make_async_copy(gs_v.at[g, i], gt_v.at[g, i], hr.at[g, i]).start()

    def spread(g):
        for i in range(2):
            whole_wait(gt_v.at[g, i], hr.at[g, i])

        def send(j):
            remote(gt_v.at[g], gb_v.at[g, chip], gs.at[g], gr.at[g], chip_at(lax.rem(chip + j, 16)))

        loop(1, 16, send)
        pltpu.make_async_copy(gt_v.at[g], gb_v.at[g, chip], gr.at[g]).start()

    def weight_slots(g):
        return [
            jnp.where(g == 0, 1, 6 + 2 * g), jnp.where(g == 0, 0, 7 + 2 * g),
            jnp.where(g == 3, 15, 2 * g + 2), jnp.where(g == 3, 14, 2 * g + 3),
        ]

    def rows_of(g):
        slots = weight_slots(g)
        for slot in slots:
            for m in range(3):
                whole_wait(pw_v.at[slot, m, :, other_lanes], wsr.at[slot, m])
        whole_wait(gb_v.at[g], gr.at[g])
        for i in range(2):
            got = gb_v[g, :, i].astype(F32)
            rows = jnp.concatenate([got[:, :8].reshape(128, 128), got[:, 8:].reshape(128, 128)], 1).astype(BF16)
            cc_v[slots[i]] = rows[:64]
            cc_v[slots[2 + i]] = rows[64:]

    def sum_of(g, m):
        terms = acc_v[m]
        for slot in weight_slots(g):
            terms = terms + dot(cc_v[slot], pw_v[slot, m])
        return terms

    def project(g):
        rows_of(g)

        def one(m):
            acc_v[m] = sum_of(g, m)

        loop(0, 3, one)

    whole_wait(wt_v.at[core], wr.at[0])
    remote(wt_v.at[core], wt_v.at[core], ws.at[2], wr.at[3], sibling)
    pw_own.wait()
    acc_v[...] = jnp.zeros_like(acc_v)
    turn(core)

    def turn_of(i):
        more = i < GROUPS - 1

        def odd(parts):
            k = 2 * i + 1
            for hp, c in parts:
                got_right(k, hp, c)
                got_left(k, hp, c)
                if hp == 0:
                    pass_right(k + 1, hp, c)
                    pl.when(more)(lambda: pass_left(k + 1, hp, c))
                else:
                    pass_left(k + 1, hp, c)
                    pl.when(more)(lambda: pass_right(k + 1, hp, c))

        def even(parts):
            k = 2 * i + 2
            for hp, c in parts:
                if hp == 0:
                    got_right(k, hp, c)
                else:
                    got_left(k, hp, c)

                @pl.when(more)
                def _():
                    if hp == 0:
                        got_left(k, hp, c)
                    else:
                        got_right(k, hp, c)
                    pass_right(k + 1, hp, c)
                    pass_left(k + 1, hp, c)

        ringing = pl.when(i < GROUPS)
        ringing(lambda: odd(parts[:2]))

        ringing(lambda: odd(parts[2:]))

        weighing = ringing
        weighing(lambda: weights_step(i + 3, 0))
        pl.when((i >= 2) & (i < GROUPS + 2))(lambda: spread(i - 2))
        pl.when((i >= 1) & (i < GROUPS + 1))(lambda: reduce(i - 1))
        ringing(lambda: even(parts[:2]))
        weighing(lambda: weights_step(i + 3, 1))
        ringing(lambda: even(parts[2:]))
        weighing(lambda: weights_step(i + 3, 2))

        @pl.when(i == 0)
        def _():
            whole_wait(wt_v.at[1 - core], wr.at[3])
            turn(1 - core)

        ringing(lambda: conv(i))

        @pl.when(i == GROUPS)
        def _():
            loop(0, 3, lambda m: weights_step(7, m))

        pl.when(i >= 3)(lambda: project(i - 3))

    loop(0, GROUPS + 2, turn_of)
    weights_end()
    rows_of(GROUPS - 1)

    first = core == 0

    swaps = []

    def send_back(i, both):
        for c in range(2):
            xs_v[i, c] = both[:, c * 128 : (c + 1) * 128]
            swaps.append(
                remote(xs_v.at[i, c], f_v.at[i, core], xs.at[i, c], xr.at[i, core], plane_at(NZ - 1, c))
            )

    offset = lax.rem(chip - z + NZ, NZ)
    place = jnp.where(offset == 0, 0, jnp.where(offset <= 8, 7 + offset, NZ - offset))
    kv_cp = []
    for m in ORDER:
        both = sum_of(GROUPS - 1, m).astype(BF16)
        if m == 0:
            send_back(0, both)
            continue
        i = m - 1
        for c in range(2):
            ys_v[i, c] = both[:, c * 128 : (c + 1) * 128]
        kv_v[i, 1, core] = jnp.where(first, both[:, :128], both[:, 128:])
        for back, away in ((3, 2), (2, 1), (0, NZ - 1)):
            for c in range(2):
                kv_cp.append(
                    remote(
                        ys_v.at[i, c], kv_v.at[i, back, core], ks.at[i, back, c], kr.at[i, back, core], plane_at(away, c)
                    )
                )
        kv_cp.append(
            remote(ys_v.at[i, 1 - core], kv_v.at[i, 1, core], ks.at[i, 1, 0], kr.at[i, 1, core], sibling)
        )
    send_back(1, cc_v[place])

    for i in range(4):
        whole_wait(pk_v.at[0], fs.at[i])
    whole_wait(wt_v.at[0, pl.ds(0, 7)], ws.at[0])
    whole_wait(wt_v.at[0], ws.at[2])
    for hp in range(2):
        whole_wait(ts_v.at[hp, pl.ds(0, 7)], as_.at[hp])

    @pl.when(core != half)
    def _():
        for hp in range(2):
            whole_wait(ts_v.at[hp, 0], as_.at[2 + hp])

    def ring_left(k):
        for c in range(2):
            for way in range(2):
                whole_wait(acts.at[0, 0, c], zs.at[way, k, way, c])
                pl.when(k < 7)(lambda: whole_wait(acts.at[0, 0, c], zs.at[way, k, 1 - way, c]))

    loop(0, 8, ring_left)
    loop(0, GROUPS, lambda g: whole_wait(sb_v.at[g, pl.ds(0, 15)], ss.at[g]))

    loop(0, GROUPS, lambda g: whole_wait(sb_v.at[g, pl.ds(0, 15)], gs.at[g]))

    def chunks_left(g):
        for i in range(2):
            pl.when((2 * g + i != 1) | (chip >= 8))(lambda: whole_wait(gt_v.at[0, 0], hs.at[g, i]))

    loop(0, GROUPS, chunks_left)

    def weights_left(k):
        for way in range(2):
            for m in range(3):
                whole_wait(held(0, m), wzs.at[way, k, m])

    loop(0, 7, weights_left)
    for m in range(3):
        whole_wait(held(0, m), wzs.at[0 if m == 2 else 1, 7, m])
    loop(0, NZ, lambda k: [whole_wait(held(0, m), wss.at[k, m]) for m in range(3)])
    def keys_here(i):
        whole_wait(kv_v.at[i, 1, 1 - core], kr.at[i, 1, 1 - core])
        for back in (0, 2, 3):
            for c in range(2):
                whole_wait(kv_v.at[i, back, c], kr.at[i, back, c])
        for c in range(2):
            whole_wait(f_v.at[i, c], xr.at[i, c])

    keys_here(0)
    q = f_v[0].reshape(128, 128)
    keys = [kv_v[0, back].reshape(128, 128) for back in range(4)]
    scores = []
    for back in range(4):
        seen = causal if back == 0 else z >= back
        scores.append(jnp.where(seen, dot_t(q, keys[back]) * SCALE, NEG))
    top = scores[0].max(1, keepdims=True)
    for back in range(1, 4):
        top = jnp.maximum(top, scores[back].max(1, keepdims=True))
    weights = [jnp.exp(scores[back] - top) for back in range(4)]
    total = sum(jnp.sum(e, 1, keepdims=True) for e in weights)
    keys_here(1)
    mixed = sum(dot(weights[back].astype(BF16), kv_v[1, back].reshape(128, 128)) for back in range(4))
    co_v[...] = (f_v[1].reshape(128, 128).astype(F32) + mixed / total).astype(BF16)
    co_cp = pltpu.make_async_copy(co_v, coarse_out.at[0], out_sem.at[1])
    co_cp.start()

    for cp in swaps + kv_cp:
        cp.wait_send()
    fo_cp.wait()
    co_cp.wait()


def per_device(fine_q, fine_k, fine_v, fine_x, conv_weight, qkv_weight):
    cw = conv_weight.transpose(0, 2, 1)
    pw = qkv_weight[0].transpose(1, 0, 2)
    dma = pltpu.SemaphoreType.DMA
    vmem = pltpu.VMEM
    scratch = [
        vmem((128, 512), BF16), vmem((128, 512), BF16), vmem((128, 512), BF16), vmem((128, 512), BF16),
        vmem((2, 128, 256), BF16), vmem((2, 128, 256), BF16),
        vmem((4, 128, 128), F32),
        vmem((4, 2, 128, 1), F32),
        vmem((128, 512), BF16),
        vmem((2, 8, 16, 256), BF16),
        vmem((16, 2, 2, 4, 16, 256), BF16),
        vmem((2, 8, 32, 512), BF16),
        vmem((2, 512, 256), BF16),
        vmem((16, 3, 256, 256), BF16),
        vmem((4, 16, 2, 16, 128), BF16),
        vmem((4, 16, 2, 16, 128), BF16),
        vmem((4, 2, 16, 128), BF16),
        vmem((4, 2, 16, 128), BF16),
        vmem((4, 16, 2, 16, 128), BF16),
        vmem((16, 64, 256), BF16),
        vmem((3, 64, 256), F32),
        vmem((2, 2, 64, 128), BF16),
        vmem((2, 2, 64, 128), BF16),
        vmem((2, 2, 64, 128), BF16),
        vmem((2, 4, 2, 64, 128), BF16),
        vmem((128, 128), BF16),
        dma((4,)), dma((4,)), dma((4,)), dma((3,)), dma((4,)), dma((4,)), dma((2,)),
        dma((2, 8, 2, 2)), dma((2, 8, 2, 2)),
        dma((4,)), dma((4,)), dma((4,)), dma((4,)),
        dma((4, 2)), dma((4, 2)), dma((2, 8, 3)), dma((2, 8, 3)), dma((16, 3)), dma((16, 3)),
        dma((2, 2)), dma((2, 2)),
        dma((2, 4, 2)), dma((2, 4, 2)), dma((2,)),
    ]
    return pl.pallas_call(
        kernel,
        out_shape=(
            jax.ShapeDtypeStruct((128, 512), BF16),
            jax.ShapeDtypeStruct((1, 128, 128), BF16),
        ),
        in_specs=[pl.BlockSpec(memory_space=pl.ANY)] * 6,
        out_specs=[pl.BlockSpec(memory_space=pl.ANY)] * 2,
        scratch_shapes=scratch,
        compiler_params=pltpu.CompilerParams(
            collective_id=0, has_side_effects=True, vmem_limit_bytes=60 * 1024 * 1024
        ),
    )(fine_q, fine_k, fine_v, fine_x, cw, pw)


def solution(mesh):
    placed = (
        P("ctx", "head"),
        P("ctx", "head"),
        P("ctx", "head"),
        P("ctx", "head"),
        P(None, "head", "ctx"),
        P("ctx", None, None, "head"),
    )
    return jax.shard_map(
        per_device,
        mesh=mesh,
        in_specs=placed,
        out_specs=(P("ctx", "head"), P("ctx", None, "head")),
        check_vma=False,
    )
```

```python
import jax
import jax.numpy as jnp
from jax import lax
from jax.experimental import pallas as pl
from jax.experimental.pallas import tpu as pltpu
from jax.sharding import PartitionSpec as P

STRIDE = 8
HEAD_DIM = 128
NZ = 16
MESH = pl.DeviceIdType.MESH
BF16 = jnp.bfloat16
F32 = jnp.float32
SCALE = HEAD_DIM ** -0.5
NEG = -1e30
GROUPS = 4
ORDER = (1, 0, 2)


def slot_of(offset):
    if offset == -8:
        offset = 8
    return -offset if offset <= 0 else 7 + offset


def dot_t(a, b):
    return lax.dot_general(a, b, (((1,), (1,)), ((), ())), preferred_element_type=F32)


def dot(a, b):
    return jnp.dot(a, b, preferred_element_type=F32)


def whole_wait(ref, sem):
    pltpu.make_async_copy(ref, ref, sem).wait()


def kernel(
    q_in, k_in, v_in, x_in, cw_in, pw_in, fine_out, coarse_out,
    q_v, k_v, v_v, x_v, pk_v, pv_v, mix_v, st_v, fo_v, ts_v, acts, wt_v, w2_v, pw_v,
    sb_v, rb_v, gs_v, gt_v, gb_v, cc_v, acc_v, xs_v, f_v, ys_v, kv_v, co_v,
    in_sem, fs, fr, ws, wr, as_, ar, zs, zr, ss, sr, gs, gr, hs, hr, wzs, wzr, wss, wsr, xs, xr, ks, kr, out_sem,
):
    ctx = lax.axis_index("ctx")
    head = lax.axis_index("head")
    z = lax.div(ctx, 8)
    s = lax.rem(ctx, 8)
    yl = lax.div(head, 2)
    core = lax.rem(head, 2)
    chip = 2 * s + yl
    half = lax.div(s, 4)
    quarter = lax.rem(s, 4)
    sibling = (ctx, 2 * yl + 1 - core)
    after = (lax.rem(ctx + 1, 128), head)
    before = (lax.rem(ctx + 127, 128), head)
    right = (lax.rem(z + 1, NZ) * 8 + s, head)
    left = (lax.rem(z + NZ - 1, NZ) * 8 + s, head)

    def chip_at(c):
        return (z * 8 + lax.div(c, 2), lax.rem(c, 2) * 2 + core)

    def loop(low, high, body):
        def step(i, carry):
            body(i)
            return carry

        lax.fori_loop(low, high, step, 0)


    def plane_at(away, c):
        return (lax.rem(z + away, NZ) * 8 + s, 2 * yl + c)

    def remote(src, dst, send, recv, dev):
        cp = pltpu.make_async_remote_copy(
            src_ref=src, dst_ref=dst, send_sem=send, recv_sem=recv, device_id=dev, device_id_type=MESH
        )
        cp.start()
        return cp

    loads = []
    for i, (src, dst) in enumerate([(q_in, q_v), (k_in, k_v), (v_in, v_v), (x_in, x_v)]):
        cp = pltpu.make_async_copy(src, dst, in_sem.at[i])
        cp.start()
        loads.append(cp)

    barrier = pltpu.get_barrier_semaphore()

    def greet(dev):
        pl.semaphore_signal(barrier, inc=1, device_id=dev, device_id_type=MESH)

    for dev in (after, before):
        greet(dev)
    loop(1, NZ, lambda j: greet(plane_at(j, core)))
    for away in (1, 2, NZ - 2, NZ - 1):
        greet(plane_at(away, 1 - core))
    loop(1, 16, lambda j: greet(chip_at(lax.rem(chip + j, 16))))
    loop(0, 8, lambda j: greet((z * 8 + j, 2 * yl + 1 - core)))

    pl.semaphore_wait(barrier, 44)

    fine_cp = []
    for hp in range(2):
        cols = pl.ds(hp * 256, 256)
        for i, (src, dst) in enumerate([(k_in, pk_v), (v_in, pv_v)]):
            fine_cp.append(remote(src.at[:, cols], dst.at[hp], fs.at[2 * hp + i], fr.at[2 * hp + i], after))

    lanes = pl.ds(pl.multiple_of(core * 128, 128), 128)
    other_lanes = pl.ds(pl.multiple_of((1 - core) * 128, 128), 128)

    def held(slot, m):
        return pw_v.at[slot, m, :, lanes]

    pw_own = pltpu.make_async_copy(pw_in, pw_v.at[0, :, :, lanes], wr.at[2])
    pw_own.start()
    for m in range(3):
        remote(pw_in.at[m], held(1, m), wzs.at[0, 0, m], wzr.at[0, 0, m], right)
        remote(pw_in.at[m], held(8, m), wzs.at[1, 0, m], wzr.at[1, 0, m], left)
    for m in range(3):
        remote(pw_in.at[m], held(0, m), wss.at[0, m], wsr.at[0, m], sibling)

    def weights_step(k, m):
        whole_wait(held(k, m), wzr.at[0, k - 1, m])
        whole_wait(held(7 + k, m), wzr.at[1, k - 1, m])

        @pl.when((k < 7) | (m == 2))
        def _():
            remote(held(k, m), held(jnp.where(k == 7, 15, k + 1), m), wzs.at[0, k, m], wzr.at[0, k, m], right)

        @pl.when((k < 7) | (m != 2))
        def _():
            remote(held(7 + k, m), held(8 + k, m), wzs.at[1, k, m], wzr.at[1, k, m], left)

        @pl.when((k == 7) & (m == 2))
        def _():
            remote(held(7, m), held(15, m), wss.at[15, m], wsr.at[15, m], plane_at(1, 1 - core))

        @pl.when((k == 7) & (m != 2))
        def _():
            remote(held(14, m), held(15, m), wss.at[15, m], wsr.at[15, m], plane_at(NZ - 1, 1 - core))

        remote(held(k, m), held(k, m), wss.at[k, m], wsr.at[k, m], sibling)
        remote(held(7 + k, m), held(7 + k, m), wss.at[7 + k, m], wsr.at[7 + k, m], sibling)

    def weights_end():
        for m in range(3):
            way = 0 if m == 2 else 1
            whole_wait(held(15, m), wzr.at[way, 7, m])

    row = lax.broadcasted_iota(jnp.int32, (128, 128), 0)
    col = lax.broadcasted_iota(jnp.int32, (128, 128), 1)
    causal = col <= row
    for cp in loads:
        cp.wait()

    def own_part(hp):
        for j in range(2):
            i = 2 * hp + j
            cols = pl.ds(pl.multiple_of(i * 128, 128), 128)
            scores = jnp.where(causal, dot_t(q_v[:, cols], k_v[:, cols]) * SCALE, NEG)
            top = jnp.max(scores, 1, keepdims=True)
            e = jnp.exp(scores - top)
            mix_v[i] = dot(e.astype(BF16), v_v[:, cols])
            st_v[i, 0] = top
            st_v[i, 1] = jnp.sum(e, 1, keepdims=True)

    loop(0, 2, own_part)
    has_before = ctx > 0

    def send_weights(j):
        to = lax.rem(s + j, 8)
        remote(cw_in.at[to], wt_v.at[core, s], ws.at[0], wr.at[0], (z * 8 + to, head))

    def all_weights():
        loop(1, 8, send_weights)
        pltpu.make_async_copy(cw_in.at[s], wt_v.at[core, s], wr.at[0]).start()

    def whole_part(hp):
        whole_wait(pk_v.at[hp], fr.at[2 * hp])
        whole_wait(pv_v.at[hp], fr.at[2 * hp + 1])
        pl.when(hp == 0)(all_weights)
        for j in range(2):
            i = 2 * hp + j
            cols = pl.ds(pl.multiple_of(i * 128, 128), 128)
            near = slice(j * 128, (j + 1) * 128)
            scores = jnp.where(has_before, dot_t(q_v[:, cols], pk_v[hp, :, near]) * SCALE, NEG)
            own_top, own_sum = st_v[i, 0], st_v[i, 1]
            top = jnp.maximum(own_top, jnp.max(scores, 1, keepdims=True))
            scale = jnp.exp(own_top - top)
            e = jnp.exp(scores - top)
            total = own_sum * scale + jnp.sum(e, 1, keepdims=True)
            mixed = mix_v[i] * scale + dot(e.astype(BF16), pv_v[hp, :, near])
            result = x_v[:, cols].astype(F32) + mixed / total
            mix_v[i] = result
            fo_v[:, cols] = result.astype(BF16)
            for tap in range(8):
                ts_v[hp, tap, :, near] = mix_v[i, pl.ds(tap, 16, stride=8), :].astype(BF16)

        def send(j):
            to = lax.rem(s + j, 8)
            remote(
                ts_v.at[hp, to], acts.at[0, hp, core, quarter], as_.at[hp], ar.at[hp], (z * 8 + to, 2 * yl + half)
            )

        loop(1, 8, send)

        @pl.when(core == half)
        def _():
            pltpu.make_async_copy(ts_v.at[hp, s], acts.at[0, hp, core, quarter], ar.at[hp]).start()

        @pl.when(core != half)
        def _():
            remote(ts_v.at[hp, s], acts.at[0, hp, core, quarter], as_.at[2 + hp], ar.at[hp], sibling)

        @pl.when(hp == 0)
        def _():
            loop(1, 3, lambda m: weights_step(1, m))

        pl.when(hp == 1)(lambda: weights_step(2, 0))


    weights_step(1, 0)
    loop(0, 2, whole_part)

    parts = [(hp, c) for hp in range(2) for c in range(2)]
    ring_parts = [(0, 0), (1, 0)]

    def place_right(k):
        return jnp.where(k == 8, 15, k)

    def place_left(k):
        return jnp.where(k == 0, 0, 7 + k)

    def pass_right(k, hp, c):
        remote(
            acts.at[place_right(k - 1), hp], acts.at[place_right(k), hp],
            zs.at[0, k - 1, hp, c], zr.at[0, k - 1, hp, c], right,
        )

    def pass_left(k, hp, c):
        remote(
            acts.at[place_left(k - 1), hp], acts.at[place_left(k), hp],
            zs.at[1, k - 1, hp, c], zr.at[1, k - 1, hp, c], left,
        )

    def got_right(k, hp, c):
        whole_wait(acts.at[place_right(k), hp], zr.at[0, k - 1, hp, c])

    def got_left(k, hp, c):
        whole_wait(acts.at[place_left(k), hp], zr.at[1, k - 1, hp, c])

    for hp in range(2):
        whole_wait(acts.at[0, hp], ar.at[hp])
        pass_right(1, hp, 0)
        pass_left(1, hp, 0)

    loop(1, 3, lambda m: weights_step(2, m))
    fo_cp = pltpu.make_async_copy(fo_v, fine_out, out_sem.at[0])
    fo_cp.start()

    def turn(c):
        def part(hp):
            cols = pl.ds(pl.multiple_of(hp * 256, 256), 256)
            w2_v[c, cols, :] = wt_v[c, :, :, cols].reshape(256, 256).T

        loop(0, 2, part)

    def group_slots(g):
        return [2 * g, 2 * g + 8, 2 * g + 1, 2 * g + 9]

    def conv(g):
        total = None
        for hp, c in parts:
            rows = jnp.concatenate([acts[a, hp, c].reshape(64, 256) for a in group_slots(g)], 0)
            term = dot(rows, w2_v[c, hp * 256 : (hp + 1) * 256, :])
            total = term if total is None else total + term
        for i in range(2):
            lo = total[i * 128 : (i + 1) * 128, :128].reshape(16, 8, 128)
            hi = total[i * 128 : (i + 1) * 128, 128:].reshape(16, 8, 128)
            sb_v[g, :, i] = jnp.concatenate([lo, hi], 1).astype(BF16)

        def send(j):
            to = lax.rem(chip + j, 16)
            remote(sb_v.at[g, to], rb_v.at[g, chip], ss.at[g], sr.at[g], chip_at(to))

        loop(1, 16, send)
        pltpu.make_async_copy(sb_v.at[g, chip], rb_v.at[g, chip], sr.at[g]).start()

    def reduce(g):
        whole_wait(rb_v.at[g], sr.at[g])
        gs_v[g] = jnp.sum(rb_v[g].astype(F32), 0).astype(BF16)

        for i in range(2):
            p = 2 * g + i
            away = jnp.where(chip < 8, lax.rem(NZ + 1 - p, NZ), p + 2)

            @pl.when(away != 0)
            def _():
                remote(gs_v.at[g, i], gt_v.at[g, i], hs.at[g, i], hr.at[g, i], plane_at(away, core))

            @pl.when(away == 0)
            def _():
                pltpu.make_async_copy(gs_v.at[g, i], gt_v.at[g, i], hr.at[g, i]).start()

    def spread(g):
        for i in range(2):
            whole_wait(gt_v.at[g, i], hr.at[g, i])

        def send(j):
            remote(gt_v.at[g], gb_v.at[g, chip], gs.at[g], gr.at[g], chip_at(lax.rem(chip + j, 16)))

        loop(1, 16, send)
        pltpu.make_async_copy(gt_v.at[g], gb_v.at[g, chip], gr.at[g]).start()

    def weight_slots(g):
        return [
            jnp.where(g == 0, 1, 6 + 2 * g), jnp.where(g == 0, 0, 7 + 2 * g),
            jnp.where(g == 3, 15, 2 * g + 2), jnp.where(g == 3, 14, 2 * g + 3),
        ]

    def rows_of(g):
        slots = weight_slots(g)
        for slot in slots:
            for m in range(3):
                whole_wait(pw_v.at[slot, m, :, other_lanes], wsr.at[slot, m])
        whole_wait(gb_v.at[g], gr.at[g])
        for i in range(2):
            got = gb_v[g, :, i].astype(F32)
            rows = jnp.concatenate([got[:, :8].reshape(128, 128), got[:, 8:].reshape(128, 128)], 1).astype(BF16)
            cc_v[slots[i]] = rows[:64]
            cc_v[slots[2 + i]] = rows[64:]

    def sum_of(g, m):
        terms = acc_v[m]
        for slot in weight_slots(g):
            terms = terms + dot(cc_v[slot], pw_v[slot, m])
        return terms

    def project(g):
        rows_of(g)

        def one(m):
            acc_v[m] = sum_of(g, m)

        loop(0, 3, one)

    whole_wait(wt_v.at[core], wr.at[0])
    remote(wt_v.at[core], wt_v.at[core], ws.at[2], wr.at[3], sibling)
    pw_own.wait()
    acc_v[...] = jnp.zeros_like(acc_v)
    turn(core)

    def turn_of(i):
        more = i < GROUPS - 1

        def odd(parts):
            k = 2 * i + 1
            for hp, c in parts:
                got_right(k, hp, c)
                got_left(k, hp, c)
                if hp == 0:
                    pass_right(k + 1, hp, c)
                    pl.when(more)(lambda: pass_left(k + 1, hp, c))
                else:
                    pass_left(k + 1, hp, c)
                    pl.when(more)(lambda: pass_right(k + 1, hp, c))

        def even(parts):
            k = 2 * i + 2
            for hp, c in parts:
                if hp == 0:
                    got_right(k, hp, c)
                else:
                    got_left(k, hp, c)

                @pl.when(more)
                def _():
                    if hp == 0:
                        got_left(k, hp, c)
                    else:
                        got_right(k, hp, c)
                    pass_right(k + 1, hp, c)
                    pass_left(k + 1, hp, c)

        ringing = pl.when(i < GROUPS)
        ringing(lambda: odd(ring_parts[:1]))

        ringing(lambda: odd(ring_parts[1:]))

        weighing = ringing
        weighing(lambda: weights_step(i + 3, 0))
        pl.when((i >= 2) & (i < GROUPS + 2))(lambda: spread(i - 2))
        pl.when((i >= 1) & (i < GROUPS + 1))(lambda: reduce(i - 1))
        ringing(lambda: even(ring_parts[:1]))
        weighing(lambda: weights_step(i + 3, 1))
        ringing(lambda: even(ring_parts[1:]))
        weighing(lambda: weights_step(i + 3, 2))

        @pl.when(i == 0)
        def _():
            whole_wait(wt_v.at[1 - core], wr.at[3])
            turn(1 - core)

        ringing(lambda: conv(i))

        @pl.when(i == GROUPS)
        def _():
            loop(0, 3, lambda m: weights_step(7, m))

        pl.when(i >= 3)(lambda: project(i - 3))

    loop(0, GROUPS + 2, turn_of)
    weights_end()
    rows_of(GROUPS - 1)

    first = core == 0

    swaps = []

    def send_back(i, both):
        for c in range(2):
            xs_v[i, c] = both[:, c * 128 : (c + 1) * 128]
            swaps.append(
                remote(xs_v.at[i, c], f_v.at[i, core], xs.at[i, c], xr.at[i, core], plane_at(NZ - 1, c))
            )

    offset = lax.rem(chip - z + NZ, NZ)
    place = jnp.where(offset == 0, 0, jnp.where(offset <= 8, 7 + offset, NZ - offset))
    kv_cp = []
    for m in ORDER:
        both = sum_of(GROUPS - 1, m).astype(BF16)
        if m == 0:
            send_back(0, both)
            continue
        i = m - 1
        for c in range(2):
            ys_v[i, c] = both[:, c * 128 : (c + 1) * 128]
        kv_v[i, 1, core] = jnp.where(first, both[:, :128], both[:, 128:])
        for back, away in ((3, 2), (2, 1), (0, NZ - 1)):
            for c in range(2):
                kv_cp.append(
                    remote(
                        ys_v.at[i, c], kv_v.at[i, back, core], ks.at[i, back, c], kr.at[i, back, core], plane_at(away, c)
                    )
                )
        kv_cp.append(
            remote(ys_v.at[i, 1 - core], kv_v.at[i, 1, core], ks.at[i, 1, 0], kr.at[i, 1, core], sibling)
        )
    send_back(1, cc_v[place])

    for i in range(4):
        whole_wait(pk_v.at[0], fs.at[i])
    whole_wait(wt_v.at[0, pl.ds(0, 7)], ws.at[0])
    whole_wait(wt_v.at[0], ws.at[2])
    for hp in range(2):
        whole_wait(ts_v.at[hp, pl.ds(0, 7)], as_.at[hp])

    @pl.when(core != half)
    def _():
        for hp in range(2):
            whole_wait(ts_v.at[hp, 0], as_.at[2 + hp])

    def ring_left(k):
        for way in range(2):
            whole_wait(acts.at[0, 0], zs.at[way, k, way, 0])
            pl.when(k < 7)(lambda: whole_wait(acts.at[0, 0], zs.at[way, k, 1 - way, 0]))

    loop(0, 8, ring_left)
    loop(0, GROUPS, lambda g: whole_wait(sb_v.at[g, pl.ds(0, 15)], ss.at[g]))

    loop(0, GROUPS, lambda g: whole_wait(sb_v.at[g, pl.ds(0, 15)], gs.at[g]))

    def chunks_left(g):
        for i in range(2):
            pl.when((2 * g + i != 1) | (chip >= 8))(lambda: whole_wait(gt_v.at[0, 0], hs.at[g, i]))

    loop(0, GROUPS, chunks_left)

    def weights_left(k):
        for way in range(2):
            for m in range(3):
                whole_wait(held(0, m), wzs.at[way, k, m])

    loop(0, 7, weights_left)
    for m in range(3):
        whole_wait(held(0, m), wzs.at[0 if m == 2 else 1, 7, m])
    loop(0, NZ, lambda k: [whole_wait(held(0, m), wss.at[k, m]) for m in range(3)])
    def keys_here(i):
        whole_wait(kv_v.at[i, 1, 1 - core], kr.at[i, 1, 1 - core])
        for back in (0, 2, 3):
            for c in range(2):
                whole_wait(kv_v.at[i, back, c], kr.at[i, back, c])
        for c in range(2):
            whole_wait(f_v.at[i, c], xr.at[i, c])

    keys_here(0)
    q = f_v[0].reshape(128, 128)
    keys = [kv_v[0, back].reshape(128, 128) for back in range(4)]
    scores = []
    for back in range(4):
        seen = causal if back == 0 else z >= back
        scores.append(jnp.where(seen, dot_t(q, keys[back]) * SCALE, NEG))
    top = scores[0].max(1, keepdims=True)
    for back in range(1, 4):
        top = jnp.maximum(top, scores[back].max(1, keepdims=True))
    weights = [jnp.exp(scores[back] - top) for back in range(4)]
    total = sum(jnp.sum(e, 1, keepdims=True) for e in weights)
    keys_here(1)
    mixed = sum(dot(weights[back].astype(BF16), kv_v[1, back].reshape(128, 128)) for back in range(4))
    co_v[...] = (f_v[1].reshape(128, 128).astype(F32) + mixed / total).astype(BF16)
    co_cp = pltpu.make_async_copy(co_v, coarse_out.at[0], out_sem.at[1])
    co_cp.start()

    for cp in swaps + kv_cp:
        cp.wait_send()
    fo_cp.wait()
    co_cp.wait()


def per_device(fine_q, fine_k, fine_v, fine_x, conv_weight, qkv_weight):
    cw = conv_weight.transpose(0, 2, 1)
    pw = qkv_weight[0].transpose(1, 0, 2)
    dma = pltpu.SemaphoreType.DMA
    vmem = pltpu.VMEM
    scratch = [
        vmem((128, 512), BF16), vmem((128, 512), BF16), vmem((128, 512), BF16), vmem((128, 512), BF16),
        vmem((2, 128, 256), BF16), vmem((2, 128, 256), BF16),
        vmem((4, 128, 128), F32),
        vmem((4, 2, 128, 1), F32),
        vmem((128, 512), BF16),
        vmem((2, 8, 16, 256), BF16),
        vmem((16, 2, 2, 4, 16, 256), BF16),
        vmem((2, 8, 32, 512), BF16),
        vmem((2, 512, 256), BF16),
        vmem((16, 3, 256, 256), BF16),
        vmem((4, 16, 2, 16, 128), BF16),
        vmem((4, 16, 2, 16, 128), BF16),
        vmem((4, 2, 16, 128), BF16),
        vmem((4, 2, 16, 128), BF16),
        vmem((4, 16, 2, 16, 128), BF16),
        vmem((16, 64, 256), BF16),
        vmem((3, 64, 256), F32),
        vmem((2, 2, 64, 128), BF16),
        vmem((2, 2, 64, 128), BF16),
        vmem((2, 2, 64, 128), BF16),
        vmem((2, 4, 2, 64, 128), BF16),
        vmem((128, 128), BF16),
        dma((4,)), dma((4,)), dma((4,)), dma((3,)), dma((4,)), dma((4,)), dma((2,)),
        dma((2, 8, 2, 2)), dma((2, 8, 2, 2)),
        dma((4,)), dma((4,)), dma((4,)), dma((4,)),
        dma((4, 2)), dma((4, 2)), dma((2, 8, 3)), dma((2, 8, 3)), dma((16, 3)), dma((16, 3)),
        dma((2, 2)), dma((2, 2)),
        dma((2, 4, 2)), dma((2, 4, 2)), dma((2,)),
    ]
    return pl.pallas_call(
        kernel,
        out_shape=(
            jax.ShapeDtypeStruct((128, 512), BF16),
            jax.ShapeDtypeStruct((1, 128, 128), BF16),
        ),
        in_specs=[pl.BlockSpec(memory_space=pl.ANY)] * 6,
        out_specs=[pl.BlockSpec(memory_space=pl.ANY)] * 2,
        scratch_shapes=scratch,
        compiler_params=pltpu.CompilerParams(
            collective_id=0, has_side_effects=True, vmem_limit_bytes=60 * 1024 * 1024
        ),
    )(fine_q, fine_k, fine_v, fine_x, cw, pw)


def solution(mesh):
    placed = (
        P("ctx", "head"),
        P("ctx", "head"),
        P("ctx", "head"),
        P("ctx", "head"),
        P(None, "head", "ctx"),
        P("ctx", None, None, "head"),
    )
    return jax.shard_map(
        per_device,
        mesh=mesh,
        in_specs=placed,
        out_specs=(P("ctx", "head"), P("ctx", None, "head")),
        check_vma=False,
    )
```

```python
import jax
import jax.numpy as jnp
from jax import lax
from jax.experimental import pallas as pl
from jax.experimental.pallas import tpu as pltpu
from jax.sharding import PartitionSpec as P

STRIDE = 8
HEAD_DIM = 128
NZ = 16
MESH = pl.DeviceIdType.MESH
BF16 = jnp.bfloat16
F32 = jnp.float32
SCALE = HEAD_DIM ** -0.5
NEG = -1e30
GROUPS = 4
ORDER = (1, 0, 2)


def slot_of(offset):
    if offset == -8:
        offset = 8
    return -offset if offset <= 0 else 7 + offset


def dot_t(a, b):
    return lax.dot_general(a, b, (((1,), (1,)), ((), ())), preferred_element_type=F32)


def dot(a, b):
    return jnp.dot(a, b, preferred_element_type=F32)


def whole_wait(ref, sem):
    pltpu.make_async_copy(ref, ref, sem).wait()


def kernel(
    q_in, k_in, v_in, x_in, cw_in, pw_in, fine_out, coarse_out,
    q_v, k_v, v_v, x_v, pk_v, pv_v, mix_v, st_v, fo_v, ts_v, acts, wt_v, w2_v, pw_v,
    sb_v, rb_v, gs_v, gt_v, gb_v, cc_v, acc_v, xs_v, f_v, ys_v, kv_v, co_v,
    in_sem, fs, fr, ws, wr, as_, ar, zs, zr, ss, sr, gs, gr, hs, hr, wzs, wzr, wss, wsr, xs, xr, ks, kr, out_sem,
):
    ctx = lax.axis_index("ctx")
    head = lax.axis_index("head")
    z = lax.div(ctx, 8)
    s = lax.rem(ctx, 8)
    yl = lax.div(head, 2)
    core = lax.rem(head, 2)
    chip = 2 * s + yl
    half = lax.div(s, 4)
    quarter = lax.rem(s, 4)
    sibling = (ctx, 2 * yl + 1 - core)
    after = (lax.rem(ctx + 1, 128), head)
    before = (lax.rem(ctx + 127, 128), head)
    right = (lax.rem(z + 1, NZ) * 8 + s, head)
    left = (lax.rem(z + NZ - 1, NZ) * 8 + s, head)

    def chip_at(c):
        return (z * 8 + lax.div(c, 2), lax.rem(c, 2) * 2 + core)

    def loop(low, high, body):
        def step(i, carry):
            body(i)
            return carry

        lax.fori_loop(low, high, step, 0)


    def plane_at(away, c):
        return (lax.rem(z + away, NZ) * 8 + s, 2 * yl + c)

    def remote(src, dst, send, recv, dev):
        cp = pltpu.make_async_remote_copy(
            src_ref=src, dst_ref=dst, send_sem=send, recv_sem=recv, device_id=dev, device_id_type=MESH
        )
        cp.start()
        return cp

    loads = []
    for i, (src, dst) in enumerate([(q_in, q_v), (k_in, k_v), (v_in, v_v), (x_in, x_v)]):
        cp = pltpu.make_async_copy(src, dst, in_sem.at[i])
        cp.start()
        loads.append(cp)

    barrier = pltpu.get_barrier_semaphore()

    def greet(dev):
        pl.semaphore_signal(barrier, inc=1, device_id=dev, device_id_type=MESH)

    for dev in (after, before):
        greet(dev)
    loop(1, NZ, lambda j: greet(plane_at(j, core)))
    for away in (1, 2, NZ - 2, NZ - 1):
        greet(plane_at(away, 1 - core))
    loop(1, 16, lambda j: greet(chip_at(lax.rem(chip + j, 16))))
    loop(0, 8, lambda j: greet((z * 8 + j, 2 * yl + 1 - core)))

    pl.semaphore_wait(barrier, 44)

    fine_cp = []
    for hp in range(2):
        cols = pl.ds(hp * 256, 256)
        for i, (src, dst) in enumerate([(k_in, pk_v), (v_in, pv_v)]):
            fine_cp.append(remote(src.at[:, cols], dst.at[hp], fs.at[2 * hp + i], fr.at[2 * hp + i], after))

    lanes = pl.ds(pl.multiple_of(core * 128, 128), 128)
    other_lanes = pl.ds(pl.multiple_of((1 - core) * 128, 128), 128)

    def held(slot, m):
        return pw_v.at[slot, m, :, lanes]

    def whole(slot):
        return pw_v.at[slot, :, :, lanes]

    pw_own = pltpu.make_async_copy(pw_in, pw_v.at[0, :, :, lanes], wr.at[2])
    pw_own.start()
    for m in range(3):
        remote(pw_in.at[m], held(1, m), wzs.at[0, 0, m], wzr.at[0, 0, m], right)
        remote(pw_in.at[m], held(8, m), wzs.at[1, 0, m], wzr.at[1, 0, m], left)
    remote(pw_in, whole(0), wss.at[0, 0], wsr.at[0, 0], sibling)

    def weights_step(k, m):
        whole_wait(held(k, m), wzr.at[0, k - 1, m])
        whole_wait(held(7 + k, m), wzr.at[1, k - 1, m])

        @pl.when((k < 7) | (m == 2))
        def _():
            remote(held(k, m), held(jnp.where(k == 7, 15, k + 1), m), wzs.at[0, k, m], wzr.at[0, k, m], right)

        @pl.when((k < 7) | (m != 2))
        def _():
            remote(held(7 + k, m), held(8 + k, m), wzs.at[1, k, m], wzr.at[1, k, m], left)

        @pl.when((k == 7) & (m == 2))
        def _():
            remote(held(7, m), held(15, m), wss.at[15, m], wsr.at[15, m], plane_at(1, 1 - core))

        @pl.when((k == 7) & (m != 2))
        def _():
            remote(held(14, m), held(15, m), wss.at[15, m], wsr.at[15, m], plane_at(NZ - 1, 1 - core))

        @pl.when(m == 2)
        def _():
            for slot in (k, 7 + k):
                remote(whole(slot), whole(slot), wss.at[slot, 0], wsr.at[slot, 0], sibling)

    def weights_end():
        for m in range(3):
            way = 0 if m == 2 else 1
            whole_wait(held(15, m), wzr.at[way, 7, m])
            whole_wait(pw_v.at[15, m, :, other_lanes], wsr.at[15, m])

    row = lax.broadcasted_iota(jnp.int32, (128, 128), 0)
    col = lax.broadcasted_iota(jnp.int32, (128, 128), 1)
    causal = col <= row
    for cp in loads:
        cp.wait()

    def own_part(hp):
        for j in range(2):
            i = 2 * hp + j
            cols = pl.ds(pl.multiple_of(i * 128, 128), 128)
            scores = jnp.where(causal, dot_t(q_v[:, cols], k_v[:, cols]) * SCALE, NEG)
            top = jnp.max(scores, 1, keepdims=True)
            e = jnp.exp(scores - top)
            mix_v[i] = dot(e.astype(BF16), v_v[:, cols])
            st_v[i, 0] = top
            st_v[i, 1] = jnp.sum(e, 1, keepdims=True)

    loop(0, 2, own_part)
    has_before = ctx > 0

    def send_weights(j):
        to = lax.rem(s + j, 8)
        remote(cw_in.at[to], wt_v.at[core, s], ws.at[0], wr.at[0], (z * 8 + to, head))

    def all_weights():
        loop(1, 8, send_weights)
        pltpu.make_async_copy(cw_in.at[s], wt_v.at[core, s], wr.at[0]).start()

    def whole_part(hp):
        whole_wait(pk_v.at[hp], fr.at[2 * hp])
        whole_wait(pv_v.at[hp], fr.at[2 * hp + 1])
        pl.when(hp == 0)(all_weights)
        for j in range(2):
            i = 2 * hp + j
            cols = pl.ds(pl.multiple_of(i * 128, 128), 128)
            near = slice(j * 128, (j + 1) * 128)
            scores = jnp.where(has_before, dot_t(q_v[:, cols], pk_v[hp, :, near]) * SCALE, NEG)
            own_top, own_sum = st_v[i, 0], st_v[i, 1]
            top = jnp.maximum(own_top, jnp.max(scores, 1, keepdims=True))
            scale = jnp.exp(own_top - top)
            e = jnp.exp(scores - top)
            total = own_sum * scale + jnp.sum(e, 1, keepdims=True)
            mixed = mix_v[i] * scale + dot(e.astype(BF16), pv_v[hp, :, near])
            result = x_v[:, cols].astype(F32) + mixed / total
            mix_v[i] = result
            fo_v[:, cols] = result.astype(BF16)
            for tap in range(8):
                ts_v[hp, tap, :, near] = mix_v[i, pl.ds(tap, 16, stride=8), :].astype(BF16)

        def send(j):
            to = lax.rem(s + j, 8)
            remote(
                ts_v.at[hp, to], acts.at[0, hp, core, quarter], as_.at[hp], ar.at[hp], (z * 8 + to, 2 * yl + half)
            )

        loop(1, 8, send)

        @pl.when(core == half)
        def _():
            pltpu.make_async_copy(ts_v.at[hp, s], acts.at[0, hp, core, quarter], ar.at[hp]).start()

        @pl.when(core != half)
        def _():
            remote(ts_v.at[hp, s], acts.at[0, hp, core, quarter], as_.at[2 + hp], ar.at[hp], sibling)

        @pl.when(hp == 0)
        def _():
            loop(1, 3, lambda m: weights_step(1, m))

        pl.when(hp == 1)(lambda: weights_step(2, 0))


    weights_step(1, 0)
    loop(0, 2, whole_part)

    parts = [(hp, c) for hp in range(2) for c in range(2)]

    def place_right(k):
        return jnp.where(k == 8, 15, k)

    def place_left(k):
        return jnp.where(k == 0, 0, 7 + k)

    def pass_right(k, hp, c):
        remote(
            acts.at[place_right(k - 1), hp, c], acts.at[place_right(k), hp, c],
            zs.at[0, k - 1, hp, c], zr.at[0, k - 1, hp, c], right,
        )

    def pass_left(k, hp, c):
        remote(
            acts.at[place_left(k - 1), hp, c], acts.at[place_left(k), hp, c],
            zs.at[1, k - 1, hp, c], zr.at[1, k - 1, hp, c], left,
        )

    def got_right(k, hp, c):
        whole_wait(acts.at[place_right(k), hp, c], zr.at[0, k - 1, hp, c])

    def got_left(k, hp, c):
        whole_wait(acts.at[place_left(k), hp, c], zr.at[1, k - 1, hp, c])

    for hp in range(2):
        whole_wait(acts.at[0, hp], ar.at[hp])
        for c in range(2):
            pass_right(1, hp, c)
            pass_left(1, hp, c)

    loop(1, 3, lambda m: weights_step(2, m))
    fo_cp = pltpu.make_async_copy(fo_v, fine_out, out_sem.at[0])
    fo_cp.start()

    def turn(c):
        def part(hp):
            cols = pl.ds(pl.multiple_of(hp * 256, 256), 256)
            w2_v[c, cols, :] = wt_v[c, :, :, cols].reshape(256, 256).T

        loop(0, 2, part)

    def group_slots(g):
        return [2 * g, 2 * g + 8, 2 * g + 1, 2 * g + 9]

    def conv(g):
        total = None
        for hp, c in parts:
            rows = jnp.concatenate([acts[a, hp, c].reshape(64, 256) for a in group_slots(g)], 0)
            term = dot(rows, w2_v[c, hp * 256 : (hp + 1) * 256, :])
            total = term if total is None else total + term
        for i in range(2):
            lo = total[i * 128 : (i + 1) * 128, :128].reshape(16, 8, 128)
            hi = total[i * 128 : (i + 1) * 128, 128:].reshape(16, 8, 128)
            sb_v[g, :, i] = jnp.concatenate([lo, hi], 1).astype(BF16)

        def send(j):
            to = lax.rem(chip + j, 16)
            remote(sb_v.at[g, to], rb_v.at[g, chip], ss.at[g], sr.at[g], chip_at(to))

        loop(1, 16, send)
        pltpu.make_async_copy(sb_v.at[g, chip], rb_v.at[g, chip], sr.at[g]).start()

    def reduce(g):
        whole_wait(rb_v.at[g], sr.at[g])
        gs_v[g] = jnp.sum(rb_v[g].astype(F32), 0).astype(BF16)

        for i in range(2):
            p = 2 * g + i
            away = jnp.where(chip < 8, lax.rem(NZ + 1 - p, NZ), p + 2)

            @pl.when(away != 0)
            def _():
                remote(gs_v.at[g, i], gt_v.at[g, i], hs.at[g, i], hr.at[g, i], plane_at(away, core))

            @pl.when(away == 0)
            def _():
                pltpu.make_async_copy(gs_v.at[g, i], gt_v.at[g, i], hr.at[g, i]).start()

    def spread(g):
        for i in range(2):
            whole_wait(gt_v.at[g, i], hr.at[g, i])

        def send(j):
            remote(gt_v.at[g], gb_v.at[g, chip], gs.at[g], gr.at[g], chip_at(lax.rem(chip + j, 16)))

        loop(1, 16, send)
        pltpu.make_async_copy(gt_v.at[g], gb_v.at[g, chip], gr.at[g]).start()

    def weight_slots(g):
        return [
            jnp.where(g == 0, 1, 6 + 2 * g), jnp.where(g == 0, 0, 7 + 2 * g),
            jnp.where(g == 3, 15, 2 * g + 2), jnp.where(g == 3, 14, 2 * g + 3),
        ]

    def rows_of(g):
        slots = weight_slots(g)
        for slot in slots:
            pl.when(slot != 15)(lambda: whole_wait(pw_v.at[slot, :, :, other_lanes], wsr.at[slot, 0]))
        whole_wait(gb_v.at[g], gr.at[g])
        for i in range(2):
            got = gb_v[g, :, i].astype(F32)
            rows = jnp.concatenate([got[:, :8].reshape(128, 128), got[:, 8:].reshape(128, 128)], 1).astype(BF16)
            cc_v[slots[i]] = rows[:64]
            cc_v[slots[2 + i]] = rows[64:]

    def sum_of(g, m):
        terms = acc_v[m]
        for slot in weight_slots(g):
            terms = terms + dot(cc_v[slot], pw_v[slot, m])
        return terms

    def project(g):
        rows_of(g)

        def one(m):
            acc_v[m] = sum_of(g, m)

        loop(0, 3, one)

    whole_wait(wt_v.at[core], wr.at[0])
    remote(wt_v.at[core], wt_v.at[core], ws.at[2], wr.at[3], sibling)
    pw_own.wait()
    acc_v[...] = jnp.zeros_like(acc_v)
    turn(core)

    def turn_of(i):
        more = i < GROUPS - 1

        def odd(parts):
            k = 2 * i + 1
            for hp, c in parts:
                got_right(k, hp, c)
                got_left(k, hp, c)
                if hp == 0:
                    pass_right(k + 1, hp, c)
                    pl.when(more)(lambda: pass_left(k + 1, hp, c))
                else:
                    pass_left(k + 1, hp, c)
                    pl.when(more)(lambda: pass_right(k + 1, hp, c))

        def even(parts):
            k = 2 * i + 2
            for hp, c in parts:
                if hp == 0:
                    got_right(k, hp, c)
                else:
                    got_left(k, hp, c)

                @pl.when(more)
                def _():
                    if hp == 0:
                        got_left(k, hp, c)
                    else:
                        got_right(k, hp, c)
                    pass_right(k + 1, hp, c)
                    pass_left(k + 1, hp, c)

        ringing = pl.when(i < GROUPS)
        ringing(lambda: odd(parts[:2]))

        ringing(lambda: odd(parts[2:]))

        weighing = ringing
        weighing(lambda: weights_step(i + 3, 0))
        pl.when((i >= 2) & (i < GROUPS + 2))(lambda: spread(i - 2))
        pl.when((i >= 1) & (i < GROUPS + 1))(lambda: reduce(i - 1))
        ringing(lambda: even(parts[:2]))
        weighing(lambda: weights_step(i + 3, 1))
        ringing(lambda: even(parts[2:]))
        weighing(lambda: weights_step(i + 3, 2))

        @pl.when(i == 0)
        def _():
            whole_wait(wt_v.at[1 - core], wr.at[3])
            turn(1 - core)

        ringing(lambda: conv(i))

        @pl.when(i == GROUPS)
        def _():
            loop(0, 3, lambda m: weights_step(7, m))

        pl.when(i >= 3)(lambda: project(i - 3))

    loop(0, GROUPS + 2, turn_of)
    weights_end()
    rows_of(GROUPS - 1)

    first = core == 0

    swaps = []

    def send_back(i, both):
        for c in range(2):
            xs_v[i, c] = both[:, c * 128 : (c + 1) * 128]
            swaps.append(
                remote(xs_v.at[i, c], f_v.at[i, core], xs.at[i, c], xr.at[i, core], plane_at(NZ - 1, c))
            )

    offset = lax.rem(chip - z + NZ, NZ)
    place = jnp.where(offset == 0, 0, jnp.where(offset <= 8, 7 + offset, NZ - offset))
    kv_cp = []
    for m in ORDER:
        both = sum_of(GROUPS - 1, m).astype(BF16)
        if m == 0:
            send_back(0, both)
            continue
        i = m - 1
        for c in range(2):
            ys_v[i, c] = both[:, c * 128 : (c + 1) * 128]
        kv_v[i, 1, core] = jnp.where(first, both[:, :128], both[:, 128:])
        for back, away in ((3, 2), (2, 1), (0, NZ - 1)):
            for c in range(2):
                kv_cp.append(
                    remote(
                        ys_v.at[i, c], kv_v.at[i, back, core], ks.at[i, back, c], kr.at[i, back, core], plane_at(away, c)
                    )
                )
        kv_cp.append(
            remote(ys_v.at[i, 1 - core], kv_v.at[i, 1, core], ks.at[i, 1, 0], kr.at[i, 1, core], sibling)
        )
    send_back(1, cc_v[place])

    for i in range(4):
        whole_wait(pk_v.at[0], fs.at[i])
    whole_wait(wt_v.at[0, pl.ds(0, 7)], ws.at[0])
    whole_wait(wt_v.at[0], ws.at[2])
    for hp in range(2):
        whole_wait(ts_v.at[hp, pl.ds(0, 7)], as_.at[hp])

    @pl.when(core != half)
    def _():
        for hp in range(2):
            whole_wait(ts_v.at[hp, 0], as_.at[2 + hp])

    def ring_left(k):
        for c in range(2):
            for way in range(2):
                whole_wait(acts.at[0, 0, c], zs.at[way, k, way, c])
                pl.when(k < 7)(lambda: whole_wait(acts.at[0, 0, c], zs.at[way, k, 1 - way, c]))

    loop(0, 8, ring_left)
    loop(0, GROUPS, lambda g: whole_wait(sb_v.at[g, pl.ds(0, 15)], ss.at[g]))

    loop(0, GROUPS, lambda g: whole_wait(sb_v.at[g, pl.ds(0, 15)], gs.at[g]))

    def chunks_left(g):
        for i in range(2):
            pl.when((2 * g + i != 1) | (chip >= 8))(lambda: whole_wait(gt_v.at[0, 0], hs.at[g, i]))

    loop(0, GROUPS, chunks_left)

    def weights_left(k):
        for way in range(2):
            for m in range(3):
                whole_wait(held(0, m), wzs.at[way, k, m])

    loop(0, 7, weights_left)
    for m in range(3):
        whole_wait(held(0, m), wzs.at[0 if m == 2 else 1, 7, m])
    loop(0, NZ - 1, lambda k: whole_wait(whole(0), wss.at[k, 0]))
    for m in range(3):
        whole_wait(held(0, m), wss.at[15, m])

    def keys_here(i):
        whole_wait(kv_v.at[i, 1, 1 - core], kr.at[i, 1, 1 - core])
        for back in (0, 2, 3):
            for c in range(2):
                whole_wait(kv_v.at[i, back, c], kr.at[i, back, c])
        for c in range(2):
            whole_wait(f_v.at[i, c], xr.at[i, c])

    keys_here(0)
    q = f_v[0].reshape(128, 128)
    keys = [kv_v[0, back].reshape(128, 128) for back in range(4)]
    scores = []
    for back in range(4):
        seen = causal if back == 0 else z >= back
        scores.append(jnp.where(seen, dot_t(q, keys[back]) * SCALE, NEG))
    top = scores[0].max(1, keepdims=True)
    for back in range(1, 4):
        top = jnp.maximum(top, scores[back].max(1, keepdims=True))
    weights = [jnp.exp(scores[back] - top) for back in range(4)]
    total = sum(jnp.sum(e, 1, keepdims=True) for e in weights)
    keys_here(1)
    mixed = sum(dot(weights[back].astype(BF16), kv_v[1, back].reshape(128, 128)) for back in range(4))
    co_v[...] = (f_v[1].reshape(128, 128).astype(F32) + mixed / total).astype(BF16)
    co_cp = pltpu.make_async_copy(co_v, coarse_out.at[0], out_sem.at[1])
    co_cp.start()

    for cp in swaps + kv_cp:
        cp.wait_send()
    fo_cp.wait()
    co_cp.wait()


def per_device(fine_q, fine_k, fine_v, fine_x, conv_weight, qkv_weight):
    cw = conv_weight.transpose(0, 2, 1)
    pw = qkv_weight[0].transpose(1, 0, 2)
    dma = pltpu.SemaphoreType.DMA
    vmem = pltpu.VMEM
    scratch = [
        vmem((128, 512), BF16), vmem((128, 512), BF16), vmem((128, 512), BF16), vmem((128, 512), BF16),
        vmem((2, 128, 256), BF16), vmem((2, 128, 256), BF16),
        vmem((4, 128, 128), F32),
        vmem((4, 2, 128, 1), F32),
        vmem((128, 512), BF16),
        vmem((2, 8, 16, 256), BF16),
        vmem((16, 2, 2, 4, 16, 256), BF16),
        vmem((2, 8, 32, 512), BF16),
        vmem((2, 512, 256), BF16),
        vmem((16, 3, 256, 256), BF16),
        vmem((4, 16, 2, 16, 128), BF16),
        vmem((4, 16, 2, 16, 128), BF16),
        vmem((4, 2, 16, 128), BF16),
        vmem((4, 2, 16, 128), BF16),
        vmem((4, 16, 2, 16, 128), BF16),
        vmem((16, 64, 256), BF16),
        vmem((3, 64, 256), F32),
        vmem((2, 2, 64, 128), BF16),
        vmem((2, 2, 64, 128), BF16),
        vmem((2, 2, 64, 128), BF16),
        vmem((2, 4, 2, 64, 128), BF16),
        vmem((128, 128), BF16),
        dma((4,)), dma((4,)), dma((4,)), dma((3,)), dma((4,)), dma((4,)), dma((2,)),
        dma((2, 8, 2, 2)), dma((2, 8, 2, 2)),
        dma((4,)), dma((4,)), dma((4,)), dma((4,)),
        dma((4, 2)), dma((4, 2)), dma((2, 8, 3)), dma((2, 8, 3)), dma((16, 3)), dma((16, 3)),
        dma((2, 2)), dma((2, 2)),
        dma((2, 4, 2)), dma((2, 4, 2)), dma((2,)),
    ]
    return pl.pallas_call(
        kernel,
        out_shape=(
            jax.ShapeDtypeStruct((128, 512), BF16),
            jax.ShapeDtypeStruct((1, 128, 128), BF16),
        ),
        in_specs=[pl.BlockSpec(memory_space=pl.ANY)] * 6,
        out_specs=[pl.BlockSpec(memory_space=pl.ANY)] * 2,
        scratch_shapes=scratch,
        compiler_params=pltpu.CompilerParams(
            collective_id=0, has_side_effects=True, vmem_limit_bytes=60 * 1024 * 1024
        ),
    )(fine_q, fine_k, fine_v, fine_x, cw, pw)


def solution(mesh):
    placed = (
        P("ctx", "head"),
        P("ctx", "head"),
        P("ctx", "head"),
        P("ctx", "head"),
        P(None, "head", "ctx"),
        P("ctx", None, None, "head"),
    )
    return jax.shard_map(
        per_device,
        mesh=mesh,
        in_specs=placed,
        out_specs=(P("ctx", "head"), P("ctx", None, "head")),
        check_vma=False,
    )
```
